32 devices in a mesh: groups: 2 (over x), rows: 16 (over z, y, core).
Axes of the slice: x: 2, y: 2, z: 4, core: 2. Of those that a mesh axis runs over, the one named last changes fastest.
Arguments:
- single_rep: bfloat16 [256, 384], P(('groups', 'rows')), parts along dimension 0, may hold values from -6 to 6
- pair_grid: bfloat16 [256, 128, 128], P('groups', 'rows'), parts along dimension 0, may hold values from -6 to 6
- frames: float32 [12, 256], P(None, ('groups', 'rows')), parts along dimension 1, may hold values from -60 to 60, as said below
- chain_ids: int32 [256], P('groups'), parts along dimension 0, may hold values from 0 to 3, never falling along the last dimension, each value on 1 to 64 neighbouring positions
- pad_mask: int32 [256], P('groups'), parts along dimension 0, may hold values from 0 to 1, as said below
- ln_pair_gain: float32 [128], replicated, may hold values from 0.5 to 1.5
- w_swiglu: bfloat16 [128, 1024], replicated, may hold values from -0.5 to 0.5
- w_pair_down: bfloat16 [512, 128], replicated, may hold values from -0.25 to 0.25
- w_bias: bfloat16 [128, 12], replicated, may hold values from -2 to 2
- w_qkv: bfloat16 [384, 576], replicated, may hold values from -0.3125 to 0.3125
- w_points: bfloat16 [384, 576], replicated, may hold values from -0.3125 to 0.3125
- gamma_raw: float32 [12], replicated, may hold values from -2 to 2
- chain_bias: float32 [2, 12], replicated, may hold values from -2 to 2
- w_out: bfloat16 [2112, 384], replicated, may hold values from -0.125 to 0.125
- ln_single_gain: float32 [384], replicated, may hold values from 0.5 to 1.5
Outputs:
- single_out: bfloat16 [256, 384], P(('groups', 'rows')), parts along dimension 0
- pair_out: bfloat16 [256, 128, 128], P('groups', 'rows'), parts along dimension 0
The draws below stay inside these ranges and needn't reach their ends.
There are 2 independent parts, one for each index of `groups`. The reference program is written for one: setup_inputs(seed, part) draws one part's arguments, and reference() takes and returns one part's arrays. A program takes and returns all parts, laid end to end along the dimension named above; an argument that names none is the same for every part. Nothing has to cross between parts.
Inputs may be any that keep to these rules, and one draw needn't show every extreme that they name: `frames`: each column is a proper rotation followed by a translation. `pad_mask`: the first residue is real and the last residue is padding.
All inputs are finite; a program needn't handle non-finite values.
Results may differ from the reference program's by a relative error of at most 0.0064.
Values may be sent and summed in bfloat16 or wider, within the bound.
No kernel may reach another device: no remote copies, remote signals or barrier semaphores. Data moves between devices by JAX's collectives and lax.ppermute only.
A program may use at most 128 MiB of HBM per device.

```python
import math
import jax
import jax.numpy as jnp
import numpy as np
from jax import lax

C = 128
S = 384
H = 512
HEADS = 12
CH = 16
QP = 4
VP = 8
NRES = 128


def mask_values(key):
    key_tail, key_gaps = jax.random.split(jax.random.fold_in(key, 7), 2)
    tail = jax.random.randint(key_tail, (), 1, NRES // 8 + 2)
    positions = jnp.arange(NRES)
    gaps = jax.random.randint(key_gaps, (NRES,), 0, 8) == 0
    padded = (positions >= NRES - tail) | gaps & (positions > 0)
    return jnp.where(padded, 0, 1).astype(jnp.int32)


def draw_pad_mask(key, part):
    mask = mask_values(key)
    return mask


def draw_frames(key, part):
    key = jax.random.fold_in(key, 13)
    key_quat, key_trans = jax.random.split(key, 2)
    quat = jax.random.normal(key_quat, (4, NRES), jnp.float32)
    first = 0.5 + jnp.abs(quat[0])
    norm_sq = first * first + quat[1] * quat[1] + quat[2] * quat[2] + quat[3] * quat[3]
    scale_q = 1.0 / jnp.sqrt(norm_sq)
    aa = first * scale_q
    bb = quat[1] * scale_q
    cc = quat[2] * scale_q
    dd = quat[3] * scale_q
    rotation = jnp.stack([aa * aa + bb * bb - cc * cc - dd * dd, 2.0 * (bb * cc - aa * dd), 2.0 * (bb * dd + aa * cc), 2.0 * (bb * cc + aa * dd), aa * aa - bb * bb + cc * cc - dd * dd, 2.0 * (cc * dd - aa * bb), 2.0 * (bb * dd - aa * cc), 2.0 * (cc * dd + aa * bb), aa * aa - bb * bb - cc * cc + dd * dd])
    trans = jnp.clip(1.5 * jax.random.normal(key_trans, (3, NRES), jnp.float32), -9.0, 9.0)
    return jnp.concatenate([rotation, trans], axis=0)


def draw_pair_grid(key, part):
    key = jax.random.fold_in(key, 21)
    key_base = jax.random.fold_in(key, 0)
    base_field = jnp.clip(jax.random.normal(key_base, (NRES, NRES, C), jnp.float32), -6.0, 6.0)
    return base_field.astype(jnp.bfloat16)


def draw_w_bias(key, part):
    key = jax.random.fold_in(key, 23)
    key_noise = jax.random.fold_in(key, 0)
    noise_part = jnp.clip(jax.random.normal(key_noise, (C, HEADS), jnp.float32), -4.0, 4.0) / jnp.sqrt(float(C))
    return noise_part.astype(jnp.bfloat16)


def level_of(stream_key, shape, cuts, least, high):
    level = 1.0
    for dim, shards_of in cuts:
        draws = jax.random.uniform(jax.random.fold_in(jax.random.fold_in(stream_key, 6), dim), (shards_of,), jnp.float32, least / len(cuts), high / len(cuts))
        level = level * jnp.repeat(jnp.exp(draws), shape[dim] // shards_of).reshape((-1,) + (1,) * (len(shape) - 1 - dim))
    return level


def profile(count, total, most, skew):
    portions = [(1 << 20) // math.isqrt(grade ** skew) + 1 for grade in range(2, count + 1)]
    surplus, given = total - most - (count - 1), [1] * (count - 1)
    while surplus > 0:
        candidates = [i for i in range(count - 1) if given[i] < most]
        mass, left = sum([portions[i] for i in candidates]), surplus
        for i in candidates:
            extra = min(most - given[i], max(1, left * portions[i] // mass), surplus)
            given[i] = given[i] + extra
            surplus = surplus - extra
    return np.array([most] + given)


def ragged_sizes(key, count, total, limit, skew):
    if count == 2:
        one = jax.random.randint(key, (), max(1, total - limit), min(limit, total - 1) + 1)
        return jnp.stack([one, total - one])
    tallies = jnp.asarray(profile(count, total, limit, skew), jnp.int32)
    couples = (count - 1) // 2
    source_of, taker = tallies[1:1 + 2 * couples:2], tallies[2:2 + 2 * couples:2]
    slack = jnp.minimum(source_of - 1, limit - taker)
    moved = jax.random.randint(jax.random.fold_in(key, 1), (couples,), 0, 1 << 20) % (slack + 1)
    tallies = tallies.at[1:1 + 2 * couples:2].set(source_of - moved).at[2:2 + 2 * couples:2].set(taker + moved)
    return tallies[jax.random.permutation(jax.random.fold_in(key, 2), count)]


def noise(own_key, dims, scale, most, cuts=(), kind=jnp.bfloat16):
    drawn = scale * jax.random.normal(own_key, dims, jnp.float32)
    if cuts:
        drawn = drawn * level_of(own_key, dims, cuts, -0.22, 0.18)
    return jnp.clip(drawn, -most, most).astype(kind)


def setup_inputs(seed: int = 0, part: int = 0) -> dict:
    splits = jax.random.split(jax.random.key(seed), 16)
    own_keys = jax.random.split(jax.random.fold_in(splits[15], part), 16)
    return {
        "single_rep": noise(own_keys[0], (NRES, S), 1.0, 6.0, ((0, 16),)),
        "pair_grid": draw_pair_grid(jax.random.fold_in(jax.random.fold_in(splits[15], part), 71), part),
        "frames": draw_frames(jax.random.fold_in(jax.random.fold_in(splits[15], part), 71), part),
        "chain_ids": jnp.searchsorted(jnp.cumsum(ragged_sizes(own_keys[3], 4, NRES, NRES // 2, 0)), jnp.arange(NRES), side="right").astype(jnp.int32),
        "pad_mask": draw_pad_mask(jax.random.fold_in(jax.random.fold_in(splits[15], part), 71), part),
        "ln_pair_gain": jnp.clip(1.0 + 0.1 * jax.random.normal(splits[5], (C,), jnp.float32), 0.5, 1.5),
        "w_swiglu": noise(splits[6], (C, 2 * H), C ** -0.5, 0.5),
        "w_pair_down": noise(splits[7], (H, C), H ** -0.5, 0.25),
        "w_bias": draw_w_bias(jax.random.fold_in(splits[15], 71), part),
        "w_qkv": noise(splits[9], (S, 3 * HEADS * CH), S ** -0.5, 0.3125),
        "w_points": noise(splits[10], (S, 3 * HEADS * (2 * QP + VP)), S ** -0.5, 0.3125),
        "gamma_raw": jnp.clip(jax.random.uniform(splits[11], (HEADS,), jnp.float32, -2.0, 2.0), -2.0, 2.0),
        "chain_bias": jnp.clip(jax.random.uniform(splits[12], (2, HEADS), jnp.float32, -2.0, 2.0), -2.0, 2.0),
        "w_out": noise(splits[13], (HEADS * (CH + 4 * VP + C), S), (HEADS * (CH + 4 * VP + C)) ** -0.5, 0.125),
        "ln_single_gain": jnp.clip(1.0 + 0.1 * jax.random.normal(splits[14], (S,), jnp.float32), 0.5, 1.5),
    }


PRECISE = lax.Precision.HIGHEST

def layer_norm(values, gain):
    centre = lax.optimization_barrier(jnp.mean(values, axis=-1, keepdims=True))
    centred = values - centre
    spread = lax.optimization_barrier(jnp.mean(centred * centred, axis=-1, keepdims=True))
    return centred * lax.rsqrt(spread + 1e-05) * gain

def transition_block(pair_rows, ln_pair_gain, w_swiglu, w_pair_down):
    values = pair_rows.astype(jnp.float32)
    normed = layer_norm(values, ln_pair_gain).astype(jnp.bfloat16)
    both_parts = jnp.dot(normed, w_swiglu, preferred_element_type=jnp.float32)
    hidden = (jax.nn.silu(both_parts[:, :H]) * both_parts[:, H:]).astype(jnp.bfloat16)
    update = jnp.dot(hidden, w_pair_down, preferred_element_type=jnp.float32)
    return (values + update).astype(jnp.bfloat16)

def pair_transition(pair_grid, ln_pair_gain, w_swiglu, w_pair_down):
    layout = pair_grid.shape
    flat = pair_grid.reshape(-1, layout[-1])
    total = flat.shape[0]
    block = math.gcd(total, 2048)
    blocks = flat.reshape(total // block, block, layout[-1])
    done = lax.map(lambda piece_rows: transition_block(piece_rows, ln_pair_gain, w_swiglu, w_pair_down), blocks)
    return done.reshape(layout)

def frame_parts(frames):
    rotation = jnp.transpose(frames[:9]).reshape(-1, 3, 3)
    offset = jnp.transpose(frames[9:])
    return (rotation, offset)

def project_heads(single_rep, frames, w_qkv, w_points):
    features = jnp.dot(single_rep, w_qkv, preferred_element_type=jnp.float32)
    local_pts = jnp.dot(single_rep, w_points, preferred_element_type=jnp.float32)
    rotation, offset = frame_parts(frames)
    residues = single_rep.shape[0]
    points = local_pts.reshape(residues, -1, 3)
    placed = jnp.einsum('rxy,rmy->rmx', rotation, points, precision=PRECISE) + offset[:, None, :]
    placed = placed.reshape(residues, -1)
    width = HEADS * CH
    qwidth = HEADS * QP * 3
    return (features[:, :width], features[:, width:2 * width], features[:, 2 * width:], placed[:, :qwidth], placed[:, qwidth:2 * qwidth], placed[:, 2 * qwidth:])

def pair_bias(pair_rows, w_bias):
    query_count, key_count = (pair_rows.shape[0], pair_rows.shape[1])
    flat = jnp.dot(pair_rows.reshape(-1, pair_rows.shape[2]), w_bias, preferred_element_type=jnp.float32)
    return jnp.transpose(flat.reshape(query_count, key_count, HEADS), (0, 2, 1))

def attention_logits(queries, query_pts, keys, key_pts, bias, same_chain, key_valid, gamma_raw, chain_bias):
    query_count, key_count = (queries.shape[0], keys.shape[0])
    query_heads = queries.reshape(query_count, HEADS, CH)
    key_heads = keys.reshape(key_count, HEADS, CH)
    dots = jnp.einsum('ihc,jhc->ihj', query_heads, key_heads, precision=PRECISE) / math.sqrt(CH)
    query_pth = query_pts.reshape(query_count, HEADS, QP * 3)
    key_pth = key_pts.reshape(key_count, HEADS, QP * 3)
    cross = jnp.einsum('ihc,jhc->ihj', query_pth, key_pth, precision=PRECISE)
    query_sq = lax.optimization_barrier(jnp.sum(query_pth * query_pth, axis=-1))
    key_sq = lax.optimization_barrier(jnp.sum(key_pth * key_pth, axis=-1))
    distance = query_sq[:, :, None] + jnp.transpose(key_sq)[None, :, :] - 2.0 * cross
    weight_c = math.sqrt(2.0 / (9.0 * QP))
    weight_l = math.sqrt(1.0 / 3.0)
    gamma = jax.nn.softplus(gamma_raw)
    chain_term = jnp.where(same_chain[:, None, :], chain_bias[0][None, :, None], chain_bias[1][None, :, None])
    scores = weight_l * (dots + bias + chain_term - gamma[None, :, None] * (0.5 * weight_c) * distance)
    return jnp.where(key_valid[None, None, :], scores, -1000000000.0)

def value_sums(attention, values, value_pts):
    query_count, key_count = (attention.shape[0], values.shape[0])
    value_out = jnp.einsum('ihj,jhc->ihc', attention, values.reshape(key_count, HEADS, CH), precision=PRECISE)
    point_out = jnp.einsum('ihj,jhm->ihm', attention, value_pts.reshape(key_count, HEADS, VP * 3), precision=PRECISE)
    return (value_out.reshape(query_count, -1), point_out.reshape(query_count, -1))

def pair_sums(attention16, pair_rows):
    summed = jnp.einsum('ihj,ijc->ihc', attention16.astype(jnp.float32), pair_rows.astype(jnp.float32), precision=PRECISE)
    return summed.reshape(attention16.shape[0], -1)

def finish_rows(value_out, point_out, pair_total, frames, single_rep, w_out, ln_single_gain):
    rotation, offset = frame_parts(frames)
    residues = single_rep.shape[0]
    shifted = point_out.reshape(residues, -1, 3) - offset[:, None, :]
    local_out = jnp.einsum('rxy,rmx->rmy', rotation, shifted, precision=PRECISE)
    lengths = jnp.sqrt(lax.optimization_barrier(jnp.sum(local_out * local_out, axis=-1)) + 1.0)
    joined = jnp.concatenate([value_out, local_out.reshape(residues, -1), lengths, pair_total], axis=1).astype(jnp.bfloat16)
    update = jnp.dot(joined, w_out, preferred_element_type=jnp.float32)
    return layer_norm(single_rep.astype(jnp.float32) + update, ln_single_gain).astype(jnp.bfloat16)

def reference(single_rep, pair_grid, frames, chain_ids, pad_mask, ln_pair_gain, w_swiglu, w_pair_down, w_bias, w_qkv, w_points, gamma_raw, chain_bias, w_out, ln_single_gain):
    pair_out = pair_transition(pair_grid, ln_pair_gain, w_swiglu, w_pair_down)
    queries, keys, values, query_pts, key_pts, value_pts = project_heads(single_rep, frames, w_qkv, w_points)
    key_valid = pad_mask > 0
    block = math.gcd(NRES, 128)
    nblocks = NRES // block
    inputs = (queries.reshape(nblocks, block, -1), query_pts.reshape(nblocks, block, -1), pair_out.reshape(nblocks, block, NRES, C), chain_ids.reshape(nblocks, block), single_rep.reshape(nblocks, block, S), jnp.transpose(frames).reshape(nblocks, block, 12))

    def one_block(pieces):
        block_q, block_qpts, block_pair, block_chain, block_single, block_frames = pieces
        bias = pair_bias(block_pair, w_bias)
        same_chain = block_chain[:, None] == chain_ids[None, :]
        scores = attention_logits(block_q, block_qpts, keys, key_pts, bias, same_chain, key_valid, gamma_raw, chain_bias)
        peak = lax.optimization_barrier(jnp.max(scores, axis=-1, keepdims=True))
        expo = jnp.exp(scores - peak)
        attention = expo / lax.optimization_barrier(jnp.sum(expo, axis=-1, keepdims=True))
        value_out, point_out = value_sums(attention, values, value_pts)
        pair_total = pair_sums(attention.astype(jnp.bfloat16), block_pair)
        return finish_rows(value_out, point_out, pair_total, jnp.transpose(block_frames), block_single, w_out, ln_single_gain)
    single_out = lax.map(one_block, inputs).reshape(NRES, S)
    return (single_out, pair_out)
```

```python
import functools
import math

import jax
import jax.numpy as jnp
from jax import lax
from jax.experimental import pallas as pl
from jax.experimental.pallas import tpu as pltpu
from jax.sharding import PartitionSpec as P

C = 128
S = 384
H = 512
HEADS = 12
CH = 16
QP = 4
VP = 8
HPAD = 16
FEAT = HEADS * CH
QPTS = HEADS * QP * 3
PLANE = HEADS * VP
F32 = jnp.float32
BF16 = jnp.bfloat16
PRECISE = lax.Precision.HIGHEST
NT = (((1,), (1,)), ((), ()))
SMALL = S // 128 + 1
VMEM_LIMIT = 40 * 1024 * 1024


def iota(shape, dim):
    return lax.broadcasted_iota(jnp.int32, shape, dim)


def layer_norm(values, gain):
    centre = jnp.mean(values, axis=-1, keepdims=True)
    centred = values - centre
    spread = jnp.mean(centred * centred, axis=-1, keepdims=True)
    return centred * lax.rsqrt(spread + 1e-05) * gain


def transition(values, gain, w_swiglu_ref, w_down_ref):
    normed = layer_norm(values, gain).astype(BF16)
    both = jnp.dot(normed, w_swiglu_ref[...], preferred_element_type=F32)
    gate = 0.5 * both[:, :H]
    hidden = (gate * (1.0 + jnp.tanh(gate)) * both[:, H:]).astype(BF16)
    update = jnp.dot(hidden, w_down_ref[...], preferred_element_type=F32)
    return (values + update).astype(BF16)


def pack_kernel(pair_ref, single_ref, frames_ref, out_ref, small_ref, sems):
    local = single_ref.shape[0]
    pair_copy = pltpu.make_async_copy(pair_ref, out_ref.at[:, :local], sems.at[0])
    pair_copy.start()
    rows = frames_ref[...]
    blank = jnp.zeros((local, 128 - 36), F32)
    turned = jnp.concatenate([rows, rows, rows, blank], axis=1)
    high = turned.astype(BF16).astype(F32)
    middle = (turned - high).astype(BF16).astype(F32)
    low = turned - high - middle
    lane = iota(turned.shape, 1)
    parts = jnp.where(lane < 12, high, jnp.where(lane < 24, middle, low)).astype(BF16)
    for dest in range(small_ref.shape[0]):
        for piece in range(SMALL - 1):
            small_ref[dest, piece] = single_ref[:, piece * 128 : piece * 128 + 128]
        small_ref[dest, SMALL - 1] = parts
    small_copy = pltpu.make_async_copy(small_ref, out_ref.at[:, local:], sems.at[1])
    small_copy.start()
    pair_copy.wait()
    small_copy.wait()


def own_kernel(pair_ref, gain_ref, w_swiglu_ref, w_down_ref, out_ref):
    local = pair_ref.shape[1]
    values = pair_ref[...].astype(F32).reshape(-1, C)
    done = transition(values, gain_ref[...], w_swiglu_ref, w_down_ref)
    out_ref[...] = done.astype(F32).reshape(-1, local, C).astype(BF16)


def attend_kernel(
    recv_ref,
    single_ref,
    frames_ref,
    turned_ref,
    chain_row_ref,
    chain_own_ref,
    pad_ref,
    gain_ref,
    w_swiglu_ref,
    w_down_ref,
    wb_ref,
    wq_ref,
    wp_ref,
    gamma_ref,
    cb_ref,
    w_out_ref,
    w_loc_ref,
    gain2_ref,
    _,
    out_ref,
    pair_scr,
    feat_scr,
    pts_scr,
    qf_scr,
    qp_scr,
    attn_scr,
    sums_scr,
):
    nsrc, _, local, _ = recv_ref.shape
    n = nsrc * local

    def piece(index):
        return recv_ref[:, index].astype(F32).reshape(n, 128)

    all_single = jnp.concatenate([piece(local + k).astype(BF16) for k in range(SMALL - 1)], axis=1)
    parts = piece(local + SMALL - 1).astype(BF16)
    rows16, lanes16 = iota((16, 128), 0), iota((16, 128), 1)
    pick = ((lanes16 % 12 == rows16) & (lanes16 < 36)).astype(BF16)
    frame_rows = lax.dot_general(pick, parts, NT, preferred_element_type=F32)
    feats = lax.dot_general(wq_ref[FEAT:, :], all_single, NT, preferred_element_type=F32)
    points = lax.dot_general(wp_ref[QPTS:, :], all_single, NT, preferred_element_type=F32)
    tiles, _, lane = feat_scr.shape
    for t in range(tiles):
        feat_scr[t] = feats[:FEAT, t * lane : (t + 1) * lane]
        pts_scr[t] = points[:, t * lane : (t + 1) * lane]

    def strided(ref, start, count, stride):
        return jnp.concatenate(
            [ref[t, pl.ds(start, count, stride=stride), :] for t in range(tiles)], axis=1
        )

    own_single = single_ref[...]
    qf_scr[...] = lax.dot_general(wq_ref[:FEAT, :], own_single, NT, preferred_element_type=F32)
    qp_scr[...] = lax.dot_general(wp_ref[:QPTS, :], own_single, NT, preferred_element_type=F32)
    own_frames = frames_ref[...]

    def rot(rows, x, y):
        return rows[3 * x + y : 3 * x + y + 1, :]

    def place(rows, triple):
        return [
            rot(rows, x, 0) * triple[0]
            + rot(rows, x, 1) * triple[1]
            + rot(rows, x, 2) * triple[2]
            + rows[9 + x : 10 + x, :]
            for x in range(3)
        ]

    key_feats = [strided(feat_scr, c, HEADS, CH) for c in range(CH)]
    query_feats = [qf_scr[pl.ds(c, HEADS, stride=CH), :] for c in range(CH)]
    key_pts, query_pts = [], []
    for p in range(QP):
        key_pts += place(
            frame_rows, [strided(pts_scr, 3 * p + y, HEADS, 3 * QP) for y in range(3)]
        )
        query_pts += place(
            own_frames, [qp_scr[pl.ds(3 * p + y, HEADS, stride=3 * QP), :] for y in range(3)]
        )
    value_planes = place(
        frame_rows, [strided(pts_scr, QPTS + y, PLANE, 3) for y in range(3)]
    )
    gap = jnp.zeros((128 - PLANE, n), F32)
    values = [feats[FEAT:], jnp.zeros((256 - FEAT, n), F32)]
    for plane in value_planes:
        values += [plane, gap]
    values = jnp.concatenate(values, axis=0)

    gain = gain_ref[...]
    group = max(1, min(local, 512 // n))
    for start in range(0, local, group):
        block = recv_ref[:, start : start + group].astype(F32)
        block = jnp.concatenate([block[:, k].reshape(n, C) for k in range(group)], axis=0)
        done = transition(block, gain, w_swiglu_ref, w_down_ref)
        for k in range(group):
            pair_scr[start + k] = done[k * n : (k + 1) * n]

    weight_c = math.sqrt(2.0 / (9.0 * QP))
    weight_l = math.sqrt(1.0 / 3.0)
    gamma = jax.nn.softplus(gamma_ref[...])
    point_scale = jnp.broadcast_to(gamma * (-0.5 * weight_c), (HEADS, n))
    same_bias = jnp.broadcast_to(cb_ref[:, 0:1], (HEADS, n))
    cross_bias = jnp.broadcast_to(cb_ref[:, 1:2], (HEADS, n))
    chain_row = jnp.broadcast_to(chain_row_ref[...], (HEADS, n))
    real = jnp.broadcast_to(pad_ref[...], (HEADS, n)) > 0
    for i in range(local):
        rows = pair_scr[i]
        bias = lax.dot_general(wb_ref[...], rows, NT, preferred_element_type=F32)[:HEADS]
        dots = sum(q[:, i : i + 1] * k for q, k in zip(query_feats, key_feats))
        distance = 0.0
        for q, k in zip(query_pts, key_pts):
            apart = q[:, i : i + 1] - k
            distance = distance + apart * apart
        chain = jnp.where(chain_row == chain_own_ref[i], same_bias, cross_bias)
        scores = weight_l * (dots * (1.0 / math.sqrt(CH)) + bias + chain + point_scale * distance)
        scores = jnp.where(real, scores, -1000000000.0)
        expo = jnp.exp(scores - jnp.max(scores, axis=-1, keepdims=True))
        attention = expo / jnp.sum(expo, axis=-1, keepdims=True)
        attention = jnp.concatenate([attention, jnp.zeros((HPAD - HEADS, n), F32)], axis=0)
        attn_scr[i * HPAD : (i + 1) * HPAD, :] = attention
        sums_scr[i * HPAD : (i + 1) * HPAD, :] = jnp.dot(
            attention.astype(BF16), rows, preferred_element_type=F32
        )

    every = lax.dot_general(
        attn_scr[...], values, NT, precision=PRECISE, preferred_element_type=F32
    )
    width = every.shape[1]
    heads, lanes = iota((HPAD, width), 0), iota((HPAD, width), 1)
    owner = jnp.where(lanes < 256, lanes // CH, (lanes % 128) // VP)
    every = every.reshape(local, HPAD, width)
    summed = jnp.sum(jnp.where((owner == heads)[None], every, 0.0), axis=1)

    turned = turned_ref[...]
    shifted = [
        summed[:, 256 + 128 * x : 384 + 128 * x] - turned[:, 9 + x : 10 + x] for x in range(3)
    ]
    local_out = [
        turned[:, y : y + 1] * shifted[0]
        + turned[:, 3 + y : 4 + y] * shifted[1]
        + turned[:, 6 + y : 7 + y] * shifted[2]
        for y in range(3)
    ]
    lengths = jnp.sqrt(
        local_out[0] * local_out[0] + local_out[1] * local_out[1] + local_out[2] * local_out[2] + 1.0
    )
    update = jnp.dot(
        summed[:, :FEAT].astype(BF16), w_out_ref[:FEAT, :], preferred_element_type=F32
    )
    for y in range(3):
        update += jnp.dot(
            local_out[y][:, :PLANE].astype(BF16), w_loc_ref[y], preferred_element_type=F32
        )
    at = FEAT + 3 * PLANE
    update += jnp.dot(
        lengths[:, :PLANE].astype(BF16), w_out_ref[at : at + PLANE, :], preferred_element_type=F32
    )
    at += PLANE
    pair_total = jnp.concatenate(
        [sums_scr[pl.ds(h, local, stride=HPAD), :] for h in range(HEADS)], axis=1
    )
    update += jnp.dot(pair_total.astype(BF16), w_out_ref[at:, :], preferred_element_type=F32)
    out_ref[...] = layer_norm(own_single.astype(F32) + update, gain2_ref[...]).astype(BF16)


def whole(memory=pltpu.VMEM):
    return pl.BlockSpec(memory_space=memory)


def on_device(
    single_rep,
    pair_grid,
    frames,
    chain_ids,
    pad_mask,
    ln_pair_gain,
    w_swiglu,
    w_pair_down,
    w_bias,
    w_qkv,
    w_points,
    gamma_raw,
    chain_bias,
    w_out,
    ln_single_gain,
):
    n, local, _ = pair_grid.shape
    nsrc = n // local
    tiles = max(1, n // 128)
    gain = ln_pair_gain.reshape(1, C)

    packed = pl.pallas_call(
        pack_kernel,
        out_shape=jax.ShapeDtypeStruct((nsrc, local + SMALL, local, C), BF16),
        in_specs=[whole(pl.ANY), whole(), whole()],
        out_specs=whole(pl.ANY),
        scratch_shapes=[
            pltpu.VMEM((nsrc, SMALL, local, C), BF16),
            pltpu.SemaphoreType.DMA((2,)),
        ],
        compiler_params=pltpu.CompilerParams(vmem_limit_bytes=VMEM_LIMIT),
        name="pack",
    )(pair_grid.reshape(nsrc, local, local, C), single_rep, frames.T)
    received = lax.all_to_all(packed, "rows", 0, 0, tiled=True)

    block = math.gcd(n, 128)
    pair_out = pl.pallas_call(
        own_kernel,
        out_shape=jax.ShapeDtypeStruct(pair_grid.shape, BF16),
        grid=(n // block,),
        in_specs=[
            pl.BlockSpec((block, local, C), lambda g: (g, 0, 0)),
            pl.BlockSpec((1, C), lambda g: (0, 0)),
            pl.BlockSpec(w_swiglu.shape, lambda g: (0, 0)),
            pl.BlockSpec(w_pair_down.shape, lambda g: (0, 0)),
        ],
        out_specs=pl.BlockSpec((block, local, C), lambda g: (g, 0, 0)),
        compiler_params=pltpu.CompilerParams(vmem_limit_bytes=VMEM_LIMIT),
        cost_estimate=pl.CostEstimate(
            flops=6 * n * local * C * H, bytes_accessed=4 * n * local * C, transcendentals=0
        ),
        name="own_transition",
    )(pair_grid, gain, w_swiglu, w_pair_down)

    first_row = lax.axis_index("rows") * local
    chain_own = lax.dynamic_slice_in_dim(chain_ids, first_row, local, 0)
    at = FEAT + 3 * PLANE
    w_loc = jnp.transpose(w_out[FEAT:at].reshape(PLANE, 3, S), (1, 0, 2))
    wb = jnp.pad(w_bias.T, ((0, HPAD - HEADS), (0, 0)))
    operands = [
        received,
        single_rep,
        frames,
        frames.T,
        chain_ids.reshape(1, n),
        chain_own,
        pad_mask.reshape(1, n),
        gain,
        w_swiglu,
        w_pair_down,
        wb,
        w_qkv.T,
        w_points.T,
        gamma_raw.reshape(HEADS, 1),
        chain_bias.T,
        w_out,
        w_loc,
        ln_single_gain.reshape(1, S),
        pair_out,
    ]
    memories = {5: pltpu.SMEM, len(operands) - 1: pl.ANY}
    specs = [whole(memories.get(k, pltpu.VMEM)) for k in range(len(operands))]
    single_out = pl.pallas_call(
        attend_kernel,
        out_shape=jax.ShapeDtypeStruct((local, S), BF16),
        in_specs=specs,
        out_specs=whole(),
        scratch_shapes=[
            pltpu.VMEM((local, n, C), BF16),
            pltpu.VMEM((tiles, FEAT, n // tiles), F32),
            pltpu.VMEM((tiles, QPTS + 3 * PLANE, n // tiles), F32),
            pltpu.VMEM((FEAT, local), F32),
            pltpu.VMEM((QPTS, local), F32),
            pltpu.VMEM((local * HPAD, n), F32),
            pltpu.VMEM((local * HPAD, C), F32),
        ],
        compiler_params=pltpu.CompilerParams(vmem_limit_bytes=VMEM_LIMIT),
        name="attend",
    )(*operands)
    return (single_out, pair_out)


def solution(mesh):
    placed = (
        P(("groups", "rows"), None),
        P("groups", "rows", None),
        P(None, ("groups", "rows")),
        P("groups"),
        P("groups"),
    ) + (P(),) * 10
    return jax.shard_map(
        on_device,
        mesh=mesh,
        in_specs=placed,
        out_specs=(P(("groups", "rows"), None), P("groups", "rows", None)),
        check_vma=False,
    )
```

```python
import math

import jax
import jax.numpy as jnp
from jax import lax
from jax.experimental import pallas as pl
from jax.experimental.pallas import tpu as pltpu
from jax.sharding import PartitionSpec as P

C = 128
S = 384
H = 512
HEADS = 12
CH = 16
QP = 4
VP = 8
HPAD = 16
FEAT = HEADS * CH
QPTS = HEADS * QP * 3
PLANE = HEADS * VP
WIDE = 256 + 3 * 128
F32 = jnp.float32
BF16 = jnp.bfloat16
NT = (((1,), (1,)), ((), ()))
MIB = 1024 * 1024
PREP_FLOPS = 10**9
WEIGHT_L = math.sqrt(1.0 / 3.0)
WEIGHT_C = math.sqrt(2.0 / (9.0 * QP))


def iota(shape, dim):
    return lax.broadcasted_iota(jnp.int32, shape, dim)


def nt_dot(a, b):
    return lax.dot_general(a, b, NT, preferred_element_type=F32)


def layer_norm(values, gain):
    centre = jnp.mean(values, axis=-1, keepdims=True)
    centred = values - centre
    spread = jnp.mean(centred * centred, axis=-1, keepdims=True)
    return centred * lax.rsqrt(spread + 1e-05) * gain


def transition(values, gain, w_swiglu_ref, w_down_ref):
    normed = layer_norm(values, gain).astype(BF16)
    both = jnp.dot(normed, w_swiglu_ref[...], preferred_element_type=F32)
    gate = 0.5 * both[:, :H]
    hidden = (gate * (1.0 + jnp.tanh(gate)) * both[:, H:]).astype(BF16)
    update = jnp.dot(hidden, w_down_ref[...], preferred_element_type=F32)
    return (values + update).astype(BF16)


def split(values):
    high = values.astype(BF16)
    return high, (values - high.astype(F32)).astype(BF16)


def pack_kernel(single_hbm, frames_hbm, out_ref, single_ref, frames_ref, sems):
    copies = [
        pltpu.make_async_copy(single_hbm, single_ref, sems.at[0]),
        pltpu.make_async_copy(frames_hbm, frames_ref, sems.at[1]),
    ]
    for copy in copies:
        copy.start()
    for copy in copies:
        copy.wait()
    rows = frames_ref[...]
    blank = jnp.zeros((rows.shape[0], 128 - 36), F32)
    turned = jnp.concatenate([rows, rows, rows, blank], axis=1)
    high = turned.astype(BF16).astype(F32)
    middle = (turned - high).astype(BF16).astype(F32)
    low = turned - high - middle
    lane = iota(turned.shape, 1)
    out_ref[:, :S] = single_ref[...]
    out_ref[:, S:] = jnp.where(lane < 12, high, jnp.where(lane < 24, middle, low)).astype(BF16)


def strided(ref, start, count, stride):
    return jnp.concatenate(
        [ref[t, pl.ds(start, count, stride=stride), :] for t in range(ref.shape[0])], axis=1
    )


def own_kernel(*refs):
    sources, refs = refs[:13], refs[13:]
    out_ref, heads_ref, rows_ref, gains_ref, wb_out_ref, w_loc_ref, wq_ref, wp_ref = refs[:8]
    held, refs = refs[8:19], refs[19:]
    loc_scr, sems = refs
    pair_hbm, *_ = sources
    n, local, _ = pair_hbm.shape
    targets = list(held) + [wq_ref, wp_ref]
    copies = []
    for k, (source, target) in enumerate(zip(sources, targets)):
        if k == 10:
            source = source.at[pl.ds(FEAT, 3 * PLANE)]
        copies.append(pltpu.make_async_copy(source, target, sems.at[k]))
        copies[k].start()
    pair_ref, w_swiglu_ref, w_down_ref, gain_ref, gamma_ref, cb_ref = held[:6]
    chain_ref, pad_ref, gain2_ref, wb_ref, loc_ref = held[6:]
    for copy in copies[:4]:
        copy.wait()
    gain = gain_ref[...].reshape(1, C)
    block = math.gcd(n, 128)

    def step(at):
        values = pair_ref[pl.ds(at, block)].astype(F32).reshape(-1, C)
        done = transition(values, gain, w_swiglu_ref, w_down_ref)
        out_ref[pl.ds(at, block)] = done.astype(F32).reshape(-1, local, C).astype(BF16)

    if n == block:
        step(0)
    else:
        pl.loop(0, n, step=block)(step)
    for copy in copies[4:]:
        copy.wait()

    diagonal = iota((HPAD, HEADS), 0) == iota((HPAD, HEADS), 1)

    def column(row):
        turned = jnp.sum(jnp.where(diagonal, row, 0.0), axis=1, keepdims=True)
        return jnp.broadcast_to(turned, (HPAD, 128))

    gamma = jax.nn.softplus(gamma_ref[...].reshape(1, HEADS))
    heads_ref[0] = column(gamma * (-0.5 * WEIGHT_C))
    heads_ref[1] = column(cb_ref[0:1, :])
    heads_ref[2] = column(cb_ref[1:2, :])
    rows_ref[0:1, :] = chain_ref[...].reshape(1, n)
    rows_ref[1:2, :] = pad_ref[...].reshape(1, n)
    gains_ref[0:1, :S] = gain2_ref[...].reshape(1, S)
    gains_ref[0:1, S:] = gain
    wb_out_ref[...] = jnp.concatenate(
        [wb_ref[...], jnp.zeros((HPAD - HEADS, C), BF16)], axis=0
    )
    local_rows = loc_ref[...].astype(F32)
    for t in range(S // 128):
        loc_scr[t] = local_rows[:, t * 128 : (t + 1) * 128]
    for y in range(3):
        w_loc_ref[y] = strided(loc_scr, y, PLANE, 3).astype(BF16)


def prepare_kernel(offsets, *refs):
    pieces, refs = refs[: len(offsets)], refs[len(offsets) :]
    heads_ref, rows_ref, wq_ref, wp_ref = refs[:4]
    base_ref, value_ref = refs[4:6]
    all_scr, feat_scr, pts_scr, qf_scr, qp_scr = refs[6:]
    tiles, _, lane = feat_scr.shape
    n = all_scr.shape[0]
    local = pieces[0].shape[1]
    me = lax.axis_index("rows")

    for piece, origins in zip(pieces, offsets):
        for k, origin in enumerate(origins):
            at = pl.multiple_of(jnp.bitwise_xor(me, origin) * local, local)
            all_scr[pl.ds(at, local), :] = piece[k].astype(F32)
    all_single = all_scr[:, :S].astype(BF16)
    all_parts = all_scr[:, S:].astype(BF16)
    own_single = pieces[0][0, :, :S]
    own_parts = pieces[0][0, :, S:]
    rows16, lanes16 = iota((16, 128), 0), iota((16, 128), 1)
    pick = ((lanes16 % 12 == rows16) & (lanes16 < 36)).astype(BF16)
    frames = nt_dot(pick, all_parts)
    own_frames = nt_dot(pick, own_parts)

    feats = nt_dot(wq_ref[FEAT : 2 * FEAT, :], all_single)
    points = nt_dot(wp_ref[QPTS:, :], all_single)
    for t in range(tiles):
        feat_scr[t] = feats[:, t * lane : (t + 1) * lane]
        pts_scr[t] = points[:, t * lane : (t + 1) * lane]
    qf_scr[...] = nt_dot(wq_ref[:FEAT, :], own_single)
    qp_scr[...] = nt_dot(wp_ref[:QPTS, :], own_single)

    def place(frame, triple):
        return [
            frame[3 * x : 3 * x + 1, :] * triple[0]
            + frame[3 * x + 1 : 3 * x + 2, :] * triple[1]
            + frame[3 * x + 2 : 3 * x + 3, :] * triple[2]
            + frame[9 + x : 10 + x, :]
            for x in range(3)
        ]

    key_feats = [strided(feat_scr, c, HEADS, CH) for c in range(CH)]
    query_feats = [qf_scr[pl.ds(c, HEADS, stride=CH), :] for c in range(CH)]
    key_pts, query_pts = [], []
    for p in range(QP):
        key_pts += place(frames, [strided(pts_scr, 3 * p + y, HEADS, 3 * QP) for y in range(3)])
        query_pts += place(
            own_frames, [qp_scr[pl.ds(3 * p + y, HEADS, stride=3 * QP), :] for y in range(3)]
        )

    def spread(index):
        return jnp.concatenate([heads_ref[index, :HEADS, :]] * max(1, n // 128), axis=1)[:, :n]

    point_scale, same_bias, cross_bias = spread(0), spread(1), spread(2)
    chain_row = rows_ref[0:1, :]
    lanes = iota((1, n), 1)
    for i in range(local):
        dots = sum(q[:, i : i + 1] * k for q, k in zip(query_feats, key_feats))
        distance = 0.0
        for q, k in zip(query_pts, key_pts):
            apart = q[:, i : i + 1] - k
            distance = distance + apart * apart
        mine = jnp.sum(jnp.where(lanes == me * local + i, chain_row, 0), axis=1, keepdims=True)
        chain = jnp.where(chain_row == mine, same_bias, cross_bias)
        base = WEIGHT_L * (dots * (1.0 / math.sqrt(CH)) + chain + point_scale * distance)
        base_ref[i] = jnp.concatenate([base, jnp.zeros((HPAD - HEADS, n), F32)], axis=0)

    planes = place(frames, [strided(pts_scr, QPTS + y, PLANE, 3) for y in range(3)])
    gap = jnp.zeros((n, 128 - PLANE), F32)
    values = [nt_dot(all_single, wq_ref[2 * FEAT :, :]), jnp.zeros((n, 256 - FEAT), F32)]
    for plane in planes:
        values += [plane.T, gap]
    high, low = split(jnp.concatenate(values, axis=1))
    value_ref[0] = high
    value_ref[1] = low


def attend_kernel(
    recv_ref,
    own_ref,
    base_ref,
    rows_ref,
    gains_ref,
    value_ref,
    w_swiglu_ref,
    w_down_ref,
    wb_ref,
    w_out_ref,
    w_loc_ref,
    out_ref,
    pair_scr,
    attn_scr,
    sums_scr,
):
    nsrc, local, _, _ = recv_ref.shape
    n = nsrc * local
    half = local * HPAD

    gain = gains_ref[0:1, S:]
    group = max(1, min(local, 512 // n))
    for start in range(0, local, group):
        block = recv_ref[:, start : start + group].astype(F32)
        block = jnp.concatenate([block[:, k].reshape(n, C) for k in range(group)], axis=0)
        done = transition(block, gain, w_swiglu_ref, w_down_ref)
        for k in range(group):
            pair_scr[start + k] = done[k * n : (k + 1) * n]

    bias = jnp.concatenate([nt_dot(wb_ref[...], pair_scr[i]) for i in range(local)], axis=0)
    real = jnp.broadcast_to(rows_ref[1:2, :], (half, n)) > 0
    scores = base_ref[...].reshape(half, n) + WEIGHT_L * bias
    scores = jnp.where(real, scores, -1000000000.0)
    expo = jnp.exp(scores - jnp.max(scores, axis=-1, keepdims=True))
    high, low = split(expo / jnp.sum(expo, axis=-1, keepdims=True))
    attn_scr[:half] = high
    attn_scr[half:] = low
    for i in range(local):
        at = i * HPAD
        sums_scr[at : at + HPAD, :] = jnp.dot(
            high[at : at + HPAD], pair_scr[i], preferred_element_type=F32
        )

    both = jnp.dot(attn_scr[...], value_ref[0], preferred_element_type=F32)
    every = both[:half] + both[half:]
    every += jnp.dot(attn_scr[:half], value_ref[1], preferred_element_type=F32)
    heads, lanes = iota((HPAD, WIDE), 0), iota((HPAD, WIDE), 1)
    owner = jnp.where(lanes < 256, lanes // CH, (lanes % 128) // VP)
    every = every.reshape(local, HPAD, WIDE)
    summed = jnp.sum(jnp.where((owner == heads)[None], every, 0.0), axis=1)

    parts = own_ref[:, S:].astype(F32)
    turned = parts[:, 0:12] + parts[:, 12:24] + parts[:, 24:36]
    shifted = [
        summed[:, 256 + 128 * x : 384 + 128 * x] - turned[:, 9 + x : 10 + x] for x in range(3)
    ]
    local_out = [
        turned[:, y : y + 1] * shifted[0]
        + turned[:, 3 + y : 4 + y] * shifted[1]
        + turned[:, 6 + y : 7 + y] * shifted[2]
        for y in range(3)
    ]
    lengths = jnp.sqrt(
        local_out[0] * local_out[0] + local_out[1] * local_out[1] + local_out[2] * local_out[2] + 1.0
    )
    update = jnp.dot(
        summed[:, :FEAT].astype(BF16), w_out_ref[:FEAT, :], preferred_element_type=F32
    )
    for y in range(3):
        update += jnp.dot(
            local_out[y][:, :PLANE].astype(BF16), w_loc_ref[y], preferred_element_type=F32
        )
    at = FEAT + 3 * PLANE
    update += jnp.dot(
        lengths[:, :PLANE].astype(BF16), w_out_ref[at : at + PLANE, :], preferred_element_type=F32
    )
    at += PLANE
    pair_total = jnp.concatenate(
        [sums_scr[pl.ds(h, local, stride=HPAD), :] for h in range(HEADS)], axis=1
    )
    update += jnp.dot(pair_total.astype(BF16), w_out_ref[at:, :], preferred_element_type=F32)
    own_single = own_ref[:, :S].astype(F32)
    out_ref[...] = layer_norm(own_single + update, gains_ref[0:1, :S]).astype(BF16)


def in_hbm(arrays):
    return [pltpu.with_memory_space_constraint(array, pltpu.HBM) for array in arrays]


def whole(memory=pltpu.VMEM):
    return pl.BlockSpec(memory_space=memory)


def params(mib):
    return pltpu.CompilerParams(vmem_limit_bytes=mib * MIB)


def gather_rows(rows, size):
    stack, origins, span = rows[None], [0], size
    while span > 4:
        span //= 4
        hops = [k * span for k in range(1, 4)]
        got = [stack] + [
            lax.ppermute(stack, "rows", [(i, i ^ hop) for i in range(size)]) for hop in hops
        ]
        stack = jnp.concatenate(got, axis=0)
        origins = [origin ^ hop for hop in [0] + hops for origin in origins]
    hops = list(range(1, span))
    got = [stack] + [
        lax.ppermute(stack, "rows", [(i, i ^ hop) for i in range(size)]) for hop in hops
    ]
    return got, [[origin ^ hop for origin in origins] for hop in [0] + hops]


def on_device(
    single_rep,
    pair_grid,
    frames,
    chain_ids,
    pad_mask,
    ln_pair_gain,
    w_swiglu,
    w_pair_down,
    w_bias,
    w_qkv,
    w_points,
    gamma_raw,
    chain_bias,
    w_out,
    ln_single_gain,
):
    n, local, _ = pair_grid.shape
    nsrc = n // local
    tiles = max(1, n // 128)
    large = 4 * (n // 128)

    own = pl.pallas_call(
        pack_kernel,
        out_shape=jax.ShapeDtypeStruct((local, S + 128), BF16),
        in_specs=[whole(pltpu.HBM), whole(pltpu.HBM)],
        out_specs=whole(),
        scratch_shapes=[
            pltpu.VMEM((local, S), BF16),
            pltpu.VMEM((local, 12), F32),
            pltpu.SemaphoreType.DMA((2,)),
        ],
        name="pack",
    )(*in_hbm([single_rep, frames.T]))
    pieces, offsets = gather_rows(own, nsrc)
    received = lax.all_to_all(
        pair_grid.reshape(nsrc, local, local, C), "rows", 0, 0, tiled=True
    )

    sources = [
        pair_grid,
        w_swiglu,
        w_pair_down,
        ln_pair_gain,
        gamma_raw,
        chain_bias,
        chain_ids,
        pad_mask,
        ln_single_gain,
        w_bias.T,
        w_out,
        w_qkv.T,
        w_points.T,
    ]
    held = [pltpu.VMEM(x.shape, x.dtype) for x in sources[:10]]
    held.append(pltpu.VMEM((3 * PLANE, S), BF16))
    pair_out, heads, rows, gains, wb, w_loc, wq, wp = pl.pallas_call(
        own_kernel,
        out_shape=[
            jax.ShapeDtypeStruct(pair_grid.shape, BF16),
            jax.ShapeDtypeStruct((3, HPAD, 128), F32),
            jax.ShapeDtypeStruct((2, n), jnp.int32),
            jax.ShapeDtypeStruct((1, S + C), F32),
            jax.ShapeDtypeStruct((HPAD, C), BF16),
            jax.ShapeDtypeStruct((3, PLANE, S), BF16),
            jax.ShapeDtypeStruct(sources[11].shape, BF16),
            jax.ShapeDtypeStruct(sources[12].shape, BF16),
        ],
        in_specs=[whole(pltpu.HBM)] * len(sources),
        out_specs=[whole()] * 8,
        scratch_shapes=held
        + [
            pltpu.VMEM((S // 128, 3 * PLANE, 128), F32),
            pltpu.SemaphoreType.DMA((len(sources),)),
        ],
        compiler_params=params(18 + large),
        name="own_transition",
    )(*in_hbm(sources))

    base, value = pl.pallas_call(
        lambda *refs: prepare_kernel(offsets, *refs),
        out_shape=[
            jax.ShapeDtypeStruct((local, HPAD, n), F32),
            jax.ShapeDtypeStruct((2, n, WIDE), BF16),
        ],
        in_specs=[whole()] * (len(pieces) + 4),
        out_specs=[whole()] * 2,
        scratch_shapes=[
            pltpu.VMEM((n, S + 128), F32),
            pltpu.VMEM((tiles, FEAT, n // tiles), F32),
            pltpu.VMEM((tiles, QPTS + 3 * PLANE, n // tiles), F32),
            pltpu.VMEM((FEAT, local), F32),
            pltpu.VMEM((QPTS, local), F32),
        ],
        compiler_params=params(12 + large),
        cost_estimate=pl.CostEstimate(flops=PREP_FLOPS, bytes_accessed=MIB, transcendentals=0),
        name="prepare",
    )(*pieces, heads, rows, wq, wp)

    single_out = pl.pallas_call(
        attend_kernel,
        out_shape=jax.ShapeDtypeStruct((local, S), BF16),
        in_specs=[whole()] * 11,
        out_specs=whole(),
        scratch_shapes=[
            pltpu.VMEM((local, n, C), BF16),
            pltpu.VMEM((2 * local * HPAD, n), BF16),
            pltpu.VMEM((local * HPAD, C), F32),
        ],
        compiler_params=params(16 + large),
        name="attend",
    )(received, own, base, rows, gains, value, w_swiglu, w_pair_down, wb, w_out, w_loc)
    return (single_out, pair_out)


def solution(mesh):
    placed = (
        P(("groups", "rows"), None),
        P("groups", "rows", None),
        P(None, ("groups", "rows")),
        P("groups"),
        P("groups"),
    ) + (P(),) * 10
    return jax.shard_map(
        on_device,
        mesh=mesh,
        in_specs=placed,
        out_specs=(P(("groups", "rows"), None), P("groups", "rows", None)),
        check_vma=False,
    )
```

```python
import math

import jax
import jax.numpy as jnp
from jax import lax
from jax.experimental import pallas as pl
from jax.experimental.pallas import tpu as pltpu
from jax.sharding import PartitionSpec as P

C = 128
S = 384
H = 512
HEADS = 12
CH = 16
QP = 4
VP = 8
HPAD = 16
FEAT = HEADS * CH
QPTS = HEADS * QP * 3
PLANE = HEADS * VP
WIDE = 256 + 3 * 128
SMALL = S // 128 + 1
PARTS = HEADS + 2 * (WIDE // 128) + 1
F32 = jnp.float32
BF16 = jnp.bfloat16
NT = (((1,), (1,)), ((), ()))
MIB = 1024 * 1024
WEIGHT_L = math.sqrt(1.0 / 3.0)
WEIGHT_C = math.sqrt(2.0 / (9.0 * QP))


def iota(shape, dim):
    return lax.broadcasted_iota(jnp.int32, shape, dim)


def nt_dot(a, b):
    return lax.dot_general(a, b, NT, preferred_element_type=F32)


def layer_norm(values, gain):
    centre = jnp.mean(values, axis=-1, keepdims=True)
    centred = values - centre
    spread = jnp.mean(centred * centred, axis=-1, keepdims=True)
    return centred * lax.rsqrt(spread + 1e-05) * gain


def transition(values, gain, w_swiglu_ref, w_down_ref):
    normed = layer_norm(values, gain).astype(BF16)
    both = jnp.dot(normed, w_swiglu_ref[...], preferred_element_type=F32)
    gate = 0.5 * both[:, :H]
    hidden = (gate * (1.0 + jnp.tanh(gate)) * both[:, H:]).astype(BF16)
    update = jnp.dot(hidden, w_down_ref[...], preferred_element_type=F32)
    return (values + update).astype(BF16)


def split(values):
    high = values.astype(BF16)
    return high, (values - high.astype(F32)).astype(BF16)


def pack_kernel(pair_hbm, single_hbm, frames_hbm, out_ref, own_ref, frames_ref, sems):
    local = own_ref.shape[0]
    copies = [
        pltpu.make_async_copy(single_hbm, own_ref.at[:, :S], sems.at[0]),
        pltpu.make_async_copy(frames_hbm, frames_ref, sems.at[1]),
    ]
    for half in range(2):
        copies.append(
            pltpu.make_async_copy(
                pair_hbm.at[half], out_ref.at[:, pl.ds(half * local, local)], sems.at[2 + half]
            )
        )
    for copy in copies:
        copy.start()
    copies[0].wait()
    copies[1].wait()
    rows = frames_ref[...]
    blank = jnp.zeros((local, 128 - 36), F32)
    turned = jnp.concatenate([rows, rows, rows, blank], axis=1)
    high = turned.astype(BF16).astype(F32)
    middle = (turned - high).astype(BF16).astype(F32)
    low = turned - high - middle
    lane = iota(turned.shape, 1)
    own_ref[:, S:] = jnp.where(lane < 12, high, jnp.where(lane < 24, middle, low)).astype(BF16)
    for dest in range(out_ref.shape[0]):
        for piece in range(SMALL):
            out_ref[dest, 2 * local + piece] = own_ref[:, piece * 128 : piece * 128 + 128]
    copies[2].wait()
    copies[3].wait()


def strided(ref, start, count, stride):
    return jnp.concatenate(
        [ref[t, pl.ds(start, count, stride=stride), :] for t in range(ref.shape[0])], axis=1
    )


def own_kernel(*refs):
    sources, refs = refs[:13], refs[13:]
    out_ref, heads_ref, rows_ref, gains_ref, wb_out_ref, w_loc_ref, wq_ref, wp_ref = refs[:8]
    held, refs = refs[8:19], refs[19:]
    loc_scr, sems = refs
    pair_hbm, *_ = sources
    n, local, _ = pair_hbm.shape
    targets = list(held) + [wq_ref, wp_ref]
    copies = []
    for k, (source, target) in enumerate(zip(sources, targets)):
        if k == 10:
            source = source.at[pl.ds(FEAT, 3 * PLANE)]
        copies.append(pltpu.make_async_copy(source, target, sems.at[k]))
        copies[k].start()
    pair_ref, w_swiglu_ref, w_down_ref, gain_ref, gamma_ref, cb_ref = held[:6]
    chain_ref, pad_ref, gain2_ref, wb_ref, loc_ref = held[6:]
    for copy in copies[:4]:
        copy.wait()
    gain = gain_ref[...].reshape(1, C)
    block = math.gcd(n, 128)

    def step(at):
        values = pair_ref[pl.ds(at, block)].astype(F32).reshape(-1, C)
        done = transition(values, gain, w_swiglu_ref, w_down_ref)
        out_ref[pl.ds(at, block)] = done.astype(F32).reshape(-1, local, C).astype(BF16)

    if n == block:
        step(0)
    else:
        pl.loop(0, n, step=block)(step)
    for copy in copies[4:]:
        copy.wait()

    diagonal = iota((HPAD, HEADS), 0) == iota((HPAD, HEADS), 1)

    def column(row):
        turned = jnp.sum(jnp.where(diagonal, row, 0.0), axis=1, keepdims=True)
        return jnp.broadcast_to(turned, (HPAD, 128))

    gamma = jax.nn.softplus(gamma_ref[...].reshape(1, HEADS))
    heads_ref[0] = column(gamma * (-0.5 * WEIGHT_C))
    heads_ref[1] = column(cb_ref[0:1, :])
    heads_ref[2] = column(cb_ref[1:2, :])
    rows_ref[0:1, :] = chain_ref[...].reshape(1, n)
    rows_ref[1:2, :] = pad_ref[...].reshape(1, n)
    gains_ref[0:1, :S] = gain2_ref[...].reshape(1, S)
    gains_ref[0:1, S:] = gain
    wb_out_ref[...] = jnp.concatenate(
        [wb_ref[...], jnp.zeros((HPAD - HEADS, C), BF16)], axis=0
    )
    local_rows = loc_ref[...].astype(F32)
    for t in range(S // 128):
        loc_scr[t] = local_rows[:, t * 128 : (t + 1) * 128]
    for y in range(3):
        w_loc_ref[y] = strided(loc_scr, y, PLANE, 3).astype(BF16)


def place(frame, triple):
    return [
        frame[3 * x : 3 * x + 1, :] * triple[0]
        + frame[3 * x + 1 : 3 * x + 2, :] * triple[1]
        + frame[3 * x + 2 : 3 * x + 3, :] * triple[2]
        + frame[9 + x : 10 + x, :]
        for x in range(3)
    ]


def head_of_lane(rows):
    lanes = iota((rows, WIDE), 1)
    return jnp.where(lanes < 256, lanes // CH, (lanes % 128) // VP)


def partial_attention(
    recv_ref, at, base, real, high_value, low_value, gain, w_swiglu_ref, w_down_ref, wb_ref,
    pair_scr, attn_scr, sums_scr,
):
    nsrc, _, local, _ = recv_ref.shape
    n = nsrc * local
    rows = local * HPAD
    group = max(1, min(local, 512 // n))
    for start in range(0, local, group):
        block = recv_ref[:, pl.ds(at + start, group)].astype(F32)
        block = jnp.concatenate([block[:, k].reshape(n, C) for k in range(group)], axis=0)
        done = transition(block, gain, w_swiglu_ref, w_down_ref)
        for k in range(group):
            pair_scr[start + k] = done[k * n : (k + 1) * n]
    bias = jnp.concatenate([nt_dot(wb_ref[...], pair_scr[i]) for i in range(local)], axis=0)
    scores = base + WEIGHT_L * bias
    scores = jnp.where(jnp.broadcast_to(real, (rows, n)) > 0, scores, -1000000000.0)
    peak = jnp.max(scores, axis=-1, keepdims=True)
    expo = jnp.exp(scores - peak)
    total = jnp.sum(expo, axis=-1, keepdims=True)
    high, low = split(expo / total)
    attn_scr[:rows] = high
    attn_scr[rows:] = low
    for i in range(local):
        first = i * HPAD
        sums_scr[first : first + HPAD, :] = jnp.dot(
            high[first : first + HPAD], pair_scr[i], preferred_element_type=F32
        )
    both = jnp.dot(attn_scr[...], high_value, preferred_element_type=F32)
    every = both[:rows] + both[rows:]
    every += jnp.dot(attn_scr[:rows], low_value, preferred_element_type=F32)
    owned = head_of_lane(HPAD) == iota((HPAD, WIDE), 0)
    every = every.reshape(local, HPAD, WIDE)
    summed = jnp.sum(jnp.where(owned[None], every, 0.0), axis=1)
    diagonal = (iota((HPAD, HPAD), 0) == iota((HPAD, HPAD), 1))[None]

    def by_head(column):
        wide = jnp.broadcast_to(column.reshape(local, HPAD, 1), (local, HPAD, HPAD))
        return jnp.sum(jnp.where(diagonal, wide, 0.0), axis=1)

    pair_sums = [sums_scr[pl.ds(h, local, stride=HPAD), :] for h in range(HEADS)]
    return pair_sums, summed, by_head(peak), by_head(total)


def first_kernel(
    recv_ref,
    own_ref,
    partner_ref,
    heads_ref,
    rows_ref,
    gains_ref,
    wq_ref,
    wp_ref,
    wb_ref,
    w_swiglu_ref,
    w_down_ref,
    send_ref,
    base_ref,
    value_ref,
    real_ref,
    feat_scr,
    pts_scr,
    qf_scr,
    qp_scr,
    pair_scr,
    attn_scr,
    sums_scr,
):
    nsrc, _, local, _ = recv_ref.shape
    tiles, _, lane = feat_scr.shape
    n = nsrc * local
    me = lax.axis_index("rows")
    upper = me // nsrc

    def piece(index):
        return recv_ref[:, index].astype(F32).reshape(n, 128).astype(BF16)

    all_single = jnp.concatenate([piece(2 * local + k) for k in range(SMALL - 1)], axis=1)
    queries = jnp.concatenate(
        [partner_ref[...].astype(F32), own_ref[...].astype(F32)], axis=0
    ).astype(BF16)
    rows16, lanes16 = iota((16, 128), 0), iota((16, 128), 1)
    pick = ((lanes16 % 12 == rows16) & (lanes16 < 36)).astype(BF16)
    frames = nt_dot(pick, piece(2 * local + SMALL - 1))
    query_frames = nt_dot(pick, queries[:, S:])

    feats = nt_dot(wq_ref[FEAT : 2 * FEAT, :], all_single)
    points = nt_dot(wp_ref[QPTS:, :], all_single)
    for t in range(tiles):
        feat_scr[t] = feats[:, t * lane : (t + 1) * lane]
        pts_scr[t] = points[:, t * lane : (t + 1) * lane]
    qf_scr[...] = nt_dot(wq_ref[:FEAT, :], queries[:, :S])
    qp_scr[...] = nt_dot(wp_ref[:QPTS, :], queries[:, :S])

    key_feats = [strided(feat_scr, c, HEADS, CH) for c in range(CH)]
    query_feats = [qf_scr[pl.ds(c, HEADS, stride=CH), :] for c in range(CH)]
    key_pts, query_pts = [], []
    for p in range(QP):
        key_pts += place(frames, [strided(pts_scr, 3 * p + y, HEADS, 3 * QP) for y in range(3)])
        query_pts += place(
            query_frames, [qp_scr[pl.ds(3 * p + y, HEADS, stride=3 * QP), :] for y in range(3)]
        )

    def spread(index):
        return jnp.concatenate([heads_ref[index, :HEADS, :]] * max(1, n // 128), axis=1)[:, :n]

    point_scale, same_bias, cross_bias = spread(0), spread(1), spread(2)
    chain_all = rows_ref[0:1, :]
    chain_row = jnp.where(upper == 0, chain_all[:, :n], chain_all[:, n:])
    real = jnp.where(upper == 0, rows_ref[1:2, :n], rows_ref[1:2, n:])
    real_ref[...] = real
    lanes = iota((1, 2 * n), 1)
    starts = [jnp.bitwise_xor(me, nsrc) * local, me * local]
    bases = []
    for i in range(2 * local):
        dots = sum(q[:, i : i + 1] * k for q, k in zip(query_feats, key_feats))
        distance = 0.0
        for q, k in zip(query_pts, key_pts):
            apart = q[:, i : i + 1] - k
            distance = distance + apart * apart
        at = starts[i // local] + i % local
        mine = jnp.sum(jnp.where(lanes == at, chain_all, 0), axis=1, keepdims=True)
        chain = jnp.where(chain_row == mine, same_bias, cross_bias)
        base = WEIGHT_L * (dots * (1.0 / math.sqrt(CH)) + chain + point_scale * distance)
        base = jnp.concatenate([base, jnp.zeros((HPAD - HEADS, n), F32)], axis=0)
        if i < local:
            bases.append(base)
        else:
            base_ref[(i - local) * HPAD : (i - local + 1) * HPAD, :] = base

    planes = place(frames, [strided(pts_scr, QPTS + y, PLANE, 3) for y in range(3)])
    gap = jnp.zeros((n, 128 - PLANE), F32)
    values = [nt_dot(all_single, wq_ref[2 * FEAT :, :]), jnp.zeros((n, 256 - FEAT), F32)]
    for plane in planes:
        values += [plane.T, gap]
    high, low = split(jnp.concatenate(values, axis=1))
    value_ref[0] = high
    value_ref[1] = low

    pair_sums, summed, peak, total = partial_attention(
        recv_ref, (1 - upper) * local, jnp.concatenate(bases, axis=0), real, high, low,
        gains_ref[0:1, S:], w_swiglu_ref, w_down_ref, wb_ref, pair_scr, attn_scr, sums_scr,
    )
    for h in range(HEADS):
        send_ref[h] = pair_sums[h].astype(BF16)
    high, low = split(summed)
    pieces = WIDE // 128
    for k in range(pieces):
        send_ref[HEADS + k] = high[:, k * 128 : (k + 1) * 128]
        send_ref[HEADS + pieces + k] = low[:, k * 128 : (k + 1) * 128]
    both = jnp.concatenate([peak, total], axis=1)
    high = both.astype(BF16).astype(F32)
    middle = (both - high).astype(BF16).astype(F32)
    low = both - high - middle
    blank = jnp.zeros((local, 128 - 6 * HPAD), F32)
    send_ref[PARTS - 1] = jnp.concatenate([high, middle, low, blank], axis=1).astype(BF16)


def second_kernel(
    recv_ref,
    base_ref,
    value_ref,
    real_ref,
    gains_ref,
    wb_ref,
    w_swiglu_ref,
    w_down_ref,
    sums_ref,
    wide_ref,
    stats_ref,
    pair_scr,
    attn_scr,
    sums_scr,
):
    nsrc, _, local, _ = recv_ref.shape
    upper = lax.axis_index("rows") // nsrc
    pair_sums, summed, peak, total = partial_attention(
        recv_ref, upper * local, base_ref[...], real_ref[...], value_ref[0], value_ref[1],
        gains_ref[0:1, S:], w_swiglu_ref, w_down_ref, wb_ref, pair_scr, attn_scr, sums_scr,
    )
    for h in range(HEADS):
        sums_ref[h] = pair_sums[h]
    wide_ref[...] = summed
    stats_ref[...] = jnp.concatenate([peak, total], axis=1)


def finish_kernel(
    got_ref,
    sums_ref,
    wide_ref,
    stats_ref,
    own_ref,
    gains_ref,
    w_out_ref,
    w_loc_ref,
    out_ref,
):
    local = own_ref.shape[0]
    got = got_ref[PARTS - 1].astype(F32)
    width = 2 * HPAD
    got = got[:, :width] + got[:, width : 2 * width] + got[:, 2 * width : 3 * width]
    mine = stats_ref[...]
    peak = jnp.maximum(got[:, :HPAD], mine[:, :HPAD])
    got = got[:, HPAD:] * jnp.exp(got[:, :HPAD] - peak)
    mine = mine[:, HPAD:] * jnp.exp(mine[:, :HPAD] - peak)
    scale = 1.0 / (got + mine)
    got, mine = got * scale, mine * scale
    owner = head_of_lane(local)
    got_wide = jnp.zeros((local, WIDE), F32)
    mine_wide = jnp.zeros((local, WIDE), F32)
    pair_total = []
    for h in range(HEADS):
        got_share, mine_share = got[:, h : h + 1], mine[:, h : h + 1]
        got_wide = jnp.where(owner == h, got_share, got_wide)
        mine_wide = jnp.where(owner == h, mine_share, mine_wide)
        pair_total.append(got_share * got_ref[h].astype(F32) + mine_share * sums_ref[h])
    pieces = WIDE // 128
    sent = jnp.concatenate(
        [
            got_ref[HEADS + k].astype(F32) + got_ref[HEADS + pieces + k].astype(F32)
            for k in range(pieces)
        ],
        axis=1,
    )
    summed = got_wide * sent + mine_wide * wide_ref[...]

    parts = own_ref[:, S:].astype(F32)
    turned = parts[:, 0:12] + parts[:, 12:24] + parts[:, 24:36]
    shifted = [
        summed[:, 256 + 128 * x : 384 + 128 * x] - turned[:, 9 + x : 10 + x] for x in range(3)
    ]
    local_out = [
        turned[:, y : y + 1] * shifted[0]
        + turned[:, 3 + y : 4 + y] * shifted[1]
        + turned[:, 6 + y : 7 + y] * shifted[2]
        for y in range(3)
    ]
    lengths = jnp.sqrt(
        local_out[0] * local_out[0] + local_out[1] * local_out[1] + local_out[2] * local_out[2] + 1.0
    )
    update = jnp.dot(
        summed[:, :FEAT].astype(BF16), w_out_ref[:FEAT, :], preferred_element_type=F32
    )
    for y in range(3):
        update += jnp.dot(
            local_out[y][:, :PLANE].astype(BF16), w_loc_ref[y], preferred_element_type=F32
        )
    at = FEAT + 3 * PLANE
    update += jnp.dot(
        lengths[:, :PLANE].astype(BF16), w_out_ref[at : at + PLANE, :], preferred_element_type=F32
    )
    at += PLANE
    pair_total = jnp.concatenate(pair_total, axis=1).astype(BF16)
    update += jnp.dot(pair_total, w_out_ref[at:, :], preferred_element_type=F32)
    own_single = own_ref[:, :S].astype(F32)
    out_ref[...] = layer_norm(own_single + update, gains_ref[0:1, :S]).astype(BF16)


def in_hbm(arrays):
    return [pltpu.with_memory_space_constraint(array, pltpu.HBM) for array in arrays]


def whole(memory=pltpu.VMEM):
    return pl.BlockSpec(memory_space=memory)


def params(mib):
    return pltpu.CompilerParams(vmem_limit_bytes=mib * MIB)


def on_device(
    single_rep,
    pair_grid,
    frames,
    chain_ids,
    pad_mask,
    ln_pair_gain,
    w_swiglu,
    w_pair_down,
    w_bias,
    w_qkv,
    w_points,
    gamma_raw,
    chain_bias,
    w_out,
    ln_single_gain,
):
    n, local, _ = pair_grid.shape
    size = n // local
    nsrc = size // 2
    near = n // 2
    tiles = max(1, near // 128)
    large = 4 * (n // 128)
    halves = [list(range(nsrc)), list(range(nsrc, size))]
    across = [(i, i ^ nsrc) for i in range(size)]

    packed, own = pl.pallas_call(
        pack_kernel,
        out_shape=[
            jax.ShapeDtypeStruct((nsrc, 2 * local + SMALL, local, C), BF16),
            jax.ShapeDtypeStruct((local, S + 128), BF16),
        ],
        in_specs=[whole(pltpu.HBM)] * 3,
        out_specs=[whole(), whole()],
        scratch_shapes=[
            pltpu.VMEM((local, 12), F32),
            pltpu.SemaphoreType.DMA((4,)),
        ],
        compiler_params=params(4 + large),
        name="pack",
    )(*in_hbm([pair_grid.reshape(2, nsrc, local, local, C), single_rep, frames.T]))
    received = lax.all_to_all(
        packed, "rows", 0, 0, tiled=True, axis_index_groups=halves
    )
    partner = lax.ppermute(own, "rows", across)

    sources = [
        pair_grid,
        w_swiglu,
        w_pair_down,
        ln_pair_gain,
        gamma_raw,
        chain_bias,
        chain_ids,
        pad_mask,
        ln_single_gain,
        w_bias.T,
        w_out,
        w_qkv.T,
        w_points.T,
    ]
    held = [pltpu.VMEM(x.shape, x.dtype) for x in sources[:10]]
    held.append(pltpu.VMEM((3 * PLANE, S), BF16))
    pair_out, heads, rows, gains, wb, w_loc, wq, wp = pl.pallas_call(
        own_kernel,
        out_shape=[
            jax.ShapeDtypeStruct(pair_grid.shape, BF16),
            jax.ShapeDtypeStruct((3, HPAD, 128), F32),
            jax.ShapeDtypeStruct((2, n), jnp.int32),
            jax.ShapeDtypeStruct((1, S + C), F32),
            jax.ShapeDtypeStruct((HPAD, C), BF16),
            jax.ShapeDtypeStruct((3, PLANE, S), BF16),
            jax.ShapeDtypeStruct(sources[11].shape, BF16),
            jax.ShapeDtypeStruct(sources[12].shape, BF16),
        ],
        in_specs=[whole(pltpu.HBM)] * len(sources),
        out_specs=[whole()] * 8,
        scratch_shapes=held
        + [
            pltpu.VMEM((S // 128, 3 * PLANE, 128), F32),
            pltpu.SemaphoreType.DMA((len(sources),)),
        ],
        compiler_params=params(18 + large),
        name="own_transition",
    )(*in_hbm(sources))

    scratch = [
        pltpu.VMEM((local, near, C), BF16),
        pltpu.VMEM((2 * local * HPAD, near), BF16),
        pltpu.VMEM((local * HPAD, C), F32),
    ]
    send, base, value, real = pl.pallas_call(
        first_kernel,
        out_shape=[
            jax.ShapeDtypeStruct((PARTS, local, 128), BF16),
            jax.ShapeDtypeStruct((local * HPAD, near), F32),
            jax.ShapeDtypeStruct((2, near, WIDE), BF16),
            jax.ShapeDtypeStruct((1, near), jnp.int32),
        ],
        in_specs=[whole()] * 11,
        out_specs=[whole()] * 4,
        scratch_shapes=[
            pltpu.VMEM((tiles, FEAT, near // tiles), F32),
            pltpu.VMEM((tiles, QPTS + 3 * PLANE, near // tiles), F32),
            pltpu.VMEM((FEAT, 2 * local), F32),
            pltpu.VMEM((QPTS, 2 * local), F32),
        ]
        + scratch,
        compiler_params=params(16 + large),
        name="first_half",
    )(received, own, partner, heads, rows, gains, wq, wp, wb, w_swiglu, w_pair_down)
    got = lax.ppermute(send, "rows", across)

    sums, wide, stats = pl.pallas_call(
        second_kernel,
        out_shape=[
            jax.ShapeDtypeStruct((HEADS, local, 128), F32),
            jax.ShapeDtypeStruct((local, WIDE), F32),
            jax.ShapeDtypeStruct((local, 2 * HPAD), F32),
        ],
        in_specs=[whole()] * 8,
        out_specs=[whole()] * 3,
        scratch_shapes=scratch,
        compiler_params=params(12 + large),
        name="second_half",
    )(received, base, value, real, gains, wb, w_swiglu, w_pair_down)

    single_out = pl.pallas_call(
        finish_kernel,
        out_shape=jax.ShapeDtypeStruct((local, S), BF16),
        in_specs=[whole()] * 8,
        out_specs=whole(),
        compiler_params=params(12),
        name="finish",
    )(got, sums, wide, stats, own, gains, w_out, w_loc)
    return (single_out, pair_out)


def solution(mesh):
    placed = (
        P(("groups", "rows"), None),
        P("groups", "rows", None),
        P(None, ("groups", "rows")),
        P("groups"),
        P("groups"),
    ) + (P(),) * 10
    return jax.shard_map(
        on_device,
        mesh=mesh,
        in_specs=placed,
        out_specs=(P(("groups", "rows"), None), P("groups", "rows", None)),
        check_vma=False,
    )
```

```python
import math

import jax
import jax.numpy as jnp
from jax import lax
from jax.experimental import pallas as pl
from jax.experimental.pallas import tpu as pltpu
from jax.sharding import PartitionSpec as P

C = 128
S = 384
H = 512
HEADS = 12
CH = 16
QP = 4
VP = 8
HPAD = 16
FEAT = HEADS * CH
QPTS = HEADS * QP * 3
PLANE = HEADS * VP
WIDE = 256 + 3 * 128
SMALL = S // 128 + 1
PARTS = HEADS + 2 * (WIDE // 128) + 1
F32 = jnp.float32
BF16 = jnp.bfloat16
NT = (((1,), (1,)), ((), ()))
MIB = 1024 * 1024
WEIGHT_L = math.sqrt(1.0 / 3.0)
WEIGHT_C = math.sqrt(2.0 / (9.0 * QP))


def iota(shape, dim):
    return lax.broadcasted_iota(jnp.int32, shape, dim)


def nt_dot(a, b):
    return lax.dot_general(a, b, NT, preferred_element_type=F32)


def layer_norm(values, gain):
    centre = jnp.mean(values, axis=-1, keepdims=True)
    centred = values - centre
    spread = jnp.mean(centred * centred, axis=-1, keepdims=True)
    return centred * lax.rsqrt(spread + 1e-05) * gain


def transition(values, gain, w_swiglu_ref, w_down_ref):
    normed = layer_norm(values, gain).astype(BF16)
    both = jnp.dot(normed, w_swiglu_ref[...], preferred_element_type=F32)
    gate = 0.5 * both[:, :H]
    hidden = (gate * (1.0 + jnp.tanh(gate)) * both[:, H:]).astype(BF16)
    update = jnp.dot(hidden, w_down_ref[...], preferred_element_type=F32)
    return (values + update).astype(BF16)


def split(values):
    high = values.astype(BF16)
    return high, (values - high.astype(F32)).astype(BF16)


def pack_kernel(pair_hbm, single_hbm, frames_hbm, out_ref, own_ref, frames_ref, sems):
    local = own_ref.shape[0]
    copies = [
        pltpu.make_async_copy(single_hbm, own_ref.at[:, :S], sems.at[0]),
        pltpu.make_async_copy(frames_hbm, frames_ref, sems.at[1]),
    ]
    for half in range(2):
        copies.append(
            pltpu.make_async_copy(
                pair_hbm.at[half], out_ref.at[:, pl.ds(half * local, local)], sems.at[2 + half]
            )
        )
    for copy in copies:
        copy.start()
    copies[0].wait()
    copies[1].wait()
    rows = frames_ref[...]
    blank = jnp.zeros((local, 128 - 36), F32)
    turned = jnp.concatenate([rows, rows, rows, blank], axis=1)
    high = turned.astype(BF16).astype(F32)
    middle = (turned - high).astype(BF16).astype(F32)
    low = turned - high - middle
    lane = iota(turned.shape, 1)
    own_ref[:, S:] = jnp.where(lane < 12, high, jnp.where(lane < 24, middle, low)).astype(BF16)
    for dest in range(out_ref.shape[0]):
        for piece in range(SMALL):
            out_ref[dest, 2 * local + piece] = own_ref[:, piece * 128 : piece * 128 + 128]
    copies[2].wait()
    copies[3].wait()


def strided(ref, start, count, stride):
    return jnp.concatenate(
        [ref[t, pl.ds(start, count, stride=stride), :] for t in range(ref.shape[0])], axis=1
    )


def own_kernel(*refs):
    sources, refs = refs[:13], refs[13:]
    out_ref, heads_ref, rows_ref, gains_ref, wb_out_ref, w_loc_ref, wq_ref, wp_ref = refs[:8]
    held, refs = refs[8:19], refs[19:]
    loc_scr, sems = refs
    pair_hbm, *_ = sources
    n, local, _ = pair_hbm.shape
    targets = list(held) + [wq_ref, wp_ref]
    copies = []
    for k, (source, target) in enumerate(zip(sources, targets)):
        if k == 10:
            source = source.at[pl.ds(FEAT, 3 * PLANE)]
        copies.append(pltpu.make_async_copy(source, target, sems.at[k]))
        copies[k].start()
    pair_ref, w_swiglu_ref, w_down_ref, gain_ref, gamma_ref, cb_ref = held[:6]
    chain_ref, pad_ref, gain2_ref, wb_ref, loc_ref = held[6:]
    for copy in copies[:4]:
        copy.wait()
    gain = gain_ref[...].reshape(1, C)
    block = math.gcd(n, 128)

    def step(at):
        values = pair_ref[pl.ds(at, block)].astype(F32).reshape(-1, C)
        done = transition(values, gain, w_swiglu_ref, w_down_ref)
        out_ref[pl.ds(at, block)] = done.astype(F32).reshape(-1, local, C).astype(BF16)

    if n == block:
        step(0)
    else:
        pl.loop(0, n, step=block)(step)
    for copy in copies[4:]:
        copy.wait()

    diagonal = iota((HPAD, HEADS), 0) == iota((HPAD, HEADS), 1)

    def column(row):
        turned = jnp.sum(jnp.where(diagonal, row, 0.0), axis=1, keepdims=True)
        return jnp.broadcast_to(turned, (HPAD, 128))

    gamma = jax.nn.softplus(gamma_ref[...].reshape(1, HEADS))
    heads_ref[0] = column(gamma * (-0.5 * WEIGHT_C))
    heads_ref[1] = column(cb_ref[0:1, :])
    heads_ref[2] = column(cb_ref[1:2, :])
    rows_ref[0:1, :] = chain_ref[...].reshape(1, n)
    rows_ref[1:2, :] = pad_ref[...].reshape(1, n)
    gains_ref[0:1, :S] = gain2_ref[...].reshape(1, S)
    gains_ref[0:1, S:] = gain
    wb_out_ref[...] = jnp.concatenate(
        [wb_ref[...], jnp.zeros((HPAD - HEADS, C), BF16)], axis=0
    )
    local_rows = loc_ref[...].astype(F32)
    for t in range(S // 128):
        loc_scr[t] = local_rows[:, t * 128 : (t + 1) * 128]
    for y in range(3):
        w_loc_ref[y] = strided(loc_scr, y, PLANE, 3).astype(BF16)


def place(frame, triple):
    return [
        frame[3 * x : 3 * x + 1, :] * triple[0]
        + frame[3 * x + 1 : 3 * x + 2, :] * triple[1]
        + frame[3 * x + 2 : 3 * x + 3, :] * triple[2]
        + frame[9 + x : 10 + x, :]
        for x in range(3)
    ]


def head_of_lane(rows):
    lanes = iota((rows, WIDE), 1)
    return jnp.where(lanes < 256, lanes // CH, (lanes % 128) // VP)


def base_scores(
    queries, query_pts, high_keys, low_keys, key_pts, heads_ref, chain_all, chain_row, first
):
    local = queries.shape[0]
    n = high_keys.shape[1]
    rows = local * HPAD
    owned = (iota((HPAD, FEAT), 1) // CH == iota((HPAD, FEAT), 0))[None]
    spread = jnp.broadcast_to(queries.reshape(local, 1, FEAT), (local, HPAD, FEAT))
    high, low = split(jnp.where(owned, spread, 0.0).reshape(rows, FEAT))
    both = jnp.dot(jnp.concatenate([high, low], axis=0), high_keys, preferred_element_type=F32)
    dots = both[:rows] + both[rows:] + jnp.dot(high, low_keys, preferred_element_type=F32)
    distances = []
    blank = jnp.zeros((HPAD - HEADS, n), F32)
    for i in range(local):
        distance = 0.0
        for q, k in zip(query_pts, key_pts):
            apart = q[:, i : i + 1] - k
            distance = distance + apart * apart
        distances += [distance, blank]
    distance = jnp.concatenate(distances, axis=0)

    def per_row(index):
        wide = jnp.concatenate([heads_ref[index]] * max(1, n // 128), axis=1)[:, :n]
        return jnp.concatenate([wide] * local, axis=0)

    width = chain_all.shape[1]
    lanes, order = iota((local, width), 1), iota((local, width), 0)
    mine = jnp.sum(jnp.where(lanes == first + order, chain_all, 0), axis=1, keepdims=True)
    mine = jnp.broadcast_to(mine.reshape(local, 1, 1), (local, HPAD, n)).reshape(rows, n)
    chain = jnp.where(chain_row == mine, per_row(1), per_row(2))
    return WEIGHT_L * (dots * (1.0 / math.sqrt(CH)) + chain + per_row(0) * distance)


def partial_attention(
    recv_ref, at, base, real, high_value, low_value, gain, w_swiglu_ref, w_down_ref, wb_ref,
    pair_scr, attn_scr, sums_scr,
):
    nsrc, _, local, _ = recv_ref.shape
    n = nsrc * local
    rows = local * HPAD
    group = max(1, min(local, 512 // n))
    for start in range(0, local, group):
        block = recv_ref[:, pl.ds(at + start, group)].astype(F32)
        block = jnp.concatenate([block[:, k].reshape(n, C) for k in range(group)], axis=0)
        done = transition(block, gain, w_swiglu_ref, w_down_ref)
        for k in range(group):
            pair_scr[start + k] = done[k * n : (k + 1) * n]
    bias = jnp.concatenate([nt_dot(wb_ref[...], pair_scr[i]) for i in range(local)], axis=0)
    scores = base + WEIGHT_L * bias
    scores = jnp.where(jnp.broadcast_to(real, (rows, n)) > 0, scores, -1000000000.0)
    peak = jnp.max(scores, axis=-1, keepdims=True)
    expo = jnp.exp(scores - peak)
    total = jnp.sum(expo, axis=-1, keepdims=True)
    high, low = split(expo / total)
    attn_scr[:rows] = high
    attn_scr[rows:] = low
    for i in range(local):
        first = i * HPAD
        sums_scr[first : first + HPAD, :] = jnp.dot(
            high[first : first + HPAD], pair_scr[i], preferred_element_type=F32
        )
    both = jnp.dot(attn_scr[...], high_value, preferred_element_type=F32)
    every = both[:rows] + both[rows:]
    every += jnp.dot(attn_scr[:rows], low_value, preferred_element_type=F32)
    owned = head_of_lane(HPAD) == iota((HPAD, WIDE), 0)
    every = every.reshape(local, HPAD, WIDE)
    summed = jnp.sum(jnp.where(owned[None], every, 0.0), axis=1)
    diagonal = (iota((HPAD, HPAD), 0) == iota((HPAD, HPAD), 1))[None]

    def by_head(column):
        wide = jnp.broadcast_to(column.reshape(local, HPAD, 1), (local, HPAD, HPAD))
        return jnp.sum(jnp.where(diagonal, wide, 0.0), axis=1)

    pair_sums = [sums_scr[pl.ds(h, local, stride=HPAD), :] for h in range(HEADS)]
    return pair_sums, summed, by_head(peak), by_head(total)


def first_kernel(
    recv_ref,
    own_ref,
    partner_ref,
    heads_ref,
    rows_ref,
    gains_ref,
    wq_ref,
    wp_ref,
    wb_ref,
    w_swiglu_ref,
    w_down_ref,
    send_ref,
    value_ref,
    near_ref,
    keys_ref,
    key_pts_ref,
    query_ref,
    query_pts_ref,
    pts_scr,
    qp_scr,
    pair_scr,
    attn_scr,
    sums_scr,
):
    nsrc, _, local, _ = recv_ref.shape
    tiles, _, lane = pts_scr.shape
    n = nsrc * local
    me = lax.axis_index("rows")
    upper = me // nsrc

    def piece(index):
        return recv_ref[:, index].astype(F32).reshape(n, 128).astype(BF16)

    all_single = jnp.concatenate([piece(2 * local + k) for k in range(SMALL - 1)], axis=1)
    queries = jnp.concatenate(
        [partner_ref[...].astype(F32), own_ref[...].astype(F32)], axis=0
    ).astype(BF16)
    rows16, lanes16 = iota((16, 128), 0), iota((16, 128), 1)
    pick = ((lanes16 % 12 == rows16) & (lanes16 < 36)).astype(BF16)
    frames = nt_dot(pick, piece(2 * local + SMALL - 1))
    query_frames = nt_dot(pick, queries[:, S:])

    high_keys, low_keys = split(nt_dot(wq_ref[FEAT : 2 * FEAT, :], all_single))
    keys_ref[0] = high_keys
    keys_ref[1] = low_keys
    points = nt_dot(wp_ref[QPTS:, :], all_single)
    for t in range(tiles):
        pts_scr[t] = points[:, t * lane : (t + 1) * lane]
    features = nt_dot(queries[:, :S], wq_ref[:FEAT, :])
    qp_scr[...] = nt_dot(wp_ref[:QPTS, :], queries[:, :S])

    key_pts, query_pts = [], []
    for p in range(QP):
        key_pts += place(frames, [strided(pts_scr, 3 * p + y, HEADS, 3 * QP) for y in range(3)])
        query_pts += place(
            query_frames, [qp_scr[pl.ds(3 * p + y, HEADS, stride=3 * QP), :] for y in range(3)]
        )
    for k in range(3 * QP):
        key_pts_ref[k] = key_pts[k]
        query_pts_ref[k] = query_pts[k][:, local:]
    query_ref[...] = features[local:]

    chain_all = rows_ref[0:1, :]
    chain_row = jnp.where(upper == 0, chain_all[:, :n], chain_all[:, n:])
    real = jnp.where(upper == 0, rows_ref[1:2, :n], rows_ref[1:2, n:])
    near_ref[0:1, :] = chain_row
    near_ref[1:2, :] = real
    base = base_scores(
        features[:local], query_pts, high_keys, low_keys, key_pts, heads_ref, chain_all, chain_row,
        jnp.bitwise_xor(me, nsrc) * local,
    )

    planes = place(frames, [strided(pts_scr, QPTS + y, PLANE, 3) for y in range(3)])
    gap = jnp.zeros((n, 128 - PLANE), F32)
    values = [nt_dot(all_single, wq_ref[2 * FEAT :, :]), jnp.zeros((n, 256 - FEAT), F32)]
    for plane in planes:
        values += [plane.T, gap]
    high, low = split(jnp.concatenate(values, axis=1))
    value_ref[0] = high
    value_ref[1] = low

    pair_sums, summed, peak, total = partial_attention(
        recv_ref, (1 - upper) * local, base, real, high, low,
        gains_ref[0:1, S:], w_swiglu_ref, w_down_ref, wb_ref, pair_scr, attn_scr, sums_scr,
    )
    for h in range(HEADS):
        send_ref[h] = pair_sums[h].astype(BF16)
    high, low = split(summed)
    pieces = WIDE // 128
    for k in range(pieces):
        send_ref[HEADS + k] = high[:, k * 128 : (k + 1) * 128]
        send_ref[HEADS + pieces + k] = low[:, k * 128 : (k + 1) * 128]
    both = jnp.concatenate([peak, total], axis=1)
    high = both.astype(BF16).astype(F32)
    middle = (both - high).astype(BF16).astype(F32)
    low = both - high - middle
    blank = jnp.zeros((local, 128 - 6 * HPAD), F32)
    send_ref[PARTS - 1] = jnp.concatenate([high, middle, low, blank], axis=1).astype(BF16)


def second_kernel(
    recv_ref,
    value_ref,
    near_ref,
    keys_ref,
    key_pts_ref,
    query_ref,
    query_pts_ref,
    heads_ref,
    rows_ref,
    gains_ref,
    wb_ref,
    w_swiglu_ref,
    w_down_ref,
    sums_ref,
    wide_ref,
    stats_ref,
    pair_scr,
    attn_scr,
    sums_scr,
):
    nsrc, _, local, _ = recv_ref.shape
    me = lax.axis_index("rows")
    base = base_scores(
        query_ref[...], [query_pts_ref[k] for k in range(3 * QP)], keys_ref[0], keys_ref[1],
        [key_pts_ref[k] for k in range(3 * QP)], heads_ref, rows_ref[0:1, :], near_ref[0:1, :],
        me * local,
    )
    pair_sums, summed, peak, total = partial_attention(
        recv_ref, me // nsrc * local, base, near_ref[1:2, :], value_ref[0], value_ref[1],
        gains_ref[0:1, S:], w_swiglu_ref, w_down_ref, wb_ref, pair_scr, attn_scr, sums_scr,
    )
    for h in range(HEADS):
        sums_ref[h] = pair_sums[h]
    wide_ref[...] = summed
    stats_ref[...] = jnp.concatenate([peak, total], axis=1)


def finish_kernel(
    got_ref,
    sums_ref,
    wide_ref,
    stats_ref,
    own_ref,
    gains_ref,
    w_out_ref,
    w_loc_ref,
    out_ref,
):
    local = own_ref.shape[0]
    got = got_ref[PARTS - 1].astype(F32)
    width = 2 * HPAD
    got = got[:, :width] + got[:, width : 2 * width] + got[:, 2 * width : 3 * width]
    mine = stats_ref[...]
    peak = jnp.maximum(got[:, :HPAD], mine[:, :HPAD])
    got = got[:, HPAD:] * jnp.exp(got[:, :HPAD] - peak)
    mine = mine[:, HPAD:] * jnp.exp(mine[:, :HPAD] - peak)
    scale = 1.0 / (got + mine)
    got, mine = got * scale, mine * scale
    owner = head_of_lane(local)
    got_wide = jnp.zeros((local, WIDE), F32)
    mine_wide = jnp.zeros((local, WIDE), F32)
    pair_total = []
    for h in range(HEADS):
        got_share, mine_share = got[:, h : h + 1], mine[:, h : h + 1]
        got_wide = jnp.where(owner == h, got_share, got_wide)
        mine_wide = jnp.where(owner == h, mine_share, mine_wide)
        pair_total.append(got_share * got_ref[h].astype(F32) + mine_share * sums_ref[h])
    pieces = WIDE // 128
    sent = jnp.concatenate(
        [
            got_ref[HEADS + k].astype(F32) + got_ref[HEADS + pieces + k].astype(F32)
            for k in range(pieces)
        ],
        axis=1,
    )
    summed = got_wide * sent + mine_wide * wide_ref[...]

    parts = own_ref[:, S:].astype(F32)
    turned = parts[:, 0:12] + parts[:, 12:24] + parts[:, 24:36]
    shifted = [
        summed[:, 256 + 128 * x : 384 + 128 * x] - turned[:, 9 + x : 10 + x] for x in range(3)
    ]
    local_out = [
        turned[:, y : y + 1] * shifted[0]
        + turned[:, 3 + y : 4 + y] * shifted[1]
        + turned[:, 6 + y : 7 + y] * shifted[2]
        for y in range(3)
    ]
    lengths = jnp.sqrt(
        local_out[0] * local_out[0] + local_out[1] * local_out[1] + local_out[2] * local_out[2] + 1.0
    )
    update = jnp.dot(
        summed[:, :FEAT].astype(BF16), w_out_ref[:FEAT, :], preferred_element_type=F32
    )
    for y in range(3):
        update += jnp.dot(
            local_out[y][:, :PLANE].astype(BF16), w_loc_ref[y], preferred_element_type=F32
        )
    at = FEAT + 3 * PLANE
    update += jnp.dot(
        lengths[:, :PLANE].astype(BF16), w_out_ref[at : at + PLANE, :], preferred_element_type=F32
    )
    at += PLANE
    pair_total = jnp.concatenate(pair_total, axis=1).astype(BF16)
    update += jnp.dot(pair_total, w_out_ref[at:, :], preferred_element_type=F32)
    own_single = own_ref[:, :S].astype(F32)
    out_ref[...] = layer_norm(own_single + update, gains_ref[0:1, :S]).astype(BF16)


def in_hbm(arrays):
    return [pltpu.with_memory_space_constraint(array, pltpu.HBM) for array in arrays]


def whole(memory=pltpu.VMEM):
    return pl.BlockSpec(memory_space=memory)


def params(mib):
    return pltpu.CompilerParams(vmem_limit_bytes=mib * MIB)


def on_device(
    single_rep,
    pair_grid,
    frames,
    chain_ids,
    pad_mask,
    ln_pair_gain,
    w_swiglu,
    w_pair_down,
    w_bias,
    w_qkv,
    w_points,
    gamma_raw,
    chain_bias,
    w_out,
    ln_single_gain,
):
    n, local, _ = pair_grid.shape
    size = n // local
    nsrc = size // 2
    near = n // 2
    tiles = max(1, near // 128)
    large = 4 * (n // 128)
    halves = [list(range(nsrc)), list(range(nsrc, size))]
    across = [(i, i ^ nsrc) for i in range(size)]

    packed, own = pl.pallas_call(
        pack_kernel,
        out_shape=[
            jax.ShapeDtypeStruct((nsrc, 2 * local + SMALL, local, C), BF16),
            jax.ShapeDtypeStruct((local, S + 128), BF16),
        ],
        in_specs=[whole(pltpu.HBM)] * 3,
        out_specs=[whole(), whole()],
        scratch_shapes=[
            pltpu.VMEM((local, 12), F32),
            pltpu.SemaphoreType.DMA((4,)),
        ],
        compiler_params=params(4 + large),
        name="pack",
    )(*in_hbm([pair_grid.reshape(2, nsrc, local, local, C), single_rep, frames.T]))
    received = lax.all_to_all(
        packed, "rows", 0, 0, tiled=True, axis_index_groups=halves
    )
    partner = lax.ppermute(own, "rows", across)

    sources = [
        pair_grid,
        w_swiglu,
        w_pair_down,
        ln_pair_gain,
        gamma_raw,
        chain_bias,
        chain_ids,
        pad_mask,
        ln_single_gain,
        w_bias.T,
        w_out,
        w_qkv.T,
        w_points.T,
    ]
    held = [pltpu.VMEM(x.shape, x.dtype) for x in sources[:10]]
    held.append(pltpu.VMEM((3 * PLANE, S), BF16))
    pair_out, heads, rows, gains, wb, w_loc, wq, wp = pl.pallas_call(
        own_kernel,
        out_shape=[
            jax.ShapeDtypeStruct(pair_grid.shape, BF16),
            jax.ShapeDtypeStruct((3, HPAD, 128), F32),
            jax.ShapeDtypeStruct((2, n), jnp.int32),
            jax.ShapeDtypeStruct((1, S + C), F32),
            jax.ShapeDtypeStruct((HPAD, C), BF16),
            jax.ShapeDtypeStruct((3, PLANE, S), BF16),
            jax.ShapeDtypeStruct(sources[11].shape, BF16),
            jax.ShapeDtypeStruct(sources[12].shape, BF16),
        ],
        in_specs=[whole(pltpu.HBM)] * len(sources),
        out_specs=[whole()] * 8,
        scratch_shapes=held
        + [
            pltpu.VMEM((S // 128, 3 * PLANE, 128), F32),
            pltpu.SemaphoreType.DMA((len(sources),)),
        ],
        compiler_params=params(18 + large),
        name="own_transition",
    )(*in_hbm(sources))

    scratch = [
        pltpu.VMEM((local, near, C), BF16),
        pltpu.VMEM((2 * local * HPAD, near), BF16),
        pltpu.VMEM((local * HPAD, C), F32),
    ]
    send, *held = pl.pallas_call(
        first_kernel,
        out_shape=[
            jax.ShapeDtypeStruct((PARTS, local, 128), BF16),
            jax.ShapeDtypeStruct((2, near, WIDE), BF16),
            jax.ShapeDtypeStruct((2, near), jnp.int32),
            jax.ShapeDtypeStruct((2, FEAT, near), BF16),
            jax.ShapeDtypeStruct((3 * QP, HEADS, near), F32),
            jax.ShapeDtypeStruct((local, FEAT), F32),
            jax.ShapeDtypeStruct((3 * QP, HEADS, local), F32),
        ],
        in_specs=[whole()] * 11,
        out_specs=[whole()] * 7,
        scratch_shapes=[
            pltpu.VMEM((tiles, QPTS + 3 * PLANE, near // tiles), F32),
            pltpu.VMEM((QPTS, 2 * local), F32),
        ]
        + scratch,
        compiler_params=params(16 + large),
        name="first_half",
    )(received, own, partner, heads, rows, gains, wq, wp, wb, w_swiglu, w_pair_down)
    got = lax.ppermute(send, "rows", across)

    sums, wide, stats = pl.pallas_call(
        second_kernel,
        out_shape=[
            jax.ShapeDtypeStruct((HEADS, local, 128), F32),
            jax.ShapeDtypeStruct((local, WIDE), F32),
            jax.ShapeDtypeStruct((local, 2 * HPAD), F32),
        ],
        in_specs=[whole()] * 13,
        out_specs=[whole()] * 3,
        scratch_shapes=scratch,
        compiler_params=params(12 + large),
        name="second_half",
    )(received, *held, heads, rows, gains, wb, w_swiglu, w_pair_down)

    single_out = pl.pallas_call(
        finish_kernel,
        out_shape=jax.ShapeDtypeStruct((local, S), BF16),
        in_specs=[whole()] * 8,
        out_specs=whole(),
        compiler_params=params(12),
        name="finish",
    )(got, sums, wide, stats, own, gains, w_out, w_loc)
    return (single_out, pair_out)


def solution(mesh):
    placed = (
        P(("groups", "rows"), None),
        P("groups", "rows", None),
        P(None, ("groups", "rows")),
        P("groups"),
        P("groups"),
    ) + (P(),) * 10
    return jax.shard_map(
        on_device,
        mesh=mesh,
        in_specs=placed,
        out_specs=(P(("groups", "rows"), None), P("groups", "rows", None)),
        check_vma=False,
    )
```

```python
import math

import jax
import jax.numpy as jnp
from jax import lax
from jax.experimental import pallas as pl
from jax.experimental.pallas import tpu as pltpu
from jax.sharding import PartitionSpec as P

C = 128
S = 384
H = 512
HEADS = 12
CH = 16
QP = 4
VP = 8
HPAD = 16
FEAT = HEADS * CH
QPTS = HEADS * QP * 3
PLANE = HEADS * VP
WIDE = 256 + 3 * 128
SMALL = S // 128 + 1
PARTS = HEADS + WIDE // 128
F32 = jnp.float32
BF16 = jnp.bfloat16
NT = (((1,), (1,)), ((), ()))
MIB = 1024 * 1024
WEIGHT_L = math.sqrt(1.0 / 3.0)
WEIGHT_C = math.sqrt(2.0 / (9.0 * QP))


def iota(shape, dim):
    return lax.broadcasted_iota(jnp.int32, shape, dim)


def nt_dot(a, b):
    return lax.dot_general(a, b, NT, preferred_element_type=F32)


def layer_norm(values, gain):
    centre = jnp.mean(values, axis=-1, keepdims=True)
    centred = values - centre
    spread = jnp.mean(centred * centred, axis=-1, keepdims=True)
    return centred * lax.rsqrt(spread + 1e-05) * gain


def transition(values, gain, w_swiglu_ref, w_down_ref):
    normed = layer_norm(values, gain).astype(BF16)
    both = jnp.dot(normed, w_swiglu_ref[...], preferred_element_type=F32)
    gate = 0.5 * both[:, :H]
    hidden = (gate * (1.0 + jnp.tanh(gate)) * both[:, H:]).astype(BF16)
    update = jnp.dot(hidden, w_down_ref[...], preferred_element_type=F32)
    return (values + update).astype(BF16)


def split(values):
    high = values.astype(BF16)
    return high, (values - high.astype(F32)).astype(BF16)


def pack_kernel(
    pair_hbm, single_hbm, frames_hbm, out_hbm, own_ref, pair_ref, small_ref, frames_ref, in_sems, out_sems
):
    nsrc = pair_ref.shape[0]
    local = own_ref.shape[0]
    step = max(1, nsrc // 4)
    chunks = [(half, at) for at in range(0, nsrc, step) for half in range(2)]
    arrivals = []
    for k, (half, at) in enumerate(chunks):
        arrivals.append(
            pltpu.make_async_copy(
                pair_hbm.at[half, pl.ds(at, step)],
                pair_ref.at[pl.ds(at, step), pl.ds(half * local, local)],
                in_sems.at[k],
            )
        )
    rows_copies = [
        pltpu.make_async_copy(single_hbm, own_ref.at[:, :S], in_sems.at[len(chunks)]),
        pltpu.make_async_copy(frames_hbm, frames_ref, in_sems.at[len(chunks) + 1]),
    ]
    for copy in rows_copies + arrivals:
        copy.start()
    for copy in rows_copies:
        copy.wait()
    rows = frames_ref[...]
    blank = jnp.zeros((local, 128 - 36), F32)
    turned = jnp.concatenate([rows, rows, rows, blank], axis=1)
    high = turned.astype(BF16).astype(F32)
    middle = (turned - high).astype(BF16).astype(F32)
    low = turned - high - middle
    lane = iota(turned.shape, 1)
    own_ref[:, S:] = jnp.where(lane < 12, high, jnp.where(lane < 24, middle, low)).astype(BF16)
    for dest in range(nsrc):
        for piece in range(SMALL):
            small_ref[dest, piece] = own_ref[:, piece * 128 : piece * 128 + 128]
    departures = [
        pltpu.make_async_copy(small_ref, out_hbm.at[:, pl.ds(2 * local, SMALL)], out_sems.at[0])
    ]
    departures[0].start()
    for k in range(0, len(chunks), 2):
        arrivals[k].wait()
        arrivals[k + 1].wait()
        at = chunks[k][1]
        departures.append(
            pltpu.make_async_copy(
                pair_ref.at[pl.ds(at, step)],
                out_hbm.at[pl.ds(at, step), pl.ds(0, 2 * local)],
                out_sems.at[1 + k // 2],
            )
        )
        departures[-1].start()
    for copy in departures:
        copy.wait()


def strided(ref, start, count, stride):
    return jnp.concatenate(
        [ref[t, pl.ds(start, count, stride=stride), :] for t in range(ref.shape[0])], axis=1
    )


def own_kernel(*refs):
    sources, refs = refs[:13], refs[13:]
    out_ref, heads_ref, rows_ref, gains_ref, wb_out_ref, w_loc_ref, wq_ref, wp_ref = refs[:8]
    held, refs = refs[8:19], refs[19:]
    loc_scr, sems = refs
    pair_hbm, *_ = sources
    n, local, _ = pair_hbm.shape
    targets = list(held) + [wq_ref, wp_ref]
    copies = []
    for k, (source, target) in enumerate(zip(sources, targets)):
        if k == 10:
            source = source.at[pl.ds(FEAT, 3 * PLANE)]
        copies.append(pltpu.make_async_copy(source, target, sems.at[k]))
        copies[k].start()
    pair_ref, w_swiglu_ref, w_down_ref, gain_ref, gamma_ref, cb_ref = held[:6]
    chain_ref, pad_ref, gain2_ref, wb_ref, loc_ref = held[6:]
    for copy in copies[:4]:
        copy.wait()
    gain = gain_ref[...].reshape(1, C)
    block = math.gcd(n, 128)

    def step(at):
        values = pair_ref[pl.ds(at, block)].astype(F32).reshape(-1, C)
        done = transition(values, gain, w_swiglu_ref, w_down_ref)
        out_ref[pl.ds(at, block)] = done.astype(F32).reshape(-1, local, C).astype(BF16)

    if n == block:
        step(0)
    else:
        pl.loop(0, n, step=block)(step)
    for copy in copies[4:]:
        copy.wait()

    diagonal = iota((HPAD, HEADS), 0) == iota((HPAD, HEADS), 1)

    def column(row):
        turned = jnp.sum(jnp.where(diagonal, row, 0.0), axis=1, keepdims=True)
        return jnp.broadcast_to(turned, (HPAD, 128))

    gamma = jax.nn.softplus(gamma_ref[...].reshape(1, HEADS))
    heads_ref[0] = column(gamma * (-0.5 * WEIGHT_C))
    heads_ref[1] = column(cb_ref[0:1, :])
    heads_ref[2] = column(cb_ref[1:2, :])
    rows_ref[0:1, :] = chain_ref[...].reshape(1, n)
    rows_ref[1:2, :] = pad_ref[...].reshape(1, n)
    gains_ref[0:1, :S] = gain2_ref[...].reshape(1, S)
    gains_ref[0:1, S:] = gain
    wb_out_ref[...] = jnp.concatenate(
        [wb_ref[...], jnp.zeros((HPAD - HEADS, C), BF16)], axis=0
    )
    local_rows = loc_ref[...].astype(F32)
    for t in range(S // 128):
        loc_scr[t] = local_rows[:, t * 128 : (t + 1) * 128]
    for y in range(3):
        w_loc_ref[y] = strided(loc_scr, y, PLANE, 3).astype(BF16)


def place(frame, triple):
    return [
        frame[3 * x : 3 * x + 1, :] * triple[0]
        + frame[3 * x + 1 : 3 * x + 2, :] * triple[1]
        + frame[3 * x + 2 : 3 * x + 3, :] * triple[2]
        + frame[9 + x : 10 + x, :]
        for x in range(3)
    ]


def head_of_lane(rows):
    lanes = iota((rows, WIDE), 1)
    return jnp.where(lanes < 256, lanes // CH, (lanes % 128) // VP)


def base_scores(
    queries, query_pts, high_keys, low_keys, key_pts, heads_ref, chain_all, chain_row, first
):
    local = queries.shape[0]
    n = high_keys.shape[1]
    rows = local * HPAD
    owned = (iota((HPAD, FEAT), 1) // CH == iota((HPAD, FEAT), 0))[None]
    spread = jnp.broadcast_to(queries.reshape(local, 1, FEAT), (local, HPAD, FEAT))
    high, low = split(jnp.where(owned, spread, 0.0).reshape(rows, FEAT))
    both = jnp.dot(jnp.concatenate([high, low], axis=0), high_keys, preferred_element_type=F32)
    dots = both[:rows] + both[rows:] + jnp.dot(high, low_keys, preferred_element_type=F32)
    distances = []
    blank = jnp.zeros((HPAD - HEADS, n), F32)
    for i in range(local):
        distance = 0.0
        for q, k in zip(query_pts, key_pts):
            apart = q[:, i : i + 1] - k
            distance = distance + apart * apart
        distances += [distance, blank]
    distance = jnp.concatenate(distances, axis=0)

    def per_row(index):
        wide = jnp.concatenate([heads_ref[index]] * max(1, n // 128), axis=1)[:, :n]
        return jnp.concatenate([wide] * local, axis=0)

    width = chain_all.shape[1]
    lanes, order = iota((local, width), 1), iota((local, width), 0)
    mine = jnp.sum(jnp.where(lanes == first + order, chain_all, 0), axis=1, keepdims=True)
    mine = jnp.broadcast_to(mine.reshape(local, 1, 1), (local, HPAD, n)).reshape(rows, n)
    chain = jnp.where(chain_row == mine, per_row(1), per_row(2))
    return WEIGHT_L * (dots * (1.0 / math.sqrt(CH)) + chain + per_row(0) * distance)


def partial_attention(
    recv_ref, at, base, real, high_value, low_value, gain, w_swiglu_ref, w_down_ref, wb_ref,
    pair_scr, attn_scr, sums_scr,
):
    nsrc, _, local, _ = recv_ref.shape
    n = nsrc * local
    rows = local * HPAD
    group = max(1, min(local, 512 // n))
    for start in range(0, local, group):
        block = recv_ref[:, pl.ds(at + start, group)].astype(F32)
        block = jnp.concatenate([block[:, k].reshape(n, C) for k in range(group)], axis=0)
        done = transition(block, gain, w_swiglu_ref, w_down_ref)
        for k in range(group):
            pair_scr[start + k] = done[k * n : (k + 1) * n]
    bias = jnp.concatenate([nt_dot(wb_ref[...], pair_scr[i]) for i in range(local)], axis=0)
    scores = base + WEIGHT_L * bias
    scores = jnp.where(jnp.broadcast_to(real, (rows, n)) > 0, scores, -1000000000.0)
    peak = jnp.max(scores, axis=-1, keepdims=True)
    expo = jnp.exp(scores - peak)
    total = jnp.sum(expo, axis=-1, keepdims=True)
    high, low = split(expo / total)
    attn_scr[:rows] = high
    attn_scr[rows:] = low
    for i in range(local):
        first = i * HPAD
        sums_scr[first : first + HPAD, :] = jnp.dot(
            high[first : first + HPAD], pair_scr[i], preferred_element_type=F32
        )
    both = jnp.dot(attn_scr[...], high_value, preferred_element_type=F32)
    every = both[:rows] + both[rows:]
    every += jnp.dot(attn_scr[:rows], low_value, preferred_element_type=F32)
    owned = head_of_lane(HPAD) == iota((HPAD, WIDE), 0)
    every = every.reshape(local, HPAD, WIDE)
    summed = jnp.sum(jnp.where(owned[None], every, 0.0), axis=1)
    diagonal = (iota((HPAD, HPAD), 0) == iota((HPAD, HPAD), 1))[None]

    level = jnp.broadcast_to((peak + jnp.log(total)).reshape(local, HPAD, 1), (local, HPAD, HPAD))
    level = jnp.sum(jnp.where(diagonal, level, 0.0), axis=1)
    pair_sums = [sums_scr[pl.ds(h, local, stride=HPAD), :] for h in range(HEADS)]
    return pair_sums, summed, level


def origin(row_ref):
    parts = row_ref[:, S:].astype(F32)
    return parts[:, 0:12] + parts[:, 12:24] + parts[:, 24:36]


def first_kernel(
    recv_ref,
    own_ref,
    partner_ref,
    heads_ref,
    rows_ref,
    gains_ref,
    wq_ref,
    wp_ref,
    wb_ref,
    w_swiglu_ref,
    w_down_ref,
    send_ref,
    value_ref,
    near_ref,
    keys_ref,
    key_pts_ref,
    query_ref,
    query_pts_ref,
    pts_scr,
    qp_scr,
    pair_scr,
    attn_scr,
    sums_scr,
):
    nsrc, _, local, _ = recv_ref.shape
    tiles, _, lane = pts_scr.shape
    n = nsrc * local
    me = lax.axis_index("rows")
    upper = me // nsrc

    def piece(index):
        return recv_ref[:, index].astype(F32).reshape(n, 128).astype(BF16)

    all_single = jnp.concatenate([piece(2 * local + k) for k in range(SMALL - 1)], axis=1)
    queries = jnp.concatenate(
        [partner_ref[...].astype(F32), own_ref[...].astype(F32)], axis=0
    ).astype(BF16)
    rows16, lanes16 = iota((16, 128), 0), iota((16, 128), 1)
    pick = ((lanes16 % 12 == rows16) & (lanes16 < 36)).astype(BF16)
    frames = nt_dot(pick, piece(2 * local + SMALL - 1))
    query_frames = nt_dot(pick, queries[:, S:])

    high_keys, low_keys = split(nt_dot(wq_ref[FEAT : 2 * FEAT, :], all_single))
    keys_ref[0] = high_keys
    keys_ref[1] = low_keys
    points = nt_dot(wp_ref[QPTS:, :], all_single)
    for t in range(tiles):
        pts_scr[t] = points[:, t * lane : (t + 1) * lane]
    features = nt_dot(queries[:, :S], wq_ref[:FEAT, :])
    qp_scr[...] = nt_dot(wp_ref[:QPTS, :], queries[:, :S])

    key_pts, query_pts = [], []
    for p in range(QP):
        key_pts += place(frames, [strided(pts_scr, 3 * p + y, HEADS, 3 * QP) for y in range(3)])
        query_pts += place(
            query_frames, [qp_scr[pl.ds(3 * p + y, HEADS, stride=3 * QP), :] for y in range(3)]
        )
    for k in range(3 * QP):
        key_pts_ref[k] = key_pts[k]
        query_pts_ref[k] = query_pts[k][:, local:]
    query_ref[...] = features[local:]

    chain_all = rows_ref[0:1, :]
    chain_row = jnp.where(upper == 0, chain_all[:, :n], chain_all[:, n:])
    real = jnp.where(upper == 0, rows_ref[1:2, :n], rows_ref[1:2, n:])
    near_ref[0:1, :] = chain_row
    near_ref[1:2, :] = real
    base = base_scores(
        features[:local], query_pts, high_keys, low_keys, key_pts, heads_ref, chain_all, chain_row,
        jnp.bitwise_xor(me, nsrc) * local,
    )

    planes = place(frames, [strided(pts_scr, QPTS + y, PLANE, 3) for y in range(3)])
    gap = jnp.zeros((n, 128 - PLANE), F32)
    values = [nt_dot(all_single, wq_ref[2 * FEAT :, :]), jnp.zeros((n, 256 - FEAT), F32)]
    for plane in planes:
        values += [plane.T, gap]
    high, low = split(jnp.concatenate(values, axis=1))
    value_ref[0] = high
    value_ref[1] = low

    pair_sums, summed, level = partial_attention(
        recv_ref, (1 - upper) * local, base, real, high, low,
        gains_ref[0:1, S:], w_swiglu_ref, w_down_ref, wb_ref, pair_scr, attn_scr, sums_scr,
    )
    for h in range(HEADS):
        send_ref[h] = pair_sums[h].astype(BF16)
    turned = origin(partner_ref)
    send_ref[HEADS] = summed[:, :128].astype(BF16)
    send_ref[HEADS + 1] = summed[:, 128:256].astype(BF16)
    high = level.astype(BF16).astype(F32)
    middle = (level - high).astype(BF16).astype(F32)
    low = level - high - middle
    blank = jnp.zeros((local, 128 - PLANE - HPAD), F32)
    for x, part in enumerate([high, middle, low]):
        plane = summed[:, 256 + 128 * x : 256 + 128 * x + PLANE] - turned[:, 9 + x : 10 + x]
        send_ref[HEADS + 2 + x] = jnp.concatenate([plane, part, blank], axis=1).astype(BF16)


def second_kernel(
    recv_ref,
    value_ref,
    near_ref,
    keys_ref,
    key_pts_ref,
    query_ref,
    query_pts_ref,
    heads_ref,
    rows_ref,
    gains_ref,
    wb_ref,
    w_swiglu_ref,
    w_down_ref,
    own_ref,
    sums_ref,
    wide_ref,
    level_ref,
    pair_scr,
    attn_scr,
    sums_scr,
):
    nsrc, _, local, _ = recv_ref.shape
    me = lax.axis_index("rows")
    base = base_scores(
        query_ref[...], [query_pts_ref[k] for k in range(3 * QP)], keys_ref[0], keys_ref[1],
        [key_pts_ref[k] for k in range(3 * QP)], heads_ref, rows_ref[0:1, :], near_ref[0:1, :],
        me * local,
    )
    pair_sums, summed, level = partial_attention(
        recv_ref, me // nsrc * local, base, near_ref[1:2, :], value_ref[0], value_ref[1],
        gains_ref[0:1, S:], w_swiglu_ref, w_down_ref, wb_ref, pair_scr, attn_scr, sums_scr,
    )
    for h in range(HEADS):
        sums_ref[h] = pair_sums[h]
    turned = origin(own_ref)
    wide_ref[:, :256] = summed[:, :256]
    for x in range(3):
        at = 256 + 128 * x
        wide_ref[:, at : at + 128] = summed[:, at : at + 128] - turned[:, 9 + x : 10 + x]
    level_ref[...] = jnp.concatenate(
        [jnp.zeros((local, PLANE), F32), level, jnp.zeros((local, 128 - PLANE - HPAD), F32)], axis=1
    )


def finish_kernel(
    got_ref,
    sums_ref,
    wide_ref,
    level_ref,
    own_ref,
    gains_ref,
    w_out_ref,
    w_loc_ref,
    out_ref,
):
    local = own_ref.shape[0]
    planes = [got_ref[HEADS + 2 + x].astype(F32) for x in range(3)]
    got = 1.0 / (1.0 + jnp.exp(level_ref[...] - (planes[0] + planes[1] + planes[2])))
    lanes = iota((local, 128), 1)
    low_share = jnp.zeros((local, 128), F32)
    high_share = jnp.zeros((local, 128), F32)
    plane_share = jnp.zeros((local, 128), F32)
    pair_total = []
    for h in range(HEADS):
        share = jnp.broadcast_to(got[:, PLANE + h : PLANE + h + 1], (local, 128))
        low_share = jnp.where(lanes // CH == h, share, low_share)
        high_share = jnp.where(lanes // CH + 8 == h, share, high_share)
        plane_share = jnp.where(lanes // VP == h, share, plane_share)
        mine = sums_ref[h]
        pair_total.append(mine + share * (got_ref[h].astype(F32) - mine))

    def joined(at, share, theirs):
        mine = wide_ref[:, at : at + 128]
        return mine + share * (theirs - mine)

    features = [
        joined(0, low_share, got_ref[HEADS].astype(F32)),
        joined(128, high_share, got_ref[HEADS + 1].astype(F32)),
    ]
    shifted = [joined(256 + 128 * x, plane_share, planes[x]) for x in range(3)]

    turned = origin(own_ref)
    local_out = [
        turned[:, y : y + 1] * shifted[0]
        + turned[:, 3 + y : 4 + y] * shifted[1]
        + turned[:, 6 + y : 7 + y] * shifted[2]
        for y in range(3)
    ]
    lengths = jnp.sqrt(
        local_out[0] * local_out[0] + local_out[1] * local_out[1] + local_out[2] * local_out[2] + 1.0
    )
    update = jnp.dot(
        jnp.concatenate(features, axis=1)[:, :FEAT].astype(BF16),
        w_out_ref[:FEAT, :],
        preferred_element_type=F32,
    )
    for y in range(3):
        update += jnp.dot(
            local_out[y][:, :PLANE].astype(BF16), w_loc_ref[y], preferred_element_type=F32
        )
    at = FEAT + 3 * PLANE
    update += jnp.dot(
        lengths[:, :PLANE].astype(BF16), w_out_ref[at : at + PLANE, :], preferred_element_type=F32
    )
    at += PLANE
    pair_total = jnp.concatenate(pair_total, axis=1).astype(BF16)
    update += jnp.dot(pair_total, w_out_ref[at:, :], preferred_element_type=F32)
    own_single = own_ref[:, :S].astype(F32)
    out_ref[...] = layer_norm(own_single + update, gains_ref[0:1, :S]).astype(BF16)


def in_hbm(arrays):
    return [pltpu.with_memory_space_constraint(array, pltpu.HBM) for array in arrays]


def whole(memory=pltpu.VMEM):
    return pl.BlockSpec(memory_space=memory)


def params(mib):
    return pltpu.CompilerParams(vmem_limit_bytes=mib * MIB)


def on_device(
    single_rep,
    pair_grid,
    frames,
    chain_ids,
    pad_mask,
    ln_pair_gain,
    w_swiglu,
    w_pair_down,
    w_bias,
    w_qkv,
    w_points,
    gamma_raw,
    chain_bias,
    w_out,
    ln_single_gain,
):
    n, local, _ = pair_grid.shape
    size = n // local
    nsrc = size // 2
    near = n // 2
    tiles = max(1, near // 128)
    large = 4 * (n // 128)
    halves = [list(range(nsrc)), list(range(nsrc, size))]
    across = [(i, i ^ nsrc) for i in range(size)]

    packed, own = pl.pallas_call(
        pack_kernel,
        out_shape=[
            jax.ShapeDtypeStruct((nsrc, 2 * local + SMALL, local, C), BF16),
            jax.ShapeDtypeStruct((local, S + 128), BF16),
        ],
        in_specs=[whole(pltpu.HBM)] * 3,
        out_specs=[whole(pltpu.HBM), whole()],
        scratch_shapes=[
            pltpu.VMEM((nsrc, 2 * local, local, C), BF16),
            pltpu.VMEM((nsrc, SMALL, local, C), BF16),
            pltpu.VMEM((local, 12), F32),
            pltpu.SemaphoreType.DMA((10,)),
            pltpu.SemaphoreType.DMA((5,)),
        ],
        compiler_params=params(4 + large),
        name="pack",
    )(*in_hbm([pair_grid.reshape(2, nsrc, local, local, C), single_rep, frames.T]))
    received = lax.all_to_all(
        packed, "rows", 0, 0, tiled=True, axis_index_groups=halves
    )
    partner = lax.ppermute(own, "rows", across)

    sources = [
        pair_grid,
        w_swiglu,
        w_pair_down,
        ln_pair_gain,
        gamma_raw,
        chain_bias,
        chain_ids,
        pad_mask,
        ln_single_gain,
        w_bias.T,
        w_out,
        w_qkv.T,
        w_points.T,
    ]
    held = [pltpu.VMEM(x.shape, x.dtype) for x in sources[:10]]
    held.append(pltpu.VMEM((3 * PLANE, S), BF16))
    pair_out, heads, rows, gains, wb, w_loc, wq, wp = pl.pallas_call(
        own_kernel,
        out_shape=[
            jax.ShapeDtypeStruct(pair_grid.shape, BF16),
            jax.ShapeDtypeStruct((3, HPAD, 128), F32),
            jax.ShapeDtypeStruct((2, n), jnp.int32),
            jax.ShapeDtypeStruct((1, S + C), F32),
            jax.ShapeDtypeStruct((HPAD, C), BF16),
            jax.ShapeDtypeStruct((3, PLANE, S), BF16),
            jax.ShapeDtypeStruct(sources[11].shape, BF16),
            jax.ShapeDtypeStruct(sources[12].shape, BF16),
        ],
        in_specs=[whole(pltpu.HBM)] * len(sources),
        out_specs=[whole()] * 8,
        scratch_shapes=held
        + [
            pltpu.VMEM((S // 128, 3 * PLANE, 128), F32),
            pltpu.SemaphoreType.DMA((len(sources),)),
        ],
        compiler_params=params(18 + large),
        name="own_transition",
    )(*in_hbm(sources))

    scratch = [
        pltpu.VMEM((local, near, C), BF16),
        pltpu.VMEM((2 * local * HPAD, near), BF16),
        pltpu.VMEM((local * HPAD, C), F32),
    ]
    send, *held = pl.pallas_call(
        first_kernel,
        out_shape=[
            jax.ShapeDtypeStruct((PARTS, local, 128), BF16),
            jax.ShapeDtypeStruct((2, near, WIDE), BF16),
            jax.ShapeDtypeStruct((2, near), jnp.int32),
            jax.ShapeDtypeStruct((2, FEAT, near), BF16),
            jax.ShapeDtypeStruct((3 * QP, HEADS, near), F32),
            jax.ShapeDtypeStruct((local, FEAT), F32),
            jax.ShapeDtypeStruct((3 * QP, HEADS, local), F32),
        ],
        in_specs=[whole()] * 11,
        out_specs=[whole()] * 7,
        scratch_shapes=[
            pltpu.VMEM((tiles, QPTS + 3 * PLANE, near // tiles), F32),
            pltpu.VMEM((QPTS, 2 * local), F32),
        ]
        + scratch,
        compiler_params=params(16 + large),
        name="first_half",
    )(received, own, partner, heads, rows, gains, wq, wp, wb, w_swiglu, w_pair_down)
    got = lax.ppermute(send, "rows", across)

    sums, wide, level = pl.pallas_call(
        second_kernel,
        out_shape=[
            jax.ShapeDtypeStruct((HEADS, local, 128), F32),
            jax.ShapeDtypeStruct((local, WIDE), F32),
            jax.ShapeDtypeStruct((local, 128), F32),
        ],
        in_specs=[whole()] * 14,
        out_specs=[whole()] * 3,
        scratch_shapes=scratch,
        compiler_params=params(12 + large),
        name="second_half",
    )(received, *held, heads, rows, gains, wb, w_swiglu, w_pair_down, own)

    single_out = pl.pallas_call(
        finish_kernel,
        out_shape=jax.ShapeDtypeStruct((local, S), BF16),
        in_specs=[whole()] * 8,
        out_specs=whole(),
        compiler_params=params(12),
        name="finish",
    )(got, sums, wide, level, own, gains, w_out, w_loc)
    return (single_out, pair_out)


def solution(mesh):
    placed = (
        P(("groups", "rows"), None),
        P("groups", "rows", None),
        P(None, ("groups", "rows")),
        P("groups"),
        P("groups"),
    ) + (P(),) * 10
    return jax.shard_map(
        on_device,
        mesh=mesh,
        in_specs=placed,
        out_specs=(P(("groups", "rows"), None), P("groups", "rows", None)),
        check_vma=False,
    )
```

```python
import math

import jax
import jax.numpy as jnp
from jax import lax
from jax.experimental import pallas as pl
from jax.experimental.pallas import tpu as pltpu
from jax.sharding import PartitionSpec as P

C = 128
S = 384
H = 512
HEADS = 12
CH = 16
QP = 4
VP = 8
HPAD = 16
FEAT = HEADS * CH
QPTS = HEADS * QP * 3
PLANE = HEADS * VP
WIDE = 256 + 3 * 128
SMALL = S // 128 + 1
PARTS = HEADS + WIDE // 128
F32 = jnp.float32
BF16 = jnp.bfloat16
NT = (((1,), (1,)), ((), ()))
MIB = 1024 * 1024
WEIGHT_L = math.sqrt(1.0 / 3.0)
WEIGHT_C = math.sqrt(2.0 / (9.0 * QP))


def iota(shape, dim):
    return lax.broadcasted_iota(jnp.int32, shape, dim)


def nt_dot(a, b):
    return lax.dot_general(a, b, NT, preferred_element_type=F32)


def layer_norm(values, gain):
    centre = jnp.mean(values, axis=-1, keepdims=True)
    centred = values - centre
    spread = jnp.mean(centred * centred, axis=-1, keepdims=True)
    return centred * lax.rsqrt(spread + 1e-05) * gain


def transition(values, gain, w_swiglu_ref, w_down_ref):
    normed = layer_norm(values, gain).astype(BF16)
    both = jnp.dot(normed, w_swiglu_ref[...], preferred_element_type=F32)
    gate = 0.5 * both[:, :H]
    hidden = (gate * (1.0 + jnp.tanh(gate)) * both[:, H:]).astype(BF16)
    update = jnp.dot(hidden, w_down_ref[...], preferred_element_type=F32)
    return (values + update).astype(BF16)


def split(values):
    high = values.astype(BF16)
    return high, (values - high.astype(F32)).astype(BF16)


def pack_kernel(
    pair_hbm, single_hbm, frames_hbm, out_hbm, own_ref, pair_ref, small_ref, frames_ref, in_sems, out_sems
):
    nsrc = pair_ref.shape[0]
    local = own_ref.shape[0]
    step = max(1, nsrc // 4)
    chunks = [(half, at) for at in range(0, nsrc, step) for half in range(2)]
    arrivals = []
    for k, (half, at) in enumerate(chunks):
        arrivals.append(
            pltpu.make_async_copy(
                pair_hbm.at[half, pl.ds(at, step)],
                pair_ref.at[pl.ds(at, step), pl.ds(half * local, local)],
                in_sems.at[k],
            )
        )
    rows_copies = [
        pltpu.make_async_copy(single_hbm, own_ref.at[:, :S], in_sems.at[len(chunks)]),
        pltpu.make_async_copy(frames_hbm, frames_ref, in_sems.at[len(chunks) + 1]),
    ]
    for copy in rows_copies + arrivals:
        copy.start()
    for copy in rows_copies:
        copy.wait()
    rows = frames_ref[...]
    blank = jnp.zeros((local, 128 - 36), F32)
    turned = jnp.concatenate([rows, rows, rows, blank], axis=1)
    high = turned.astype(BF16).astype(F32)
    middle = (turned - high).astype(BF16).astype(F32)
    low = turned - high - middle
    lane = iota(turned.shape, 1)
    own_ref[:, S:] = jnp.where(lane < 12, high, jnp.where(lane < 24, middle, low)).astype(BF16)
    for dest in range(nsrc):
        for piece in range(SMALL):
            small_ref[dest, piece] = own_ref[:, piece * 128 : piece * 128 + 128]
    departures = [
        pltpu.make_async_copy(small_ref, out_hbm.at[:, pl.ds(2 * local, SMALL)], out_sems.at[0])
    ]
    departures[0].start()
    for k in range(0, len(chunks), 2):
        arrivals[k].wait()
        arrivals[k + 1].wait()
        at = chunks[k][1]
        departures.append(
            pltpu.make_async_copy(
                pair_ref.at[pl.ds(at, step)],
                out_hbm.at[pl.ds(at, step), pl.ds(0, 2 * local)],
                out_sems.at[1 + k // 2],
            )
        )
        departures[-1].start()
    for copy in departures:
        copy.wait()


def strided(ref, start, count, stride):
    return jnp.concatenate(
        [ref[t, pl.ds(start, count, stride=stride), :] for t in range(ref.shape[0])], axis=1
    )


def own_kernel(*refs):
    sources, refs = refs[:13], refs[13:]
    out_ref, heads_ref, rows_ref, gains_ref, wb_out_ref, w_loc_ref, wq_ref, wp_ref = refs[:8]
    held, refs = refs[8:19], refs[19:]
    loc_scr, sems = refs
    pair_hbm, *_ = sources
    n, local, _ = pair_hbm.shape
    targets = list(held) + [wq_ref, wp_ref]
    copies = []
    for k, (source, target) in enumerate(zip(sources, targets)):
        if k == 10:
            source = source.at[pl.ds(FEAT, 3 * PLANE)]
        copies.append(pltpu.make_async_copy(source, target, sems.at[k]))
        copies[k].start()
    pair_ref, w_swiglu_ref, w_down_ref, gain_ref, gamma_ref, cb_ref = held[:6]
    chain_ref, pad_ref, gain2_ref, wb_ref, loc_ref = held[6:]
    for copy in copies[:4]:
        copy.wait()
    gain = gain_ref[...].reshape(1, C)
    block = math.gcd(n, 128)

    def step(at):
        values = pair_ref[pl.ds(at, block)].astype(F32).reshape(-1, C)
        done = transition(values, gain, w_swiglu_ref, w_down_ref)
        out_ref[pl.ds(at, block)] = done.astype(F32).reshape(-1, local, C).astype(BF16)

    if n == block:
        step(0)
    else:
        pl.loop(0, n, step=block)(step)
    for copy in copies[4:]:
        copy.wait()

    diagonal = iota((HPAD, HEADS), 0) == iota((HPAD, HEADS), 1)

    def column(row):
        turned = jnp.sum(jnp.where(diagonal, row, 0.0), axis=1, keepdims=True)
        return jnp.broadcast_to(turned, (HPAD, 128))

    gamma = jax.nn.softplus(gamma_ref[...].reshape(1, HEADS))
    heads_ref[0] = column(gamma * (-0.5 * WEIGHT_C))
    heads_ref[1] = column(cb_ref[0:1, :])
    heads_ref[2] = column(cb_ref[1:2, :])
    rows_ref[0:1, :] = chain_ref[...].reshape(1, n)
    rows_ref[1:2, :] = pad_ref[...].reshape(1, n)
    gains_ref[0:1, :S] = gain2_ref[...].reshape(1, S)
    gains_ref[0:1, S:] = gain
    wb_out_ref[...] = jnp.concatenate(
        [wb_ref[...], jnp.zeros((HPAD - HEADS, C), BF16)], axis=0
    )
    local_rows = loc_ref[...].astype(F32)
    for t in range(S // 128):
        loc_scr[t] = local_rows[:, t * 128 : (t + 1) * 128]
    for y in range(3):
        w_loc_ref[y] = strided(loc_scr, y, PLANE, 3).astype(BF16)


def place(frame, triple):
    return [
        frame[3 * x : 3 * x + 1, :] * triple[0]
        + frame[3 * x + 1 : 3 * x + 2, :] * triple[1]
        + frame[3 * x + 2 : 3 * x + 3, :] * triple[2]
        + frame[9 + x : 10 + x, :]
        for x in range(3)
    ]


def head_of_lane(rows):
    lanes = iota((rows, WIDE), 1)
    return jnp.where(lanes < 256, lanes // CH, (lanes % 128) // VP)


def base_scores(
    queries, query_pts, high_keys, low_keys, key_pts, heads_ref, chain_all, chain_row, first
):
    local = queries.shape[0]
    n = high_keys.shape[1]
    rows = local * HPAD
    owned = (iota((HPAD, FEAT), 1) // CH == iota((HPAD, FEAT), 0))[None]
    spread = jnp.broadcast_to(queries.reshape(local, 1, FEAT), (local, HPAD, FEAT))
    high, low = split(jnp.where(owned, spread, 0.0).reshape(rows, FEAT))
    both = jnp.dot(jnp.concatenate([high, low], axis=0), high_keys, preferred_element_type=F32)
    dots = both[:rows] + both[rows:] + jnp.dot(high, low_keys, preferred_element_type=F32)
    distances = []
    blank = jnp.zeros((HPAD - HEADS, n), F32)
    for i in range(local):
        distance = 0.0
        for q, k in zip(query_pts, key_pts):
            apart = q[:, i : i + 1] - k
            distance = distance + apart * apart
        distances += [distance, blank]
    distance = jnp.concatenate(distances, axis=0)

    def per_row(index):
        wide = jnp.concatenate([heads_ref[index]] * max(1, n // 128), axis=1)[:, :n]
        return jnp.concatenate([wide] * local, axis=0)

    width = chain_all.shape[1]
    lanes, order = iota((local, width), 1), iota((local, width), 0)
    mine = jnp.sum(jnp.where(lanes == first + order, chain_all, 0), axis=1, keepdims=True)
    mine = jnp.broadcast_to(mine.reshape(local, 1, 1), (local, HPAD, n)).reshape(rows, n)
    chain = jnp.where(chain_row == mine, per_row(1), per_row(2))
    return WEIGHT_L * (dots * (1.0 / math.sqrt(CH)) + chain + per_row(0) * distance)


def pair_rows(recv_ref, at, gain, w_swiglu_ref, w_down_ref, pair_scr):
    nsrc, _, local, _ = recv_ref.shape
    n = nsrc * local
    group = max(1, min(local, 512 // n))
    for start in range(0, local, group):
        block = recv_ref[:, pl.ds(at + start, group)].astype(F32)
        block = jnp.concatenate([block[:, k].reshape(n, C) for k in range(group)], axis=0)
        done = transition(block, gain, w_swiglu_ref, w_down_ref)
        for k in range(group):
            pair_scr[start + k] = done[k * n : (k + 1) * n]


def partial_attention(base, real, high_value, low_value, wb_ref, pair_scr, attn_scr, sums_scr):
    local, n, _ = pair_scr.shape
    rows = local * HPAD
    bias = jnp.concatenate([nt_dot(wb_ref[...], pair_scr[i]) for i in range(local)], axis=0)
    scores = base + WEIGHT_L * bias
    scores = jnp.where(jnp.broadcast_to(real, (rows, n)) > 0, scores, -1000000000.0)
    peak = jnp.max(scores, axis=-1, keepdims=True)
    expo = jnp.exp(scores - peak)
    high, low = split(expo)
    total = jnp.sum(expo, axis=-1, keepdims=True)
    share = 1.0 / total
    attn_scr[:rows] = high
    attn_scr[rows:] = low
    for i in range(local):
        at = i * HPAD
        sums_scr[at : at + HPAD, :] = share[at : at + HPAD] * jnp.dot(
            high[at : at + HPAD], pair_scr[i], preferred_element_type=F32
        )
    both = jnp.dot(attn_scr[...], high_value, preferred_element_type=F32)
    every = both[:rows] + both[rows:]
    every += jnp.dot(attn_scr[:rows], low_value, preferred_element_type=F32)
    every *= share
    owned = head_of_lane(HPAD) == iota((HPAD, WIDE), 0)
    every = every.reshape(local, HPAD, WIDE)
    summed = jnp.sum(jnp.where(owned[None], every, 0.0), axis=1)
    diagonal = (iota((HPAD, HPAD), 0) == iota((HPAD, HPAD), 1))[None]

    level = jnp.broadcast_to((peak + jnp.log(total)).reshape(local, HPAD, 1), (local, HPAD, HPAD))
    level = jnp.sum(jnp.where(diagonal, level, 0.0), axis=1)
    pair_sums = [sums_scr[pl.ds(h, local, stride=HPAD), :] for h in range(HEADS)]
    return pair_sums, summed, level


def origin(row_ref):
    parts = row_ref[:, S:].astype(F32)
    return parts[:, 0:12] + parts[:, 12:24] + parts[:, 24:36]


def first_kernel(
    recv_ref,
    own_ref,
    partner_ref,
    heads_ref,
    rows_ref,
    gains_ref,
    wq_ref,
    wp_ref,
    wb_ref,
    w_swiglu_ref,
    w_down_ref,
    send_ref,
    value_ref,
    near_ref,
    keys_ref,
    key_pts_ref,
    query_ref,
    query_pts_ref,
    pts_scr,
    qp_scr,
    pair_scr,
    attn_scr,
    sums_scr,
):
    nsrc, _, local, _ = recv_ref.shape
    tiles, _, lane = pts_scr.shape
    n = nsrc * local
    me = lax.axis_index("rows")
    upper = me // nsrc

    def piece(index):
        return recv_ref[:, index].astype(F32).reshape(n, 128).astype(BF16)

    all_single = jnp.concatenate([piece(2 * local + k) for k in range(SMALL - 1)], axis=1)
    queries = jnp.concatenate(
        [partner_ref[...].astype(F32), own_ref[...].astype(F32)], axis=0
    ).astype(BF16)
    rows16, lanes16 = iota((16, 128), 0), iota((16, 128), 1)
    pick = ((lanes16 % 12 == rows16) & (lanes16 < 36)).astype(BF16)
    frames = nt_dot(pick, piece(2 * local + SMALL - 1))
    query_frames = nt_dot(pick, queries[:, S:])

    high_keys, low_keys = split(nt_dot(wq_ref[FEAT : 2 * FEAT, :], all_single))
    keys_ref[0] = high_keys
    keys_ref[1] = low_keys
    points = nt_dot(wp_ref[QPTS:, :], all_single)
    for t in range(tiles):
        pts_scr[t] = points[:, t * lane : (t + 1) * lane]
    features = nt_dot(queries[:, :S], wq_ref[:FEAT, :])
    qp_scr[:QPTS, :] = nt_dot(wp_ref[:QPTS, :], queries[:, :S])

    key_pts, query_pts = [], []
    for p in range(QP):
        key_pts += place(frames, [strided(pts_scr, 3 * p + y, HEADS, 3 * QP) for y in range(3)])
        query_pts += place(
            query_frames, [qp_scr[pl.ds(3 * p + y, HEADS, stride=3 * QP), :] for y in range(3)]
        )
    for k in range(3 * QP):
        key_pts_ref[k] = key_pts[k]
        query_pts_ref[k] = query_pts[k][:, local:]
    query_ref[...] = features[local:]

    chain_all = rows_ref[0:1, :]
    chain_row = jnp.where(upper == 0, chain_all[:, :n], chain_all[:, n:])
    real = jnp.where(upper == 0, rows_ref[1:2, :n], rows_ref[1:2, n:])
    near_ref[0:1, :] = chain_row
    near_ref[1:2, :] = real
    base = base_scores(
        features[:local], query_pts, high_keys, low_keys, key_pts, heads_ref, chain_all, chain_row,
        jnp.bitwise_xor(me, nsrc) * local,
    )

    planes = place(frames, [strided(pts_scr, QPTS + y, PLANE, 3) for y in range(3)])
    gap = jnp.zeros((n, 128 - PLANE), F32)
    values = [nt_dot(all_single, wq_ref[2 * FEAT :, :]), jnp.zeros((n, 256 - FEAT), F32)]
    for plane in planes:
        values += [plane.T, gap]
    high, low = split(jnp.concatenate(values, axis=1))
    value_ref[0] = high
    value_ref[1] = low

    pair_rows(
        recv_ref, (1 - upper) * local, gains_ref[0:1, S:], w_swiglu_ref, w_down_ref, pair_scr
    )
    pair_sums, summed, level = partial_attention(
        base, real, high, low, wb_ref, pair_scr, attn_scr, sums_scr
    )
    for h in range(HEADS):
        send_ref[h] = pair_sums[h].astype(BF16)
    turned = origin(partner_ref)
    send_ref[HEADS] = summed[:, :128].astype(BF16)
    send_ref[HEADS + 1] = summed[:, 128:256].astype(BF16)
    high = level.astype(BF16).astype(F32)
    middle = (level - high).astype(BF16).astype(F32)
    low = level - high - middle
    blank = jnp.zeros((local, 128 - PLANE - HPAD), F32)
    for x, part in enumerate([high, middle, low]):
        plane = summed[:, 256 + 128 * x : 256 + 128 * x + PLANE] - turned[:, 9 + x : 10 + x]
        send_ref[HEADS + 2 + x] = jnp.concatenate([plane, part, blank], axis=1).astype(BF16)


def second_kernel(
    recv_ref,
    value_ref,
    near_ref,
    keys_ref,
    key_pts_ref,
    query_ref,
    query_pts_ref,
    heads_ref,
    rows_ref,
    gains_ref,
    wb_ref,
    w_swiglu_ref,
    w_down_ref,
    own_ref,
    sums_ref,
    wide_ref,
    level_ref,
    pair_scr,
    attn_scr,
    sums_scr,
):
    nsrc, _, local, _ = recv_ref.shape
    me = lax.axis_index("rows")
    pair_rows(
        recv_ref, me // nsrc * local, gains_ref[0:1, S:], w_swiglu_ref, w_down_ref, pair_scr
    )
    base = base_scores(
        query_ref[...], [query_pts_ref[k] for k in range(3 * QP)], keys_ref[0], keys_ref[1],
        [key_pts_ref[k] for k in range(3 * QP)], heads_ref, rows_ref[0:1, :], near_ref[0:1, :],
        me * local,
    )
    pair_sums, summed, level = partial_attention(
        base, near_ref[1:2, :], value_ref[0], value_ref[1], wb_ref, pair_scr, attn_scr, sums_scr
    )
    for h in range(HEADS):
        sums_ref[h] = pair_sums[h]
    turned = origin(own_ref)
    wide_ref[:, :256] = summed[:, :256]
    for x in range(3):
        at = 256 + 128 * x
        wide_ref[:, at : at + 128] = summed[:, at : at + 128] - turned[:, 9 + x : 10 + x]
    level_ref[...] = jnp.concatenate(
        [jnp.zeros((local, PLANE), F32), level, jnp.zeros((local, 128 - PLANE - HPAD), F32)], axis=1
    )


def finish_kernel(
    got_ref,
    sums_ref,
    wide_ref,
    level_ref,
    own_ref,
    gains_ref,
    w_out_ref,
    w_loc_ref,
    out_ref,
):
    local = own_ref.shape[0]
    planes = [got_ref[HEADS + 2 + x].astype(F32) for x in range(3)]
    got = 1.0 / (1.0 + jnp.exp(level_ref[...] - (planes[0] + planes[1] + planes[2])))
    lanes = iota((local, 128), 1)
    low_share = jnp.zeros((local, 128), F32)
    high_share = jnp.zeros((local, 128), F32)
    plane_share = jnp.zeros((local, 128), F32)
    pair_total = []
    for h in range(HEADS):
        share = jnp.broadcast_to(got[:, PLANE + h : PLANE + h + 1], (local, 128))
        low_share = jnp.where(lanes // CH == h, share, low_share)
        high_share = jnp.where(lanes // CH + 8 == h, share, high_share)
        plane_share = jnp.where(lanes // VP == h, share, plane_share)
        mine = sums_ref[h]
        pair_total.append(mine + share * (got_ref[h].astype(F32) - mine))

    def joined(at, share, theirs):
        mine = wide_ref[:, at : at + 128]
        return mine + share * (theirs - mine)

    features = [
        joined(0, low_share, got_ref[HEADS].astype(F32)),
        joined(128, high_share, got_ref[HEADS + 1].astype(F32)),
    ]
    shifted = [joined(256 + 128 * x, plane_share, planes[x]) for x in range(3)]

    turned = origin(own_ref)
    local_out = [
        turned[:, y : y + 1] * shifted[0]
        + turned[:, 3 + y : 4 + y] * shifted[1]
        + turned[:, 6 + y : 7 + y] * shifted[2]
        for y in range(3)
    ]
    lengths = jnp.sqrt(
        local_out[0] * local_out[0] + local_out[1] * local_out[1] + local_out[2] * local_out[2] + 1.0
    )
    update = jnp.dot(
        jnp.concatenate(features, axis=1)[:, :FEAT].astype(BF16),
        w_out_ref[:FEAT, :],
        preferred_element_type=F32,
    )
    for y in range(3):
        update += jnp.dot(
            local_out[y][:, :PLANE].astype(BF16), w_loc_ref[y], preferred_element_type=F32
        )
    at = FEAT + 3 * PLANE
    update += jnp.dot(
        lengths[:, :PLANE].astype(BF16), w_out_ref[at : at + PLANE, :], preferred_element_type=F32
    )
    at += PLANE
    pair_total = jnp.concatenate(pair_total, axis=1).astype(BF16)
    update += jnp.dot(pair_total, w_out_ref[at:, :], preferred_element_type=F32)
    own_single = own_ref[:, :S].astype(F32)
    out_ref[...] = layer_norm(own_single + update, gains_ref[0:1, :S]).astype(BF16)


def in_hbm(arrays):
    return [pltpu.with_memory_space_constraint(array, pltpu.HBM) for array in arrays]


def whole(memory=pltpu.VMEM):
    return pl.BlockSpec(memory_space=memory)


def params(mib):
    return pltpu.CompilerParams(vmem_limit_bytes=mib * MIB)


def on_device(
    single_rep,
    pair_grid,
    frames,
    chain_ids,
    pad_mask,
    ln_pair_gain,
    w_swiglu,
    w_pair_down,
    w_bias,
    w_qkv,
    w_points,
    gamma_raw,
    chain_bias,
    w_out,
    ln_single_gain,
):
    n, local, _ = pair_grid.shape
    size = n // local
    nsrc = size // 2
    near = n // 2
    tiles = max(1, near // 128)
    large = 4 * (n // 128)
    halves = [list(range(nsrc)), list(range(nsrc, size))]
    across = [(i, i ^ nsrc) for i in range(size)]

    packed, own = pl.pallas_call(
        pack_kernel,
        out_shape=[
            jax.ShapeDtypeStruct((nsrc, 2 * local + SMALL, local, C), BF16),
            jax.ShapeDtypeStruct((local, S + 128), BF16),
        ],
        in_specs=[whole(pltpu.HBM)] * 3,
        out_specs=[whole(pltpu.HBM), whole()],
        scratch_shapes=[
            pltpu.VMEM((nsrc, 2 * local, local, C), BF16),
            pltpu.VMEM((nsrc, SMALL, local, C), BF16),
            pltpu.VMEM((local, 12), F32),
            pltpu.SemaphoreType.DMA((10,)),
            pltpu.SemaphoreType.DMA((5,)),
        ],
        compiler_params=params(4 + large),
        name="pack",
    )(*in_hbm([pair_grid.reshape(2, nsrc, local, local, C), single_rep, frames.T]))
    received = lax.all_to_all(
        packed, "rows", 0, 0, tiled=True, axis_index_groups=halves
    )
    partner = lax.ppermute(own, "rows", across)

    sources = [
        pair_grid,
        w_swiglu,
        w_pair_down,
        ln_pair_gain,
        gamma_raw,
        chain_bias,
        chain_ids,
        pad_mask,
        ln_single_gain,
        w_bias.T,
        w_out,
        w_qkv.T,
        w_points.T,
    ]
    held = [pltpu.VMEM(x.shape, x.dtype) for x in sources[:10]]
    held.append(pltpu.VMEM((3 * PLANE, S), BF16))
    pair_out, heads, rows, gains, wb, w_loc, wq, wp = pl.pallas_call(
        own_kernel,
        out_shape=[
            jax.ShapeDtypeStruct(pair_grid.shape, BF16),
            jax.ShapeDtypeStruct((3, HPAD, 128), F32),
            jax.ShapeDtypeStruct((2, n), jnp.int32),
            jax.ShapeDtypeStruct((1, S + C), F32),
            jax.ShapeDtypeStruct((HPAD, C), BF16),
            jax.ShapeDtypeStruct((3, PLANE, S), BF16),
            jax.ShapeDtypeStruct(sources[11].shape, BF16),
            jax.ShapeDtypeStruct(sources[12].shape, BF16),
        ],
        in_specs=[whole(pltpu.HBM)] * len(sources),
        out_specs=[whole()] * 8,
        scratch_shapes=held
        + [
            pltpu.VMEM((S // 128, 3 * PLANE, 128), F32),
            pltpu.SemaphoreType.DMA((len(sources),)),
        ],
        compiler_params=params(18 + large),
        name="own_transition",
    )(*in_hbm(sources))

    scratch = [
        pltpu.VMEM((local, near, C), BF16),
        pltpu.VMEM((2 * local * HPAD, near), BF16),
        pltpu.VMEM((local * HPAD, C), F32),
    ]
    send, *held = pl.pallas_call(
        first_kernel,
        out_shape=[
            jax.ShapeDtypeStruct((PARTS, local, 128), BF16),
            jax.ShapeDtypeStruct((2, near, WIDE), BF16),
            jax.ShapeDtypeStruct((2, near), jnp.int32),
            jax.ShapeDtypeStruct((2, FEAT, near), BF16),
            jax.ShapeDtypeStruct((3 * QP, HEADS, near), F32),
            jax.ShapeDtypeStruct((local, FEAT), F32),
            jax.ShapeDtypeStruct((3 * QP, HEADS, local), F32),
        ],
        in_specs=[whole()] * 11,
        out_specs=[whole()] * 7,
        scratch_shapes=[
            pltpu.VMEM((tiles, QPTS + 3 * PLANE, near // tiles), F32),
            pltpu.VMEM((QPTS + 4 * 3 * QP, 2 * local), F32),
        ]
        + scratch,
        compiler_params=params(16 + large),
        name="first_half",
    )(received, own, partner, heads, rows, gains, wq, wp, wb, w_swiglu, w_pair_down)
    got = lax.ppermute(send, "rows", across)

    sums, wide, level = pl.pallas_call(
        second_kernel,
        out_shape=[
            jax.ShapeDtypeStruct((HEADS, local, 128), F32),
            jax.ShapeDtypeStruct((local, WIDE), F32),
            jax.ShapeDtypeStruct((local, 128), F32),
        ],
        in_specs=[whole()] * 14,
        out_specs=[whole()] * 3,
        scratch_shapes=scratch,
        compiler_params=params(12 + large),
        name="second_half",
    )(received, *held, heads, rows, gains, wb, w_swiglu, w_pair_down, own)

    single_out = pl.pallas_call(
        finish_kernel,
        out_shape=jax.ShapeDtypeStruct((local, S), BF16),
        in_specs=[whole()] * 8,
        out_specs=whole(),
        compiler_params=params(12),
        name="finish",
    )(got, sums, wide, level, own, gains, w_out, w_loc)
    return (single_out, pair_out)


def solution(mesh):
    placed = (
        P(("groups", "rows"), None),
        P("groups", "rows", None),
        P(None, ("groups", "rows")),
        P("groups"),
        P("groups"),
    ) + (P(),) * 10
    return jax.shard_map(
        on_device,
        mesh=mesh,
        in_specs=placed,
        out_specs=(P(("groups", "rows"), None), P("groups", "rows", None)),
        check_vma=False,
    )
```

```python
import math

import jax
import jax.numpy as jnp
from jax import lax
from jax.experimental import pallas as pl
from jax.experimental.pallas import tpu as pltpu
from jax.sharding import PartitionSpec as P

C = 128
S = 384
H = 512
HEADS = 12
CH = 16
QP = 4
VP = 8
HPAD = 16
FEAT = HEADS * CH
QPTS = HEADS * QP * 3
PLANE = HEADS * VP
WIDE = 256 + 3 * 128
SMALL = S // 128 + 1
PARTS = HEADS + WIDE // 128
F32 = jnp.float32
BF16 = jnp.bfloat16
NT = (((1,), (1,)), ((), ()))
MIB = 1024 * 1024
WEIGHT_L = math.sqrt(1.0 / 3.0)
WEIGHT_C = math.sqrt(2.0 / (9.0 * QP))


def iota(shape, dim):
    return lax.broadcasted_iota(jnp.int32, shape, dim)


def nt_dot(a, b):
    return lax.dot_general(a, b, NT, preferred_element_type=F32)


def layer_norm(values, gain):
    centre = jnp.mean(values, axis=-1, keepdims=True)
    centred = values - centre
    spread = jnp.mean(centred * centred, axis=-1, keepdims=True)
    return centred * lax.rsqrt(spread + 1e-05) * gain


def transition(values, gain, w_swiglu_ref, w_down_ref):
    normed = layer_norm(values, gain).astype(BF16)
    both = jnp.dot(normed, w_swiglu_ref[...], preferred_element_type=F32)
    gate = 0.5 * both[:, :H]
    hidden = (gate * (1.0 + jnp.tanh(gate)) * both[:, H:]).astype(BF16)
    update = jnp.dot(hidden, w_down_ref[...], preferred_element_type=F32)
    return (values + update).astype(BF16)


def split(values):
    high = values.astype(BF16)
    return high, (values - high.astype(F32)).astype(BF16)


def pack_kernel(
    pair_hbm, single_hbm, frames_hbm, out_hbm, own_ref, pair_ref, small_ref, frames_ref, in_sems, out_sems
):
    nsrc = pair_ref.shape[0]
    local = own_ref.shape[0]
    step = max(1, nsrc // 4)
    upper = lax.axis_index("rows") // nsrc
    starts = range(0, nsrc, step)
    arrivals = []
    for at in starts:
        mine = [(pair_hbm.at[upper, pl.ds(at, step)], pair_ref.at[pl.ds(at, step), pl.ds(0, local)])]
        theirs = [
            (pair_hbm.at[1 - upper, dest ^ 1], pair_ref.at[dest, pl.ds(local, local)])
            for dest in range(at, at + step)
        ]
        for source, target in mine + theirs:
            arrivals.append(pltpu.make_async_copy(source, target, in_sems.at[len(arrivals)]))
    rows_copies = [
        pltpu.make_async_copy(single_hbm, own_ref.at[:, :S], in_sems.at[len(arrivals)]),
        pltpu.make_async_copy(frames_hbm, frames_ref, in_sems.at[len(arrivals) + 1]),
    ]
    for copy in rows_copies + arrivals:
        copy.start()
    for copy in rows_copies:
        copy.wait()
    rows = frames_ref[...]
    blank = jnp.zeros((local, 128 - 36), F32)
    turned = jnp.concatenate([rows, rows, rows, blank], axis=1)
    high = turned.astype(BF16).astype(F32)
    middle = (turned - high).astype(BF16).astype(F32)
    low = turned - high - middle
    lane = iota(turned.shape, 1)
    own_ref[:, S:] = jnp.where(lane < 12, high, jnp.where(lane < 24, middle, low)).astype(BF16)
    for dest in range(nsrc):
        for piece in range(SMALL):
            small_ref[dest, piece] = own_ref[:, piece * 128 : piece * 128 + 128]
    departures = [
        pltpu.make_async_copy(small_ref, out_hbm.at[:, pl.ds(2 * local, SMALL)], out_sems.at[0])
    ]
    departures[0].start()
    for k, at in enumerate(starts):
        for copy in arrivals[k * (step + 1) : (k + 1) * (step + 1)]:
            copy.wait()
        departures.append(
            pltpu.make_async_copy(
                pair_ref.at[pl.ds(at, step)],
                out_hbm.at[pl.ds(at, step), pl.ds(0, 2 * local)],
                out_sems.at[1 + k],
            )
        )
        departures[-1].start()
    for copy in departures:
        copy.wait()


def strided(ref, start, count, stride):
    return jnp.concatenate(
        [ref[t, pl.ds(start, count, stride=stride), :] for t in range(ref.shape[0])], axis=1
    )


def own_kernel(*refs):
    sources, refs = refs[:13], refs[13:]
    out_ref, heads_ref, rows_ref, gains_ref, wb_out_ref, w_loc_ref, wq_ref, wp_ref = refs[:8]
    held, refs = refs[8:19], refs[19:]
    loc_scr, sems = refs
    pair_hbm, *_ = sources
    n, local, _ = pair_hbm.shape
    targets = list(held) + [wq_ref, wp_ref]
    copies = []
    for k, (source, target) in enumerate(zip(sources, targets)):
        if k == 10:
            source = source.at[pl.ds(FEAT, 3 * PLANE)]
        copies.append(pltpu.make_async_copy(source, target, sems.at[k]))
        copies[k].start()
    pair_ref, w_swiglu_ref, w_down_ref, gain_ref, gamma_ref, cb_ref = held[:6]
    chain_ref, pad_ref, gain2_ref, wb_ref, loc_ref = held[6:]
    for copy in copies[:4]:
        copy.wait()
    gain = gain_ref[...].reshape(1, C)
    block = math.gcd(n, 128)

    def step(at):
        values = pair_ref[pl.ds(at, block)].astype(F32).reshape(-1, C)
        done = transition(values, gain, w_swiglu_ref, w_down_ref)
        out_ref[pl.ds(at, block)] = done.astype(F32).reshape(-1, local, C).astype(BF16)

    if n == block:
        step(0)
    else:
        pl.loop(0, n, step=block)(step)
    for copy in copies[4:]:
        copy.wait()

    diagonal = iota((HPAD, HEADS), 0) == iota((HPAD, HEADS), 1)

    def column(row):
        turned = jnp.sum(jnp.where(diagonal, row, 0.0), axis=1, keepdims=True)
        return jnp.broadcast_to(turned, (HPAD, 128))

    gamma = jax.nn.softplus(gamma_ref[...].reshape(1, HEADS))
    heads_ref[0] = column(gamma * (-0.5 * WEIGHT_C))
    heads_ref[1] = column(cb_ref[0:1, :])
    heads_ref[2] = column(cb_ref[1:2, :])
    rows_ref[0:1, :] = chain_ref[...].reshape(1, n)
    rows_ref[1:2, :] = pad_ref[...].reshape(1, n)
    gains_ref[0:1, :S] = gain2_ref[...].reshape(1, S)
    gains_ref[0:1, S:] = gain
    wb_out_ref[...] = jnp.concatenate(
        [wb_ref[...], jnp.zeros((HPAD - HEADS, C), BF16)], axis=0
    )
    local_rows = loc_ref[...].astype(F32)
    for t in range(S // 128):
        loc_scr[t] = local_rows[:, t * 128 : (t + 1) * 128]
    for y in range(3):
        w_loc_ref[y] = strided(loc_scr, y, PLANE, 3).astype(BF16)


def place(frame, triple):
    return [
        frame[3 * x : 3 * x + 1, :] * triple[0]
        + frame[3 * x + 1 : 3 * x + 2, :] * triple[1]
        + frame[3 * x + 2 : 3 * x + 3, :] * triple[2]
        + frame[9 + x : 10 + x, :]
        for x in range(3)
    ]


def head_of_lane(rows):
    lanes = iota((rows, WIDE), 1)
    return jnp.where(lanes < 256, lanes // CH, (lanes % 128) // VP)


def base_scores(
    queries, query_pts, high_keys, low_keys, key_pts, heads_ref, chain_all, chain_row, first
):
    local = queries.shape[0]
    n = high_keys.shape[1]
    rows = local * HPAD
    owned = (iota((HPAD, FEAT), 1) // CH == iota((HPAD, FEAT), 0))[None]
    spread = jnp.broadcast_to(queries.reshape(local, 1, FEAT), (local, HPAD, FEAT))
    high, low = split(jnp.where(owned, spread, 0.0).reshape(rows, FEAT))
    both = jnp.dot(jnp.concatenate([high, low], axis=0), high_keys, preferred_element_type=F32)
    dots = both[:rows] + both[rows:] + jnp.dot(high, low_keys, preferred_element_type=F32)
    distances = []
    blank = jnp.zeros((HPAD - HEADS, n), F32)
    for i in range(local):
        distance = 0.0
        for q, k in zip(query_pts, key_pts):
            apart = q[:, i : i + 1] - k
            distance = distance + apart * apart
        distances += [distance, blank]
    distance = jnp.concatenate(distances, axis=0)

    def per_row(index):
        wide = jnp.concatenate([heads_ref[index]] * max(1, n // 128), axis=1)[:, :n]
        return jnp.concatenate([wide] * local, axis=0)

    width = chain_all.shape[1]
    lanes, order = iota((local, width), 1), iota((local, width), 0)
    mine = jnp.sum(jnp.where(lanes == first + order, chain_all, 0), axis=1, keepdims=True)
    mine = jnp.broadcast_to(mine.reshape(local, 1, 1), (local, HPAD, n)).reshape(rows, n)
    chain = jnp.where(chain_row == mine, per_row(1), per_row(2))
    return WEIGHT_L * (dots * (1.0 / math.sqrt(CH)) + chain + per_row(0) * distance)


def pair_rows(recv_ref, at, gain, w_swiglu_ref, w_down_ref, pair_scr):
    nsrc, _, local, _ = recv_ref.shape
    n = nsrc * local
    group = max(1, min(local, 512 // n))
    for start in range(0, local, group):
        block = recv_ref[:, pl.ds(at + start, group)].astype(F32)
        block = jnp.concatenate([block[:, k].reshape(n, C) for k in range(group)], axis=0)
        done = transition(block, gain, w_swiglu_ref, w_down_ref)
        for k in range(group):
            pair_scr[start + k] = done[k * n : (k + 1) * n]


def partial_attention(base, real, high_value, low_value, wb_ref, pair_scr, attn_scr, sums_scr):
    local, n, _ = pair_scr.shape
    rows = local * HPAD
    bias = jnp.concatenate([nt_dot(wb_ref[...], pair_scr[i]) for i in range(local)], axis=0)
    scores = base + WEIGHT_L * bias
    scores = jnp.where(jnp.broadcast_to(real, (rows, n)) > 0, scores, -1000000000.0)
    peak = jnp.max(scores, axis=-1, keepdims=True)
    expo = jnp.exp(scores - peak)
    high, low = split(expo)
    total = jnp.sum(expo, axis=-1, keepdims=True)
    share = 1.0 / total
    attn_scr[:rows] = high
    attn_scr[rows:] = low
    for i in range(local):
        at = i * HPAD
        sums_scr[at : at + HPAD, :] = share[at : at + HPAD] * jnp.dot(
            high[at : at + HPAD], pair_scr[i], preferred_element_type=F32
        )
    both = jnp.dot(attn_scr[...], high_value, preferred_element_type=F32)
    every = both[:rows] + both[rows:]
    every += jnp.dot(attn_scr[:rows], low_value, preferred_element_type=F32)
    every *= share
    owned = head_of_lane(HPAD) == iota((HPAD, WIDE), 0)
    every = every.reshape(local, HPAD, WIDE)
    summed = jnp.sum(jnp.where(owned[None], every, 0.0), axis=1)
    diagonal = (iota((HPAD, HPAD), 0) == iota((HPAD, HPAD), 1))[None]

    level = jnp.broadcast_to((peak + jnp.log(total)).reshape(local, HPAD, 1), (local, HPAD, HPAD))
    level = jnp.sum(jnp.where(diagonal, level, 0.0), axis=1)
    pair_sums = [sums_scr[pl.ds(h, local, stride=HPAD), :] for h in range(HEADS)]
    return pair_sums, summed, level


def origin(row_ref):
    parts = row_ref[:, S:].astype(F32)
    return parts[:, 0:12] + parts[:, 12:24] + parts[:, 24:36]


def first_kernel(
    recv_ref,
    own_ref,
    partner_ref,
    heads_ref,
    rows_ref,
    gains_ref,
    wq_ref,
    wp_ref,
    wb_ref,
    w_swiglu_ref,
    w_down_ref,
    send_ref,
    value_ref,
    near_ref,
    keys_ref,
    key_pts_ref,
    query_ref,
    query_pts_ref,
    pts_scr,
    qp_scr,
    pair_scr,
    attn_scr,
    sums_scr,
):
    nsrc, _, local, _ = recv_ref.shape
    tiles, _, lane = pts_scr.shape
    n = nsrc * local
    me = lax.axis_index("rows")
    upper = me // nsrc

    def piece(index):
        return recv_ref[:, index].astype(F32).reshape(n, 128).astype(BF16)

    all_single = jnp.concatenate([piece(2 * local + k) for k in range(SMALL - 1)], axis=1)
    queries = jnp.concatenate(
        [partner_ref[...].astype(F32), own_ref[...].astype(F32)], axis=0
    ).astype(BF16)
    rows16, lanes16 = iota((16, 128), 0), iota((16, 128), 1)
    pick = ((lanes16 % 12 == rows16) & (lanes16 < 36)).astype(BF16)
    frames = nt_dot(pick, piece(2 * local + SMALL - 1))
    query_frames = nt_dot(pick, queries[:, S:])

    high_keys, low_keys = split(nt_dot(wq_ref[FEAT : 2 * FEAT, :], all_single))
    keys_ref[0] = high_keys
    keys_ref[1] = low_keys
    points = nt_dot(wp_ref[QPTS:, :], all_single)
    for t in range(tiles):
        pts_scr[t] = points[:, t * lane : (t + 1) * lane]
    features = nt_dot(queries[:, :S], wq_ref[:FEAT, :])
    qp_scr[:QPTS, :] = nt_dot(wp_ref[:QPTS, :], queries[:, :S])

    key_pts, query_pts = [], []
    for p in range(QP):
        key_pts += place(frames, [strided(pts_scr, 3 * p + y, HEADS, 3 * QP) for y in range(3)])
        query_pts += place(
            query_frames, [qp_scr[pl.ds(3 * p + y, HEADS, stride=3 * QP), :] for y in range(3)]
        )
    for k in range(3 * QP):
        key_pts_ref[k] = key_pts[k]
        query_pts_ref[k] = query_pts[k][:, local:]
    query_ref[...] = features[local:]

    chain_all = rows_ref[0:1, :]
    chain_row = jnp.where(upper == 0, chain_all[:, :n], chain_all[:, n:])
    real = jnp.where(upper == 0, rows_ref[1:2, :n], rows_ref[1:2, n:])
    near_ref[0:1, :] = chain_row
    near_ref[1:2, :] = real
    base = base_scores(
        features[:local], query_pts, high_keys, low_keys, key_pts, heads_ref, chain_all, chain_row,
        jnp.bitwise_xor(me, nsrc + 1) * local,
    )

    planes = place(frames, [strided(pts_scr, QPTS + y, PLANE, 3) for y in range(3)])
    gap = jnp.zeros((n, 128 - PLANE), F32)
    values = [nt_dot(all_single, wq_ref[2 * FEAT :, :]), jnp.zeros((n, 256 - FEAT), F32)]
    for plane in planes:
        values += [plane.T, gap]
    high, low = split(jnp.concatenate(values, axis=1))
    value_ref[0] = high
    value_ref[1] = low

    pair_rows(
        recv_ref, local, gains_ref[0:1, S:], w_swiglu_ref, w_down_ref, pair_scr
    )
    pair_sums, summed, level = partial_attention(
        base, real, high, low, wb_ref, pair_scr, attn_scr, sums_scr
    )
    for h in range(HEADS):
        send_ref[h] = pair_sums[h].astype(BF16)
    turned = origin(partner_ref)
    send_ref[HEADS] = summed[:, :128].astype(BF16)
    send_ref[HEADS + 1] = summed[:, 128:256].astype(BF16)
    high = level.astype(BF16).astype(F32)
    middle = (level - high).astype(BF16).astype(F32)
    low = level - high - middle
    blank = jnp.zeros((local, 128 - PLANE - HPAD), F32)
    for x, part in enumerate([high, middle, low]):
        plane = summed[:, 256 + 128 * x : 256 + 128 * x + PLANE] - turned[:, 9 + x : 10 + x]
        send_ref[HEADS + 2 + x] = jnp.concatenate([plane, part, blank], axis=1).astype(BF16)


def second_kernel(
    recv_ref,
    value_ref,
    near_ref,
    keys_ref,
    key_pts_ref,
    query_ref,
    query_pts_ref,
    heads_ref,
    rows_ref,
    gains_ref,
    wb_ref,
    w_swiglu_ref,
    w_down_ref,
    own_ref,
    sums_ref,
    wide_ref,
    level_ref,
    pair_scr,
    attn_scr,
    sums_scr,
):
    nsrc, _, local, _ = recv_ref.shape
    me = lax.axis_index("rows")
    pair_rows(
        recv_ref, 0, gains_ref[0:1, S:], w_swiglu_ref, w_down_ref, pair_scr
    )
    base = base_scores(
        query_ref[...], [query_pts_ref[k] for k in range(3 * QP)], keys_ref[0], keys_ref[1],
        [key_pts_ref[k] for k in range(3 * QP)], heads_ref, rows_ref[0:1, :], near_ref[0:1, :],
        me * local,
    )
    pair_sums, summed, level = partial_attention(
        base, near_ref[1:2, :], value_ref[0], value_ref[1], wb_ref, pair_scr, attn_scr, sums_scr
    )
    for h in range(HEADS):
        sums_ref[h] = pair_sums[h]
    turned = origin(own_ref)
    wide_ref[:, :256] = summed[:, :256]
    for x in range(3):
        at = 256 + 128 * x
        wide_ref[:, at : at + 128] = summed[:, at : at + 128] - turned[:, 9 + x : 10 + x]
    level_ref[...] = jnp.concatenate(
        [jnp.zeros((local, PLANE), F32), level, jnp.zeros((local, 128 - PLANE - HPAD), F32)], axis=1
    )


def finish_kernel(
    got_ref,
    sums_ref,
    wide_ref,
    level_ref,
    own_ref,
    gains_ref,
    w_out_ref,
    w_loc_ref,
    out_ref,
):
    local = own_ref.shape[0]
    planes = [got_ref[HEADS + 2 + x].astype(F32) for x in range(3)]
    got = 1.0 / (1.0 + jnp.exp(level_ref[...] - (planes[0] + planes[1] + planes[2])))
    lanes = iota((local, 128), 1)
    low_share = jnp.zeros((local, 128), F32)
    high_share = jnp.zeros((local, 128), F32)
    plane_share = jnp.zeros((local, 128), F32)
    pair_total = []
    for h in range(HEADS):
        share = jnp.broadcast_to(got[:, PLANE + h : PLANE + h + 1], (local, 128))
        low_share = jnp.where(lanes // CH == h, share, low_share)
        high_share = jnp.where(lanes // CH + 8 == h, share, high_share)
        plane_share = jnp.where(lanes // VP == h, share, plane_share)
        mine = sums_ref[h]
        pair_total.append(mine + share * (got_ref[h].astype(F32) - mine))

    def joined(at, share, theirs):
        mine = wide_ref[:, at : at + 128]
        return mine + share * (theirs - mine)

    features = [
        joined(0, low_share, got_ref[HEADS].astype(F32)),
        joined(128, high_share, got_ref[HEADS + 1].astype(F32)),
    ]
    shifted = [joined(256 + 128 * x, plane_share, planes[x]) for x in range(3)]

    turned = origin(own_ref)
    local_out = [
        turned[:, y : y + 1] * shifted[0]
        + turned[:, 3 + y : 4 + y] * shifted[1]
        + turned[:, 6 + y : 7 + y] * shifted[2]
        for y in range(3)
    ]
    lengths = jnp.sqrt(
        local_out[0] * local_out[0] + local_out[1] * local_out[1] + local_out[2] * local_out[2] + 1.0
    )
    update = jnp.dot(
        jnp.concatenate(features, axis=1)[:, :FEAT].astype(BF16),
        w_out_ref[:FEAT, :],
        preferred_element_type=F32,
    )
    for y in range(3):
        update += jnp.dot(
            local_out[y][:, :PLANE].astype(BF16), w_loc_ref[y], preferred_element_type=F32
        )
    at = FEAT + 3 * PLANE
    update += jnp.dot(
        lengths[:, :PLANE].astype(BF16), w_out_ref[at : at + PLANE, :], preferred_element_type=F32
    )
    at += PLANE
    pair_total = jnp.concatenate(pair_total, axis=1).astype(BF16)
    update += jnp.dot(pair_total, w_out_ref[at:, :], preferred_element_type=F32)
    own_single = own_ref[:, :S].astype(F32)
    out_ref[...] = layer_norm(own_single + update, gains_ref[0:1, :S]).astype(BF16)


def in_hbm(arrays):
    return [pltpu.with_memory_space_constraint(array, pltpu.HBM) for array in arrays]


def whole(memory=pltpu.VMEM):
    return pl.BlockSpec(memory_space=memory)


def params(mib):
    return pltpu.CompilerParams(vmem_limit_bytes=mib * MIB)


def on_device(
    single_rep,
    pair_grid,
    frames,
    chain_ids,
    pad_mask,
    ln_pair_gain,
    w_swiglu,
    w_pair_down,
    w_bias,
    w_qkv,
    w_points,
    gamma_raw,
    chain_bias,
    w_out,
    ln_single_gain,
):
    n, local, _ = pair_grid.shape
    size = n // local
    nsrc = size // 2
    near = n // 2
    tiles = max(1, near // 128)
    large = 4 * (n // 128)
    halves = [list(range(nsrc)), list(range(nsrc, size))]
    across = [(i, i ^ (nsrc + 1)) for i in range(size)]

    packed, own = pl.pallas_call(
        pack_kernel,
        out_shape=[
            jax.ShapeDtypeStruct((nsrc, 2 * local + SMALL, local, C), BF16),
            jax.ShapeDtypeStruct((local, S + 128), BF16),
        ],
        in_specs=[whole(pltpu.HBM)] * 3,
        out_specs=[whole(pltpu.HBM), whole()],
        scratch_shapes=[
            pltpu.VMEM((nsrc, 2 * local, local, C), BF16),
            pltpu.VMEM((nsrc, SMALL, local, C), BF16),
            pltpu.VMEM((local, 12), F32),
            pltpu.SemaphoreType.DMA((nsrc + 6,)),
            pltpu.SemaphoreType.DMA((5,)),
        ],
        compiler_params=params(4 + large),
        name="pack",
    )(*in_hbm([pair_grid.reshape(2, nsrc, local, local, C), single_rep, frames.T]))
    received = lax.all_to_all(
        packed, "rows", 0, 0, tiled=True, axis_index_groups=halves
    )
    partner = lax.ppermute(own, "rows", across)

    sources = [
        pair_grid,
        w_swiglu,
        w_pair_down,
        ln_pair_gain,
        gamma_raw,
        chain_bias,
        chain_ids,
        pad_mask,
        ln_single_gain,
        w_bias.T,
        w_out,
        w_qkv.T,
        w_points.T,
    ]
    held = [pltpu.VMEM(x.shape, x.dtype) for x in sources[:10]]
    held.append(pltpu.VMEM((3 * PLANE, S), BF16))
    pair_out, heads, rows, gains, wb, w_loc, wq, wp = pl.pallas_call(
        own_kernel,
        out_shape=[
            jax.ShapeDtypeStruct(pair_grid.shape, BF16),
            jax.ShapeDtypeStruct((3, HPAD, 128), F32),
            jax.ShapeDtypeStruct((2, n), jnp.int32),
            jax.ShapeDtypeStruct((1, S + C), F32),
            jax.ShapeDtypeStruct((HPAD, C), BF16),
            jax.ShapeDtypeStruct((3, PLANE, S), BF16),
            jax.ShapeDtypeStruct(sources[11].shape, BF16),
            jax.ShapeDtypeStruct(sources[12].shape, BF16),
        ],
        in_specs=[whole(pltpu.HBM)] * len(sources),
        out_specs=[whole()] * 8,
        scratch_shapes=held
        + [
            pltpu.VMEM((S // 128, 3 * PLANE, 128), F32),
            pltpu.SemaphoreType.DMA((len(sources),)),
        ],
        compiler_params=params(18 + large),
        name="own_transition",
    )(*in_hbm(sources))

    scratch = [
        pltpu.VMEM((local, near, C), BF16),
        pltpu.VMEM((2 * local * HPAD, near), BF16),
        pltpu.VMEM((local * HPAD, C), F32),
    ]
    send, *held = pl.pallas_call(
        first_kernel,
        out_shape=[
            jax.ShapeDtypeStruct((PARTS, local, 128), BF16),
            jax.ShapeDtypeStruct((2, near, WIDE), BF16),
            jax.ShapeDtypeStruct((2, near), jnp.int32),
            jax.ShapeDtypeStruct((2, FEAT, near), BF16),
            jax.ShapeDtypeStruct((3 * QP, HEADS, near), F32),
            jax.ShapeDtypeStruct((local, FEAT), F32),
            jax.ShapeDtypeStruct((3 * QP, HEADS, local), F32),
        ],
        in_specs=[whole()] * 11,
        out_specs=[whole()] * 7,
        scratch_shapes=[
            pltpu.VMEM((tiles, QPTS + 3 * PLANE, near // tiles), F32),
            pltpu.VMEM((QPTS + 4 * 3 * QP, 2 * local), F32),
        ]
        + scratch,
        compiler_params=params(16 + large),
        name="first_half",
    )(received, own, partner, heads, rows, gains, wq, wp, wb, w_swiglu, w_pair_down)
    got = lax.ppermute(send, "rows", across)

    sums, wide, level = pl.pallas_call(
        second_kernel,
        out_shape=[
            jax.ShapeDtypeStruct((HEADS, local, 128), F32),
            jax.ShapeDtypeStruct((local, WIDE), F32),
            jax.ShapeDtypeStruct((local, 128), F32),
        ],
        in_specs=[whole()] * 14,
        out_specs=[whole()] * 3,
        scratch_shapes=scratch,
        compiler_params=params(12 + large),
        name="second_half",
    )(received, *held, heads, rows, gains, wb, w_swiglu, w_pair_down, own)

    single_out = pl.pallas_call(
        finish_kernel,
        out_shape=jax.ShapeDtypeStruct((local, S), BF16),
        in_specs=[whole()] * 8,
        out_specs=whole(),
        compiler_params=params(12),
        name="finish",
    )(got, sums, wide, level, own, gains, w_out, w_loc)
    return (single_out, pair_out)


def solution(mesh):
    placed = (
        P(("groups", "rows"), None),
        P("groups", "rows", None),
        P(None, ("groups", "rows")),
        P("groups"),
        P("groups"),
    ) + (P(),) * 10
    return jax.shard_map(
        on_device,
        mesh=mesh,
        in_specs=placed,
        out_specs=(P(("groups", "rows"), None), P("groups", "rows", None)),
        check_vma=False,
    )
```

```python
import math

import jax
import jax.numpy as jnp
from jax import lax
from jax.experimental import pallas as pl
from jax.experimental.pallas import tpu as pltpu
from jax.sharding import PartitionSpec as P

C = 128
S = 384
H = 512
HEADS = 12
CH = 16
QP = 4
VP = 8
HPAD = 16
FEAT = HEADS * CH
QPTS = HEADS * QP * 3
PLANE = HEADS * VP
WIDE = 256 + 3 * 128
SMALL = S // 128 + 1
PARTS = HEADS + WIDE // 128
F32 = jnp.float32
BF16 = jnp.bfloat16
NT = (((1,), (1,)), ((), ()))
MIB = 1024 * 1024
WEIGHT_L = math.sqrt(1.0 / 3.0)
WEIGHT_C = math.sqrt(2.0 / (9.0 * QP))


def iota(shape, dim):
    return lax.broadcasted_iota(jnp.int32, shape, dim)


def nt_dot(a, b):
    return lax.dot_general(a, b, NT, preferred_element_type=F32)


def layer_norm(values, gain):
    centre = jnp.mean(values, axis=-1, keepdims=True)
    centred = values - centre
    spread = jnp.mean(centred * centred, axis=-1, keepdims=True)
    return centred * lax.rsqrt(spread + 1e-05) * gain


def transition(values, gain, w_swiglu_ref, w_down_ref):
    normed = layer_norm(values, gain).astype(BF16)
    both = jnp.dot(normed, w_swiglu_ref[...], preferred_element_type=F32)
    gate = 0.5 * both[:, :H]
    hidden = (gate * (1.0 + jnp.tanh(gate)) * both[:, H:]).astype(BF16)
    update = jnp.dot(hidden, w_down_ref[...], preferred_element_type=F32)
    return (values + update).astype(BF16)


def split(values):
    high = values.astype(BF16)
    return high, (values - high.astype(F32)).astype(BF16)


def pack_kernel(
    pair_hbm, single_hbm, frames_hbm, out_hbm, own_ref, pair_ref, small_ref, frames_ref, in_sems, out_sems
):
    nsrc = pair_ref.shape[0]
    local = own_ref.shape[0]
    step = max(1, nsrc // 4)
    upper = lax.axis_index("rows") // nsrc
    starts = range(0, nsrc, step)
    arrivals = []
    for at in starts:
        mine = [(pair_hbm.at[upper, pl.ds(at, step)], pair_ref.at[pl.ds(at, step), pl.ds(0, local)])]
        theirs = [
            (pair_hbm.at[1 - upper, dest ^ 1], pair_ref.at[dest, pl.ds(local, local)])
            for dest in range(at, at + step)
        ]
        for source, target in mine + theirs:
            arrivals.append(pltpu.make_async_copy(source, target, in_sems.at[len(arrivals)]))
    rows_copies = [
        pltpu.make_async_copy(single_hbm, own_ref.at[:, :S], in_sems.at[len(arrivals)]),
        pltpu.make_async_copy(frames_hbm, frames_ref, in_sems.at[len(arrivals) + 1]),
    ]
    for copy in rows_copies + arrivals:
        copy.start()
    for copy in rows_copies:
        copy.wait()
    rows = frames_ref[...]
    blank = jnp.zeros((local, 128 - 36), F32)
    turned = jnp.concatenate([rows, rows, rows, blank], axis=1)
    high = turned.astype(BF16).astype(F32)
    middle = (turned - high).astype(BF16).astype(F32)
    low = turned - high - middle
    lane = iota(turned.shape, 1)
    own_ref[:, S:] = jnp.where(lane < 12, high, jnp.where(lane < 24, middle, low)).astype(BF16)
    for dest in range(nsrc):
        for piece in range(SMALL):
            small_ref[dest, piece] = own_ref[:, piece * 128 : piece * 128 + 128]
    departures = [
        pltpu.make_async_copy(small_ref, out_hbm.at[:, pl.ds(2 * local, SMALL)], out_sems.at[0])
    ]
    departures[0].start()
    for k, at in enumerate(starts):
        for copy in arrivals[k * (step + 1) : (k + 1) * (step + 1)]:
            copy.wait()
        departures.append(
            pltpu.make_async_copy(
                pair_ref.at[pl.ds(at, step)],
                out_hbm.at[pl.ds(at, step), pl.ds(0, 2 * local)],
                out_sems.at[1 + k],
            )
        )
        departures[-1].start()
    for copy in departures:
        copy.wait()


def strided(ref, start, count, stride):
    return jnp.concatenate(
        [ref[t, pl.ds(start, count, stride=stride), :] for t in range(ref.shape[0])], axis=1
    )


def own_kernel(*refs):
    sources, refs = refs[:13], refs[13:]
    out_ref, heads_ref, rows_ref, gains_ref, wb_out_ref, w_loc_ref, wq_ref, wp_ref = refs[:8]
    held, refs = refs[8:19], refs[19:]
    loc_scr, sems = refs
    pair_hbm, *_ = sources
    n, local, _ = pair_hbm.shape
    targets = list(held) + [wq_ref, wp_ref]
    copies = []
    for k, (source, target) in enumerate(zip(sources, targets)):
        if k == 10:
            source = source.at[pl.ds(FEAT, 3 * PLANE)]
        copies.append(pltpu.make_async_copy(source, target, sems.at[k]))
        copies[k].start()
    pair_ref, w_swiglu_ref, w_down_ref, gain_ref, gamma_ref, cb_ref = held[:6]
    chain_ref, pad_ref, gain2_ref, wb_ref, loc_ref = held[6:]
    for copy in copies[:4]:
        copy.wait()
    gain = gain_ref[...].reshape(1, C)
    block = math.gcd(n, 128)

    def step(at):
        values = pair_ref[pl.ds(at, block)].astype(F32).reshape(-1, C)
        done = transition(values, gain, w_swiglu_ref, w_down_ref)
        out_ref[pl.ds(at, block)] = done.astype(F32).reshape(-1, local, C).astype(BF16)

    if n == block:
        step(0)
    else:
        pl.loop(0, n, step=block)(step)
    for copy in copies[4:]:
        copy.wait()

    diagonal = iota((HPAD, HEADS), 0) == iota((HPAD, HEADS), 1)

    def column(row):
        turned = jnp.sum(jnp.where(diagonal, row, 0.0), axis=1, keepdims=True)
        return jnp.broadcast_to(turned, (HPAD, 128))

    gamma = jax.nn.softplus(gamma_ref[...].reshape(1, HEADS))
    heads_ref[0] = column(gamma * (-0.5 * WEIGHT_C))
    heads_ref[1] = column(cb_ref[0:1, :])
    heads_ref[2] = column(cb_ref[1:2, :])
    rows_ref[0:1, :] = chain_ref[...].reshape(1, n)
    rows_ref[1:2, :] = pad_ref[...].reshape(1, n)
    gains_ref[0:1, :S] = gain2_ref[...].reshape(1, S)
    gains_ref[0:1, S:] = gain
    wb_out_ref[...] = jnp.concatenate(
        [wb_ref[...], jnp.zeros((HPAD - HEADS, C), BF16)], axis=0
    )
    local_rows = loc_ref[...].astype(F32)
    for t in range(S // 128):
        loc_scr[t] = local_rows[:, t * 128 : (t + 1) * 128]
    for y in range(3):
        w_loc_ref[y] = strided(loc_scr, y, PLANE, 3).astype(BF16)


def place(frame, triple):
    return [
        frame[3 * x : 3 * x + 1, :] * triple[0]
        + frame[3 * x + 1 : 3 * x + 2, :] * triple[1]
        + frame[3 * x + 2 : 3 * x + 3, :] * triple[2]
        + frame[9 + x : 10 + x, :]
        for x in range(3)
    ]


def head_of_lane(rows):
    lanes = iota((rows, WIDE), 1)
    return jnp.where(lanes < 256, lanes // CH, (lanes % 128) // VP)


def base_scores(
    queries, query_pts, high_keys, low_keys, key_pts, heads_ref, chain_all, chain_row, first
):
    local = queries.shape[0]
    n = high_keys.shape[1]
    rows = local * HPAD
    owned = (iota((HPAD, FEAT), 1) // CH == iota((HPAD, FEAT), 0))[None]
    spread = jnp.broadcast_to(queries.reshape(local, 1, FEAT), (local, HPAD, FEAT))
    high, low = split(jnp.where(owned, spread, 0.0).reshape(rows, FEAT))
    both = jnp.dot(jnp.concatenate([high, low], axis=0), high_keys, preferred_element_type=F32)
    dots = both[:rows] + both[rows:] + jnp.dot(high, low_keys, preferred_element_type=F32)
    distances = []
    blank = jnp.zeros((HPAD - HEADS, n), F32)
    for i in range(local):
        distance = 0.0
        for q, k in zip(query_pts, key_pts):
            apart = q[:, i : i + 1] - k
            distance = distance + apart * apart
        distances += [distance, blank]
    distance = jnp.concatenate(distances, axis=0)

    def per_row(index):
        wide = jnp.concatenate([heads_ref[index]] * max(1, n // 128), axis=1)[:, :n]
        return jnp.concatenate([wide] * local, axis=0)

    width = chain_all.shape[1]
    lanes, order = iota((local, width), 1), iota((local, width), 0)
    mine = jnp.sum(jnp.where(lanes == first + order, chain_all, 0), axis=1, keepdims=True)
    mine = jnp.broadcast_to(mine.reshape(local, 1, 1), (local, HPAD, n)).reshape(rows, n)
    chain = jnp.where(chain_row == mine, per_row(1), per_row(2))
    return WEIGHT_L * (dots * (1.0 / math.sqrt(CH)) + chain + per_row(0) * distance)


def pair_rows(recv_ref, at, gain, w_swiglu_ref, w_down_ref, pair_scr):
    nsrc, _, local, _ = recv_ref.shape
    n = nsrc * local
    group = max(1, min(local, 512 // n))
    for start in range(0, local, group):
        block = recv_ref[:, pl.ds(at + start, group)].astype(F32)
        block = jnp.concatenate([block[:, k].reshape(n, C) for k in range(group)], axis=0)
        done = transition(block, gain, w_swiglu_ref, w_down_ref)
        for k in range(group):
            pair_scr[start + k] = done[k * n : (k + 1) * n]


def partial_attention(base, real, high_value, low_value, wb_ref, pair_scr, attn_scr, sums_scr):
    local, n, _ = pair_scr.shape
    rows = local * HPAD
    bias = jnp.concatenate([nt_dot(wb_ref[...], pair_scr[i]) for i in range(local)], axis=0)
    scores = base + WEIGHT_L * bias
    scores = jnp.where(jnp.broadcast_to(real, (rows, n)) > 0, scores, -1000000000.0)
    peak = jnp.max(scores, axis=-1, keepdims=True)
    expo = jnp.exp(scores - peak)
    high, low = split(expo)
    total = jnp.sum(expo, axis=-1, keepdims=True)
    share = 1.0 / total
    attn_scr[:rows] = high
    attn_scr[rows:] = low
    for i in range(local):
        at = i * HPAD
        sums_scr[at : at + HPAD, :] = share[at : at + HPAD] * jnp.dot(
            high[at : at + HPAD], pair_scr[i], preferred_element_type=F32
        )
    both = jnp.dot(attn_scr[...], high_value, preferred_element_type=F32)
    every = both[:rows] + both[rows:]
    every += jnp.dot(attn_scr[:rows], low_value, preferred_element_type=F32)
    every *= share
    owned = head_of_lane(HPAD) == iota((HPAD, WIDE), 0)
    every = every.reshape(local, HPAD, WIDE)
    summed = jnp.sum(jnp.where(owned[None], every, 0.0), axis=1)
    diagonal = (iota((HPAD, HPAD), 0) == iota((HPAD, HPAD), 1))[None]

    level = jnp.broadcast_to((peak + jnp.log(total)).reshape(local, HPAD, 1), (local, HPAD, HPAD))
    level = jnp.sum(jnp.where(diagonal, level, 0.0), axis=1)
    pair_sums = [sums_scr[pl.ds(h, local, stride=HPAD), :] for h in range(HEADS)]
    return pair_sums, summed, level


def origin(row_ref):
    parts = row_ref[:, S:].astype(F32)
    return parts[:, 0:12] + parts[:, 12:24] + parts[:, 24:36]


def into_frame(row_ref, summed):
    turned = origin(row_ref)
    shifted = [
        summed[:, 256 + 128 * x : 384 + 128 * x] - turned[:, 9 + x : 10 + x] for x in range(3)
    ]
    return [
        turned[:, y : y + 1] * shifted[0]
        + turned[:, 3 + y : 4 + y] * shifted[1]
        + turned[:, 6 + y : 7 + y] * shifted[2]
        for y in range(3)
    ]


def first_kernel(
    recv_ref,
    own_ref,
    partner_ref,
    heads_ref,
    rows_ref,
    gains_ref,
    wq_ref,
    wp_ref,
    wb_ref,
    w_swiglu_ref,
    w_down_ref,
    send_ref,
    value_ref,
    near_ref,
    keys_ref,
    key_pts_ref,
    query_ref,
    query_pts_ref,
    pts_scr,
    qp_scr,
    pair_scr,
    attn_scr,
    sums_scr,
):
    nsrc, _, local, _ = recv_ref.shape
    tiles, _, lane = pts_scr.shape
    n = nsrc * local
    me = lax.axis_index("rows")
    upper = me // nsrc

    def piece(index):
        return recv_ref[:, index].astype(F32).reshape(n, 128).astype(BF16)

    all_single = jnp.concatenate([piece(2 * local + k) for k in range(SMALL - 1)], axis=1)
    queries = jnp.concatenate(
        [partner_ref[...].astype(F32), own_ref[...].astype(F32)], axis=0
    ).astype(BF16)
    rows16, lanes16 = iota((16, 128), 0), iota((16, 128), 1)
    pick = ((lanes16 % 12 == rows16) & (lanes16 < 36)).astype(BF16)
    frames = nt_dot(pick, piece(2 * local + SMALL - 1))
    query_frames = nt_dot(pick, queries[:, S:])

    high_keys, low_keys = split(nt_dot(wq_ref[FEAT : 2 * FEAT, :], all_single))
    keys_ref[0] = high_keys
    keys_ref[1] = low_keys
    points = nt_dot(wp_ref[QPTS:, :], all_single)
    for t in range(tiles):
        pts_scr[t] = points[:, t * lane : (t + 1) * lane]
    features = nt_dot(queries[:, :S], wq_ref[:FEAT, :])
    qp_scr[:QPTS, :] = nt_dot(wp_ref[:QPTS, :], queries[:, :S])

    key_pts, query_pts = [], []
    for p in range(QP):
        key_pts += place(frames, [strided(pts_scr, 3 * p + y, HEADS, 3 * QP) for y in range(3)])
        query_pts += place(
            query_frames, [qp_scr[pl.ds(3 * p + y, HEADS, stride=3 * QP), :] for y in range(3)]
        )
    for k in range(3 * QP):
        key_pts_ref[k] = key_pts[k]
        query_pts_ref[k] = query_pts[k][:, local:]
    query_ref[...] = features[local:]

    chain_all = rows_ref[0:1, :]
    chain_row = jnp.where(upper == 0, chain_all[:, :n], chain_all[:, n:])
    real = jnp.where(upper == 0, rows_ref[1:2, :n], rows_ref[1:2, n:])
    near_ref[0:1, :] = chain_row
    near_ref[1:2, :] = real
    base = base_scores(
        features[:local], query_pts, high_keys, low_keys, key_pts, heads_ref, chain_all, chain_row,
        jnp.bitwise_xor(me, nsrc + 1) * local,
    )

    planes = place(frames, [strided(pts_scr, QPTS + y, PLANE, 3) for y in range(3)])
    gap = jnp.zeros((n, 128 - PLANE), F32)
    values = [nt_dot(all_single, wq_ref[2 * FEAT :, :]), jnp.zeros((n, 256 - FEAT), F32)]
    for plane in planes:
        values += [plane.T, gap]
    high, low = split(jnp.concatenate(values, axis=1))
    value_ref[0] = high
    value_ref[1] = low

    pair_rows(
        recv_ref, local, gains_ref[0:1, S:], w_swiglu_ref, w_down_ref, pair_scr
    )
    pair_sums, summed, level = partial_attention(
        base, real, high, low, wb_ref, pair_scr, attn_scr, sums_scr
    )
    for h in range(HEADS):
        send_ref[h] = pair_sums[h].astype(BF16)
    planes = into_frame(partner_ref, summed)
    send_ref[HEADS] = summed[:, :128].astype(BF16)
    send_ref[HEADS + 1] = summed[:, 128:256].astype(BF16)
    high = level.astype(BF16).astype(F32)
    middle = (level - high).astype(BF16).astype(F32)
    low = level - high - middle
    blank = jnp.zeros((local, 128 - PLANE - HPAD), F32)
    for x, part in enumerate([high, middle, low]):
        plane = planes[x][:, :PLANE]
        send_ref[HEADS + 2 + x] = jnp.concatenate([plane, part, blank], axis=1).astype(BF16)


def second_kernel(
    recv_ref,
    value_ref,
    near_ref,
    keys_ref,
    key_pts_ref,
    query_ref,
    query_pts_ref,
    heads_ref,
    rows_ref,
    gains_ref,
    wb_ref,
    w_swiglu_ref,
    w_down_ref,
    own_ref,
    sums_ref,
    wide_ref,
    level_ref,
    pair_scr,
    attn_scr,
    sums_scr,
):
    nsrc, _, local, _ = recv_ref.shape
    me = lax.axis_index("rows")
    pair_rows(
        recv_ref, 0, gains_ref[0:1, S:], w_swiglu_ref, w_down_ref, pair_scr
    )
    base = base_scores(
        query_ref[...], [query_pts_ref[k] for k in range(3 * QP)], keys_ref[0], keys_ref[1],
        [key_pts_ref[k] for k in range(3 * QP)], heads_ref, rows_ref[0:1, :], near_ref[0:1, :],
        me * local,
    )
    pair_sums, summed, level = partial_attention(
        base, near_ref[1:2, :], value_ref[0], value_ref[1], wb_ref, pair_scr, attn_scr, sums_scr
    )
    for h in range(HEADS):
        sums_ref[h] = pair_sums[h]
    wide_ref[:, :256] = summed[:, :256]
    for x, plane in enumerate(into_frame(own_ref, summed)):
        wide_ref[:, 256 + 128 * x : 384 + 128 * x] = plane
    level_ref[...] = jnp.concatenate(
        [jnp.zeros((local, PLANE), F32), level, jnp.zeros((local, 128 - PLANE - HPAD), F32)], axis=1
    )


def finish_kernel(
    got_ref,
    sums_ref,
    wide_ref,
    level_ref,
    own_ref,
    gains_ref,
    w_out_ref,
    w_loc_ref,
    out_ref,
):
    local = own_ref.shape[0]
    planes = [got_ref[HEADS + 2 + x].astype(F32) for x in range(3)]
    got = 1.0 / (1.0 + jnp.exp(level_ref[...] - (planes[0] + planes[1] + planes[2])))
    lanes = iota((local, 128), 1)
    low_share = jnp.zeros((local, 128), F32)
    high_share = jnp.zeros((local, 128), F32)
    plane_share = jnp.zeros((local, 128), F32)
    pair_total = []
    for h in range(HEADS):
        share = jnp.broadcast_to(got[:, PLANE + h : PLANE + h + 1], (local, 128))
        low_share = jnp.where(lanes // CH == h, share, low_share)
        high_share = jnp.where(lanes // CH + 8 == h, share, high_share)
        plane_share = jnp.where(lanes // VP == h, share, plane_share)
        mine = sums_ref[h]
        pair_total.append(mine + share * (got_ref[h].astype(F32) - mine))

    def joined(at, share, theirs):
        mine = wide_ref[:, at : at + 128]
        return mine + share * (theirs - mine)

    features = [
        joined(0, low_share, got_ref[HEADS].astype(F32)),
        joined(128, high_share, got_ref[HEADS + 1].astype(F32)),
    ]
    local_out = [joined(256 + 128 * x, plane_share, planes[x]) for x in range(3)]

    pair_total = jnp.concatenate(pair_total, axis=1).astype(BF16)
    at = FEAT + 4 * PLANE
    update = jnp.dot(pair_total, w_out_ref[at:, :], preferred_element_type=F32)
    update += jnp.dot(
        jnp.concatenate(features, axis=1)[:, :FEAT].astype(BF16),
        w_out_ref[:FEAT, :],
        preferred_element_type=F32,
    )

    lengths = jnp.sqrt(
        local_out[0] * local_out[0] + local_out[1] * local_out[1] + local_out[2] * local_out[2] + 1.0
    )
    for y in range(3):
        update += jnp.dot(
            local_out[y][:, :PLANE].astype(BF16), w_loc_ref[y], preferred_element_type=F32
        )
    update += jnp.dot(
        lengths[:, :PLANE].astype(BF16),
        w_out_ref[at - PLANE : at, :],
        preferred_element_type=F32,
    )
    own_single = own_ref[:, :S].astype(F32)
    out_ref[...] = layer_norm(own_single + update, gains_ref[0:1, :S]).astype(BF16)


def in_hbm(arrays):
    return [pltpu.with_memory_space_constraint(array, pltpu.HBM) for array in arrays]


def whole(memory=pltpu.VMEM):
    return pl.BlockSpec(memory_space=memory)


def params(mib):
    return pltpu.CompilerParams(vmem_limit_bytes=mib * MIB)


def on_device(
    single_rep,
    pair_grid,
    frames,
    chain_ids,
    pad_mask,
    ln_pair_gain,
    w_swiglu,
    w_pair_down,
    w_bias,
    w_qkv,
    w_points,
    gamma_raw,
    chain_bias,
    w_out,
    ln_single_gain,
):
    n, local, _ = pair_grid.shape
    size = n // local
    nsrc = size // 2
    near = n // 2
    tiles = max(1, near // 128)
    large = 4 * (n // 128)
    halves = [list(range(nsrc)), list(range(nsrc, size))]
    across = [(i, i ^ (nsrc + 1)) for i in range(size)]

    packed, own = pl.pallas_call(
        pack_kernel,
        out_shape=[
            jax.ShapeDtypeStruct((nsrc, 2 * local + SMALL, local, C), BF16),
            jax.ShapeDtypeStruct((local, S + 128), BF16),
        ],
        in_specs=[whole(pltpu.HBM)] * 3,
        out_specs=[whole(pltpu.HBM), whole()],
        scratch_shapes=[
            pltpu.VMEM((nsrc, 2 * local, local, C), BF16),
            pltpu.VMEM((nsrc, SMALL, local, C), BF16),
            pltpu.VMEM((local, 12), F32),
            pltpu.SemaphoreType.DMA((nsrc + 6,)),
            pltpu.SemaphoreType.DMA((5,)),
        ],
        compiler_params=params(4 + large),
        name="pack",
    )(*in_hbm([pair_grid.reshape(2, nsrc, local, local, C), single_rep, frames.T]))
    received = lax.all_to_all(
        packed, "rows", 0, 0, tiled=True, axis_index_groups=halves
    )
    partner = lax.ppermute(own, "rows", across)

    sources = [
        pair_grid,
        w_swiglu,
        w_pair_down,
        ln_pair_gain,
        gamma_raw,
        chain_bias,
        chain_ids,
        pad_mask,
        ln_single_gain,
        w_bias.T,
        w_out,
        w_qkv.T,
        w_points.T,
    ]
    held = [pltpu.VMEM(x.shape, x.dtype) for x in sources[:10]]
    held.append(pltpu.VMEM((3 * PLANE, S), BF16))
    pair_out, heads, rows, gains, wb, w_loc, wq, wp = pl.pallas_call(
        own_kernel,
        out_shape=[
            jax.ShapeDtypeStruct(pair_grid.shape, BF16),
            jax.ShapeDtypeStruct((3, HPAD, 128), F32),
            jax.ShapeDtypeStruct((2, n), jnp.int32),
            jax.ShapeDtypeStruct((1, S + C), F32),
            jax.ShapeDtypeStruct((HPAD, C), BF16),
            jax.ShapeDtypeStruct((3, PLANE, S), BF16),
            jax.ShapeDtypeStruct(sources[11].shape, BF16),
            jax.ShapeDtypeStruct(sources[12].shape, BF16),
        ],
        in_specs=[whole(pltpu.HBM)] * len(sources),
        out_specs=[whole()] * 8,
        scratch_shapes=held
        + [
            pltpu.VMEM((S // 128, 3 * PLANE, 128), F32),
            pltpu.SemaphoreType.DMA((len(sources),)),
        ],
        compiler_params=params(18 + large),
        name="own_transition",
    )(*in_hbm(sources))

    scratch = [
        pltpu.VMEM((local, near, C), BF16),
        pltpu.VMEM((2 * local * HPAD, near), BF16),
        pltpu.VMEM((local * HPAD, C), F32),
    ]
    send, *held = pl.pallas_call(
        first_kernel,
        out_shape=[
            jax.ShapeDtypeStruct((PARTS, local, 128), BF16),
            jax.ShapeDtypeStruct((2, near, WIDE), BF16),
            jax.ShapeDtypeStruct((2, near), jnp.int32),
            jax.ShapeDtypeStruct((2, FEAT, near), BF16),
            jax.ShapeDtypeStruct((3 * QP, HEADS, near), F32),
            jax.ShapeDtypeStruct((local, FEAT), F32),
            jax.ShapeDtypeStruct((3 * QP, HEADS, local), F32),
        ],
        in_specs=[whole()] * 11,
        out_specs=[whole()] * 7,
        scratch_shapes=[
            pltpu.VMEM((tiles, QPTS + 3 * PLANE, near // tiles), F32),
            pltpu.VMEM((QPTS + 4 * 3 * QP, 2 * local), F32),
        ]
        + scratch,
        compiler_params=params(16 + large),
        name="first_half",
    )(received, own, partner, heads, rows, gains, wq, wp, wb, w_swiglu, w_pair_down)
    got = lax.ppermute(send, "rows", across)

    sums, wide, level = pl.pallas_call(
        second_kernel,
        out_shape=[
            jax.ShapeDtypeStruct((HEADS, local, 128), F32),
            jax.ShapeDtypeStruct((local, WIDE), F32),
            jax.ShapeDtypeStruct((local, 128), F32),
        ],
        in_specs=[whole()] * 14,
        out_specs=[whole()] * 3,
        scratch_shapes=scratch,
        compiler_params=params(12 + large),
        name="second_half",
    )(received, *held, heads, rows, gains, wb, w_swiglu, w_pair_down, own)

    single_out = pl.pallas_call(
        finish_kernel,
        out_shape=jax.ShapeDtypeStruct((local, S), BF16),
        in_specs=[whole()] * 8,
        out_specs=whole(),
        compiler_params=params(12),
        name="finish",
    )(got, sums, wide, level, own, gains, w_out, w_loc)
    return (single_out, pair_out)


def solution(mesh):
    placed = (
        P(("groups", "rows"), None),
        P("groups", "rows", None),
        P(None, ("groups", "rows")),
        P("groups"),
        P("groups"),
    ) + (P(),) * 10
    return jax.shard_map(
        on_device,
        mesh=mesh,
        in_specs=placed,
        out_specs=(P(("groups", "rows"), None), P("groups", "rows", None)),
        check_vma=False,
    )
```

```python
import math

import jax
import jax.numpy as jnp
from jax import lax
from jax.experimental import pallas as pl
from jax.experimental.pallas import tpu as pltpu
from jax.sharding import PartitionSpec as P

C = 128
S = 384
H = 512
HEADS = 12
CH = 16
QP = 4
VP = 8
HPAD = 16
FEAT = HEADS * CH
QPTS = HEADS * QP * 3
PLANE = HEADS * VP
WIDE = 256 + 3 * 128
SMALL = S // 128 + 1
PIECES = 2
PARTS = HEADS + WIDE // 128
F32 = jnp.float32
BF16 = jnp.bfloat16
NT = (((1,), (1,)), ((), ()))
MIB = 1024 * 1024
WEIGHT_L = math.sqrt(1.0 / 3.0)
WEIGHT_C = math.sqrt(2.0 / (9.0 * QP))


def iota(shape, dim):
    return lax.broadcasted_iota(jnp.int32, shape, dim)


def nt_dot(a, b):
    return lax.dot_general(a, b, NT, preferred_element_type=F32)


def layer_norm(values, gain):
    centre = jnp.mean(values, axis=-1, keepdims=True)
    centred = values - centre
    spread = jnp.mean(centred * centred, axis=-1, keepdims=True)
    return centred * lax.rsqrt(spread + 1e-05) * gain


def transition(values, gain, w_swiglu_ref, w_down_ref):
    normed = layer_norm(values, gain).astype(BF16)
    both = jnp.dot(normed, w_swiglu_ref[...], preferred_element_type=F32)
    gate = 0.5 * both[:, :H]
    hidden = (gate * (1.0 + jnp.tanh(gate)) * both[:, H:]).astype(BF16)
    update = jnp.dot(hidden, w_down_ref[...], preferred_element_type=F32)
    return (values + update).astype(BF16)


def split(values):
    high = values.astype(BF16)
    return high, (values - high.astype(F32)).astype(BF16)


def pack_kernel(
    pair_hbm, single_hbm, frames_hbm, out_hbm, own_ref, pair_ref, small_ref, frames_ref, in_sems, out_sems
):
    chips = pair_ref.shape[0]
    local = own_ref.shape[0]
    upper = lax.axis_index("rows") // (2 * chips)
    step = max(1, chips // PIECES)
    starts = range(0, chips, step)
    arrivals = []
    for at in starts:
        span = pl.ds(at, step)
        moves = [(pair_hbm.at[upper, span], pair_ref.at[span, :, pl.ds(0, local)])]
        for core in range(2):
            moves.append(
                (
                    pair_hbm.at[1 - upper, span, 1 - core],
                    pair_ref.at[span, core, pl.ds(local, local)],
                )
            )
        for source, target in moves:
            arrivals.append(pltpu.make_async_copy(source, target, in_sems.at[len(arrivals)]))
    rows_copies = [
        pltpu.make_async_copy(single_hbm, own_ref.at[:, :S], in_sems.at[len(arrivals)]),
        pltpu.make_async_copy(frames_hbm, frames_ref, in_sems.at[len(arrivals) + 1]),
    ]
    for copy in rows_copies + arrivals:
        copy.start()
    for copy in rows_copies:
        copy.wait()
    rows = frames_ref[...]
    blank = jnp.zeros((local, 128 - 36), F32)
    turned = jnp.concatenate([rows, rows, rows, blank], axis=1)
    high = turned.astype(BF16).astype(F32)
    middle = (turned - high).astype(BF16).astype(F32)
    low = turned - high - middle
    lane = iota(turned.shape, 1)
    own_ref[:, S:] = jnp.where(lane < 12, high, jnp.where(lane < 24, middle, low)).astype(BF16)
    for chip in range(chips):
        for core in range(2):
            for piece in range(SMALL):
                small_ref[chip, core, piece] = own_ref[:, piece * 128 : piece * 128 + 128]
    departures = [
        pltpu.make_async_copy(small_ref, out_hbm.at[:, :, pl.ds(2 * local, SMALL)], out_sems.at[0])
    ]
    departures[0].start()
    for k, at in enumerate(starts):
        for copy in arrivals[3 * k : 3 * k + 3]:
            copy.wait()
        departures.append(
            pltpu.make_async_copy(
                pair_ref.at[pl.ds(at, step)],
                out_hbm.at[pl.ds(at, step), :, pl.ds(0, 2 * local)],
                out_sems.at[1 + k],
            )
        )
        departures[-1].start()
    for copy in departures:
        copy.wait()


def strided(ref, start, count, stride):
    return jnp.concatenate(
        [ref[t, pl.ds(start, count, stride=stride), :] for t in range(ref.shape[0])], axis=1
    )


def own_kernel(*refs):
    sources, refs = refs[:13], refs[13:]
    out_ref, heads_ref, rows_ref, gains_ref, wb_out_ref, w_loc_ref, wq_ref, wp_ref = refs[:8]
    held, refs = refs[8:19], refs[19:]
    loc_scr, sems = refs
    pair_hbm, *_ = sources
    n, local, _ = pair_hbm.shape
    targets = list(held) + [wq_ref, wp_ref]
    copies = []
    for k, (source, target) in enumerate(zip(sources, targets)):
        if k == 10:
            source = source.at[pl.ds(FEAT, 3 * PLANE)]
        copies.append(pltpu.make_async_copy(source, target, sems.at[k]))
        copies[k].start()
    pair_ref, w_swiglu_ref, w_down_ref, gain_ref, gamma_ref, cb_ref = held[:6]
    chain_ref, pad_ref, gain2_ref, wb_ref, loc_ref = held[6:]
    for copy in copies[:4]:
        copy.wait()
    gain = gain_ref[...].reshape(1, C)
    block = math.gcd(n, 128)

    def step(at):
        values = pair_ref[pl.ds(at, block)].astype(F32).reshape(-1, C)
        done = transition(values, gain, w_swiglu_ref, w_down_ref)
        out_ref[pl.ds(at, block)] = done.astype(F32).reshape(-1, local, C).astype(BF16)

    if n == block:
        step(0)
    else:
        pl.loop(0, n, step=block)(step)
    for copy in copies[4:]:
        copy.wait()

    diagonal = iota((HPAD, HEADS), 0) == iota((HPAD, HEADS), 1)

    def column(row):
        turned = jnp.sum(jnp.where(diagonal, row, 0.0), axis=1, keepdims=True)
        return jnp.broadcast_to(turned, (HPAD, 128))

    gamma = jax.nn.softplus(gamma_ref[...].reshape(1, HEADS))
    heads_ref[0] = column(gamma * (-0.5 * WEIGHT_C))
    heads_ref[1] = column(cb_ref[0:1, :])
    heads_ref[2] = column(cb_ref[1:2, :])
    rows_ref[0:1, :] = chain_ref[...].reshape(1, n)
    rows_ref[1:2, :] = pad_ref[...].reshape(1, n)
    gains_ref[0:1, :S] = gain2_ref[...].reshape(1, S)
    gains_ref[0:1, S:] = gain
    wb_out_ref[...] = jnp.concatenate(
        [wb_ref[...], jnp.zeros((HPAD - HEADS, C), BF16)], axis=0
    )
    local_rows = loc_ref[...].astype(F32)
    for t in range(S // 128):
        loc_scr[t] = local_rows[:, t * 128 : (t + 1) * 128]
    for y in range(3):
        w_loc_ref[y] = strided(loc_scr, y, PLANE, 3).astype(BF16)


def place(frame, triple):
    return [
        frame[3 * x : 3 * x + 1, :] * triple[0]
        + frame[3 * x + 1 : 3 * x + 2, :] * triple[1]
        + frame[3 * x + 2 : 3 * x + 3, :] * triple[2]
        + frame[9 + x : 10 + x, :]
        for x in range(3)
    ]


def head_of_lane(rows):
    lanes = iota((rows, WIDE), 1)
    return jnp.where(lanes < 256, lanes // CH, (lanes % 128) // VP)


def base_scores(
    queries, query_pts, high_keys, low_keys, key_pts, heads_ref, chain_all, chain_row, first
):
    local = queries.shape[0]
    n = high_keys.shape[1]
    rows = local * HPAD
    owned = (iota((HPAD, FEAT), 1) // CH == iota((HPAD, FEAT), 0))[None]
    spread = jnp.broadcast_to(queries.reshape(local, 1, FEAT), (local, HPAD, FEAT))
    high, low = split(jnp.where(owned, spread, 0.0).reshape(rows, FEAT))
    both = jnp.dot(jnp.concatenate([high, low], axis=0), high_keys, preferred_element_type=F32)
    dots = both[:rows] + both[rows:] + jnp.dot(high, low_keys, preferred_element_type=F32)
    distances = []
    blank = jnp.zeros((HPAD - HEADS, n), F32)
    for i in range(local):
        distance = 0.0
        for q, k in zip(query_pts, key_pts):
            apart = q[:, i : i + 1] - k
            distance = distance + apart * apart
        distances += [distance, blank]
    distance = jnp.concatenate(distances, axis=0)

    def per_row(index):
        wide = jnp.concatenate([heads_ref[index]] * max(1, n // 128), axis=1)[:, :n]
        return jnp.concatenate([wide] * local, axis=0)

    width = chain_all.shape[1]
    lanes, order = iota((local, width), 1), iota((local, width), 0)
    mine = jnp.sum(jnp.where(lanes == first + order, chain_all, 0), axis=1, keepdims=True)
    mine = jnp.broadcast_to(mine.reshape(local, 1, 1), (local, HPAD, n)).reshape(rows, n)
    chain = jnp.where(chain_row == mine, per_row(1), per_row(2))
    return WEIGHT_L * (dots * (1.0 / math.sqrt(CH)) + chain + per_row(0) * distance)


def pair_rows(recv_ref, at, gain, w_swiglu_ref, w_down_ref, pair_scr):
    nsrc, _, local, _ = recv_ref.shape
    n = nsrc * local
    group = max(1, min(local, 512 // n))
    for start in range(0, local, group):
        block = recv_ref[:, pl.ds(at + start, group)].astype(F32)
        block = jnp.concatenate([block[:, k].reshape(n, C) for k in range(group)], axis=0)
        done = transition(block, gain, w_swiglu_ref, w_down_ref)
        for k in range(group):
            pair_scr[start + k] = done[k * n : (k + 1) * n]


def partial_attention(base, real, high_value, low_value, wb_ref, pair_scr, attn_scr, sums_scr):
    local, n, _ = pair_scr.shape
    rows = local * HPAD
    bias = jnp.concatenate([nt_dot(wb_ref[...], pair_scr[i]) for i in range(local)], axis=0)
    scores = base + WEIGHT_L * bias
    scores = jnp.where(jnp.broadcast_to(real, (rows, n)) > 0, scores, -1000000000.0)
    peak = jnp.max(scores, axis=-1, keepdims=True)
    expo = jnp.exp(scores - peak)
    high, low = split(expo)
    total = jnp.sum(expo, axis=-1, keepdims=True)
    share = 1.0 / total
    attn_scr[:rows] = high
    attn_scr[rows:] = low
    for i in range(local):
        at = i * HPAD
        sums_scr[at : at + HPAD, :] = share[at : at + HPAD] * jnp.dot(
            high[at : at + HPAD], pair_scr[i], preferred_element_type=F32
        )
    both = jnp.dot(attn_scr[...], high_value, preferred_element_type=F32)
    every = both[:rows] + both[rows:]
    every += jnp.dot(attn_scr[:rows], low_value, preferred_element_type=F32)
    every *= share
    owned = head_of_lane(HPAD) == iota((HPAD, WIDE), 0)
    every = every.reshape(local, HPAD, WIDE)
    summed = jnp.sum(jnp.where(owned[None], every, 0.0), axis=1)
    diagonal = (iota((HPAD, HPAD), 0) == iota((HPAD, HPAD), 1))[None]

    level = jnp.broadcast_to((peak + jnp.log(total)).reshape(local, HPAD, 1), (local, HPAD, HPAD))
    level = jnp.sum(jnp.where(diagonal, level, 0.0), axis=1)
    pair_sums = [sums_scr[pl.ds(h, local, stride=HPAD), :] for h in range(HEADS)]
    return pair_sums, summed, level


def origin(row_ref):
    parts = row_ref[:, S:].astype(F32)
    return parts[:, 0:12] + parts[:, 12:24] + parts[:, 24:36]


def into_frame(row_ref, summed):
    turned = origin(row_ref)
    shifted = [
        summed[:, 256 + 128 * x : 384 + 128 * x] - turned[:, 9 + x : 10 + x] for x in range(3)
    ]
    return [
        turned[:, y : y + 1] * shifted[0]
        + turned[:, 3 + y : 4 + y] * shifted[1]
        + turned[:, 6 + y : 7 + y] * shifted[2]
        for y in range(3)
    ]


def first_kernel(
    recv_ref,
    own_ref,
    partner_ref,
    heads_ref,
    rows_ref,
    gains_ref,
    wq_ref,
    wp_ref,
    wb_ref,
    w_swiglu_ref,
    w_down_ref,
    send_ref,
    value_ref,
    near_ref,
    keys_ref,
    key_pts_ref,
    query_ref,
    query_pts_ref,
    pts_scr,
    qp_scr,
    pair_scr,
    attn_scr,
    sums_scr,
):
    nsrc, _, local, _ = recv_ref.shape
    tiles, _, lane = pts_scr.shape
    n = nsrc * local
    me = lax.axis_index("rows")
    upper = me // nsrc

    def piece(index):
        return recv_ref[:, index].astype(F32).reshape(n, 128).astype(BF16)

    all_single = jnp.concatenate([piece(2 * local + k) for k in range(SMALL - 1)], axis=1)
    queries = jnp.concatenate(
        [partner_ref[...].astype(F32), own_ref[...].astype(F32)], axis=0
    ).astype(BF16)
    rows16, lanes16 = iota((16, 128), 0), iota((16, 128), 1)
    pick = ((lanes16 % 12 == rows16) & (lanes16 < 36)).astype(BF16)
    frames = nt_dot(pick, piece(2 * local + SMALL - 1))
    query_frames = nt_dot(pick, queries[:, S:])

    high_keys, low_keys = split(nt_dot(wq_ref[FEAT : 2 * FEAT, :], all_single))
    keys_ref[0] = high_keys
    keys_ref[1] = low_keys
    points = nt_dot(wp_ref[QPTS:, :], all_single)
    for t in range(tiles):
        pts_scr[t] = points[:, t * lane : (t + 1) * lane]
    features = nt_dot(queries[:, :S], wq_ref[:FEAT, :])
    qp_scr[:QPTS, :] = nt_dot(wp_ref[:QPTS, :], queries[:, :S])

    key_pts, query_pts = [], []
    for p in range(QP):
        key_pts += place(frames, [strided(pts_scr, 3 * p + y, HEADS, 3 * QP) for y in range(3)])
        query_pts += place(
            query_frames, [qp_scr[pl.ds(3 * p + y, HEADS, stride=3 * QP), :] for y in range(3)]
        )
    for k in range(3 * QP):
        key_pts_ref[k] = key_pts[k]
        query_pts_ref[k] = query_pts[k][:, local:]
    query_ref[...] = features[local:]

    chain_all = rows_ref[0:1, :]
    chain_row = jnp.where(upper == 0, chain_all[:, :n], chain_all[:, n:])
    real = jnp.where(upper == 0, rows_ref[1:2, :n], rows_ref[1:2, n:])
    near_ref[0:1, :] = chain_row
    near_ref[1:2, :] = real
    base = base_scores(
        features[:local], query_pts, high_keys, low_keys, key_pts, heads_ref, chain_all, chain_row,
        jnp.bitwise_xor(me, nsrc + 1) * local,
    )

    planes = place(frames, [strided(pts_scr, QPTS + y, PLANE, 3) for y in range(3)])
    gap = jnp.zeros((n, 128 - PLANE), F32)
    values = [nt_dot(all_single, wq_ref[2 * FEAT :, :]), jnp.zeros((n, 256 - FEAT), F32)]
    for plane in planes:
        values += [plane.T, gap]
    high, low = split(jnp.concatenate(values, axis=1))
    value_ref[0] = high
    value_ref[1] = low

    pair_rows(
        recv_ref, local, gains_ref[0:1, S:], w_swiglu_ref, w_down_ref, pair_scr
    )
    pair_sums, summed, level = partial_attention(
        base, real, high, low, wb_ref, pair_scr, attn_scr, sums_scr
    )
    for h in range(HEADS):
        send_ref[h] = pair_sums[h].astype(BF16)
    planes = into_frame(partner_ref, summed)
    send_ref[HEADS] = summed[:, :128].astype(BF16)
    send_ref[HEADS + 1] = summed[:, 128:256].astype(BF16)
    high = level.astype(BF16).astype(F32)
    middle = (level - high).astype(BF16).astype(F32)
    low = level - high - middle
    blank = jnp.zeros((local, 128 - PLANE - HPAD), F32)
    for x, part in enumerate([high, middle, low]):
        plane = planes[x][:, :PLANE]
        send_ref[HEADS + 2 + x] = jnp.concatenate([plane, part, blank], axis=1).astype(BF16)


def second_kernel(
    recv_ref,
    value_ref,
    near_ref,
    keys_ref,
    key_pts_ref,
    query_ref,
    query_pts_ref,
    heads_ref,
    rows_ref,
    gains_ref,
    wb_ref,
    w_swiglu_ref,
    w_down_ref,
    own_ref,
    sums_ref,
    wide_ref,
    level_ref,
    pair_scr,
    attn_scr,
    sums_scr,
):
    nsrc, _, local, _ = recv_ref.shape
    me = lax.axis_index("rows")
    pair_rows(
        recv_ref, 0, gains_ref[0:1, S:], w_swiglu_ref, w_down_ref, pair_scr
    )
    base = base_scores(
        query_ref[...], [query_pts_ref[k] for k in range(3 * QP)], keys_ref[0], keys_ref[1],
        [key_pts_ref[k] for k in range(3 * QP)], heads_ref, rows_ref[0:1, :], near_ref[0:1, :],
        me * local,
    )
    pair_sums, summed, level = partial_attention(
        base, near_ref[1:2, :], value_ref[0], value_ref[1], wb_ref, pair_scr, attn_scr, sums_scr
    )
    for h in range(HEADS):
        sums_ref[h] = pair_sums[h]
    wide_ref[:, :256] = summed[:, :256]
    for x, plane in enumerate(into_frame(own_ref, summed)):
        wide_ref[:, 256 + 128 * x : 384 + 128 * x] = plane
    level_ref[...] = jnp.concatenate(
        [jnp.zeros((local, PLANE), F32), level, jnp.zeros((local, 128 - PLANE - HPAD), F32)], axis=1
    )


def finish_kernel(
    got_ref,
    sums_ref,
    wide_ref,
    level_ref,
    own_ref,
    gains_ref,
    w_out_ref,
    w_loc_ref,
    out_ref,
):
    local = own_ref.shape[0]
    planes = [got_ref[HEADS + 2 + x].astype(F32) for x in range(3)]
    got = 1.0 / (1.0 + jnp.exp(level_ref[...] - (planes[0] + planes[1] + planes[2])))
    lanes = iota((local, 128), 1)
    low_share = jnp.zeros((local, 128), F32)
    high_share = jnp.zeros((local, 128), F32)
    plane_share = jnp.zeros((local, 128), F32)
    pair_total = []
    for h in range(HEADS):
        share = jnp.broadcast_to(got[:, PLANE + h : PLANE + h + 1], (local, 128))
        low_share = jnp.where(lanes // CH == h, share, low_share)
        high_share = jnp.where(lanes // CH + 8 == h, share, high_share)
        plane_share = jnp.where(lanes // VP == h, share, plane_share)
        mine = sums_ref[h]
        pair_total.append(mine + share * (got_ref[h].astype(F32) - mine))

    def joined(at, share, theirs):
        mine = wide_ref[:, at : at + 128]
        return mine + share * (theirs - mine)

    features = [
        joined(0, low_share, got_ref[HEADS].astype(F32)),
        joined(128, high_share, got_ref[HEADS + 1].astype(F32)),
    ]
    local_out = [joined(256 + 128 * x, plane_share, planes[x]) for x in range(3)]

    pair_total = jnp.concatenate(pair_total, axis=1).astype(BF16)
    at = FEAT + 4 * PLANE
    update = jnp.dot(pair_total, w_out_ref[at:, :], preferred_element_type=F32)
    update += jnp.dot(
        jnp.concatenate(features, axis=1)[:, :FEAT].astype(BF16),
        w_out_ref[:FEAT, :],
        preferred_element_type=F32,
    )

    lengths = jnp.sqrt(
        local_out[0] * local_out[0] + local_out[1] * local_out[1] + local_out[2] * local_out[2] + 1.0
    )
    for y in range(3):
        update += jnp.dot(
            local_out[y][:, :PLANE].astype(BF16), w_loc_ref[y], preferred_element_type=F32
        )
    update += jnp.dot(
        lengths[:, :PLANE].astype(BF16),
        w_out_ref[at - PLANE : at, :],
        preferred_element_type=F32,
    )
    own_single = own_ref[:, :S].astype(F32)
    out_ref[...] = layer_norm(own_single + update, gains_ref[0:1, :S]).astype(BF16)


def in_hbm(arrays):
    return [pltpu.with_memory_space_constraint(array, pltpu.HBM) for array in arrays]


def whole(memory=pltpu.VMEM):
    return pl.BlockSpec(memory_space=memory)


def params(mib):
    return pltpu.CompilerParams(vmem_limit_bytes=mib * MIB)


def on_device(
    single_rep,
    pair_grid,
    frames,
    chain_ids,
    pad_mask,
    ln_pair_gain,
    w_swiglu,
    w_pair_down,
    w_bias,
    w_qkv,
    w_points,
    gamma_raw,
    chain_bias,
    w_out,
    ln_single_gain,
):
    n, local, _ = pair_grid.shape
    size = n // local
    nsrc = size // 2
    near = n // 2
    tiles = max(1, near // 128)
    large = 4 * (n // 128)
    halves = [list(range(nsrc)), list(range(nsrc, size))]
    across = [(i, i ^ (nsrc + 1)) for i in range(size)]

    packed, own = pl.pallas_call(
        pack_kernel,
        out_shape=[
            jax.ShapeDtypeStruct((nsrc // 2, 2, 2 * local + SMALL, local, C), BF16),
            jax.ShapeDtypeStruct((local, S + 128), BF16),
        ],
        in_specs=[whole(pltpu.HBM)] * 3,
        out_specs=[whole(pltpu.HBM), whole()],
        scratch_shapes=[
            pltpu.VMEM((nsrc // 2, 2, 2 * local, local, C), BF16),
            pltpu.VMEM((nsrc // 2, 2, SMALL, local, C), BF16),
            pltpu.VMEM((local, 12), F32),
            pltpu.SemaphoreType.DMA((3 * PIECES + 2,)),
            pltpu.SemaphoreType.DMA((PIECES + 1,)),
        ],
        compiler_params=params(4 + large),
        name="pack",
    )(*in_hbm([pair_grid.reshape(2, nsrc // 2, 2, local, local, C), single_rep, frames.T]))
    received = lax.all_to_all(
        packed.reshape(nsrc, 2 * local + SMALL, local, C), "rows", 0, 0, tiled=True, axis_index_groups=halves
    )
    partner = lax.ppermute(own, "rows", across)

    sources = [
        pair_grid,
        w_swiglu,
        w_pair_down,
        ln_pair_gain,
        gamma_raw,
        chain_bias,
        chain_ids,
        pad_mask,
        ln_single_gain,
        w_bias.T,
        w_out,
        w_qkv.T,
        w_points.T,
    ]
    held = [pltpu.VMEM(x.shape, x.dtype) for x in sources[:10]]
    held.append(pltpu.VMEM((3 * PLANE, S), BF16))
    pair_out, heads, rows, gains, wb, w_loc, wq, wp = pl.pallas_call(
        own_kernel,
        out_shape=[
            jax.ShapeDtypeStruct(pair_grid.shape, BF16),
            jax.ShapeDtypeStruct((3, HPAD, 128), F32),
            jax.ShapeDtypeStruct((2, n), jnp.int32),
            jax.ShapeDtypeStruct((1, S + C), F32),
            jax.ShapeDtypeStruct((HPAD, C), BF16),
            jax.ShapeDtypeStruct((3, PLANE, S), BF16),
            jax.ShapeDtypeStruct(sources[11].shape, BF16),
            jax.ShapeDtypeStruct(sources[12].shape, BF16),
        ],
        in_specs=[whole(pltpu.HBM)] * len(sources),
        out_specs=[whole()] * 8,
        scratch_shapes=held
        + [
            pltpu.VMEM((S // 128, 3 * PLANE, 128), F32),
            pltpu.SemaphoreType.DMA((len(sources),)),
        ],
        compiler_params=params(18 + large),
        name="own_transition",
    )(*in_hbm(sources))

    scratch = [
        pltpu.VMEM((local, near, C), BF16),
        pltpu.VMEM((2 * local * HPAD, near), BF16),
        pltpu.VMEM((local * HPAD, C), F32),
    ]
    send, *held = pl.pallas_call(
        first_kernel,
        out_shape=[
            jax.ShapeDtypeStruct((PARTS, local, 128), BF16),
            jax.ShapeDtypeStruct((2, near, WIDE), BF16),
            jax.ShapeDtypeStruct((2, near), jnp.int32),
            jax.ShapeDtypeStruct((2, FEAT, near), BF16),
            jax.ShapeDtypeStruct((3 * QP, HEADS, near), F32),
            jax.ShapeDtypeStruct((local, FEAT), F32),
            jax.ShapeDtypeStruct((3 * QP, HEADS, local), F32),
        ],
        in_specs=[whole()] * 11,
        out_specs=[whole()] * 7,
        scratch_shapes=[
            pltpu.VMEM((tiles, QPTS + 3 * PLANE, near // tiles), F32),
            pltpu.VMEM((QPTS + 4 * 3 * QP, 2 * local), F32),
        ]
        + scratch,
        compiler_params=params(16 + large),
        name="first_half",
    )(received, own, partner, heads, rows, gains, wq, wp, wb, w_swiglu, w_pair_down)
    got = lax.ppermute(send, "rows", across)

    sums, wide, level = pl.pallas_call(
        second_kernel,
        out_shape=[
            jax.ShapeDtypeStruct((HEADS, local, 128), F32),
            jax.ShapeDtypeStruct((local, WIDE), F32),
            jax.ShapeDtypeStruct((local, 128), F32),
        ],
        in_specs=[whole()] * 14,
        out_specs=[whole()] * 3,
        scratch_shapes=scratch,
        compiler_params=params(12 + large),
        name="second_half",
    )(received, *held, heads, rows, gains, wb, w_swiglu, w_pair_down, own)

    single_out = pl.pallas_call(
        finish_kernel,
        out_shape=jax.ShapeDtypeStruct((local, S), BF16),
        in_specs=[whole()] * 8,
        out_specs=whole(),
        compiler_params=params(12),
        name="finish",
    )(got, sums, wide, level, own, gains, w_out, w_loc)
    return (single_out, pair_out)


def solution(mesh):
    placed = (
        P(("groups", "rows"), None),
        P("groups", "rows", None),
        P(None, ("groups", "rows")),
        P("groups"),
        P("groups"),
    ) + (P(),) * 10
    return jax.shard_map(
        on_device,
        mesh=mesh,
        in_specs=placed,
        out_specs=(P(("groups", "rows"), None), P("groups", "rows", None)),
        check_vma=False,
    )
```

```python
import math

import jax
import jax.numpy as jnp
from jax import lax
from jax.experimental import pallas as pl
from jax.experimental.pallas import tpu as pltpu
from jax.sharding import PartitionSpec as P

C = 128
S = 384
H = 512
HEADS = 12
CH = 16
QP = 4
VP = 8
HPAD = 16
FEAT = HEADS * CH
QPTS = HEADS * QP * 3
PLANE = HEADS * VP
WIDE = 256 + 3 * 128
SMALL = S // 128 + 1
PIECES = 2
PARTS = HEADS + WIDE // 128
F32 = jnp.float32
BF16 = jnp.bfloat16
NT = (((1,), (1,)), ((), ()))
MIB = 1024 * 1024
WEIGHT_L = math.sqrt(1.0 / 3.0)
WEIGHT_C = math.sqrt(2.0 / (9.0 * QP))


def iota(shape, dim):
    return lax.broadcasted_iota(jnp.int32, shape, dim)


def nt_dot(a, b):
    return lax.dot_general(a, b, NT, preferred_element_type=F32)


def layer_norm(values, gain):
    centre = jnp.mean(values, axis=-1, keepdims=True)
    centred = values - centre
    spread = jnp.mean(centred * centred, axis=-1, keepdims=True)
    return centred * lax.rsqrt(spread + 1e-05) * gain


def transition(values, gain, w_swiglu_ref, w_down_ref):
    normed = layer_norm(values, gain).astype(BF16)
    both = jnp.dot(normed, w_swiglu_ref[...], preferred_element_type=F32)
    gate = 0.5 * both[:, :H]
    hidden = (gate * (1.0 + jnp.tanh(gate)) * both[:, H:]).astype(BF16)
    update = jnp.dot(hidden, w_down_ref[...], preferred_element_type=F32)
    return (values + update).astype(BF16)


def split(values):
    high = values.astype(BF16)
    return high, (values - high.astype(F32)).astype(BF16)


def pack_kernel(
    pair_hbm, single_hbm, frames_hbm, out_hbm, own_ref, pair_ref, small_ref, frames_ref, in_sems, out_sems
):
    chips = pair_ref.shape[0]
    local = own_ref.shape[0]
    upper = lax.axis_index("rows") // (2 * chips)
    step = max(1, chips // PIECES)
    starts = range(0, chips, step)
    arrivals = []
    for at in starts:
        span = pl.ds(at, step)
        moves = [(pair_hbm.at[upper, span], pair_ref.at[span, :, pl.ds(0, local)])]
        for core in range(2):
            moves.append(
                (
                    pair_hbm.at[1 - upper, span, 1 - core],
                    pair_ref.at[span, core, pl.ds(local, local)],
                )
            )
        for source, target in moves:
            arrivals.append(pltpu.make_async_copy(source, target, in_sems.at[len(arrivals)]))
    rows_copies = [
        pltpu.make_async_copy(single_hbm, own_ref.at[:, :S], in_sems.at[len(arrivals)]),
        pltpu.make_async_copy(frames_hbm, frames_ref, in_sems.at[len(arrivals) + 1]),
    ]
    for copy in rows_copies + arrivals:
        copy.start()
    for copy in rows_copies:
        copy.wait()
    rows = frames_ref[...]
    blank = jnp.zeros((local, 128 - 36), F32)
    turned = jnp.concatenate([rows, rows, rows, blank], axis=1)
    high = turned.astype(BF16).astype(F32)
    middle = (turned - high).astype(BF16).astype(F32)
    low = turned - high - middle
    lane = iota(turned.shape, 1)
    own_ref[:, S:] = jnp.where(lane < 12, high, jnp.where(lane < 24, middle, low)).astype(BF16)
    for chip in range(chips):
        for core in range(2):
            for piece in range(SMALL):
                small_ref[chip, core, piece] = own_ref[:, piece * 128 : piece * 128 + 128]
    departures = [
        pltpu.make_async_copy(small_ref, out_hbm.at[:, :, pl.ds(2 * local, SMALL)], out_sems.at[0])
    ]
    departures[0].start()
    for k, at in enumerate(starts):
        for copy in arrivals[3 * k : 3 * k + 3]:
            copy.wait()
        departures.append(
            pltpu.make_async_copy(
                pair_ref.at[pl.ds(at, step)],
                out_hbm.at[pl.ds(at, step), :, pl.ds(0, 2 * local)],
                out_sems.at[1 + k],
            )
        )
        departures[-1].start()
    for copy in departures:
        copy.wait()


def strided(ref, start, count, stride):
    return jnp.concatenate(
        [ref[t, pl.ds(start, count, stride=stride), :] for t in range(ref.shape[0])], axis=1
    )


def own_kernel(*refs):
    sources, refs = refs[:13], refs[13:]
    out_hbm, heads_ref, rows_ref, gains_ref, wb_out_ref, w_loc_ref, wq_ref, wp_ref = refs[:8]
    held, refs = refs[8:19], refs[19:]
    done_ref, loc_scr, sems, out_sem = refs
    pair_hbm, *_ = sources
    n, local, _ = pair_hbm.shape
    targets = list(held) + [wq_ref, wp_ref]
    copies = []
    for k, (source, target) in enumerate(zip(sources, targets)):
        if k == 10:
            source = source.at[pl.ds(FEAT, 3 * PLANE)]
        copies.append(pltpu.make_async_copy(source, target, sems.at[k]))
        copies[k].start()
    pair_ref, w_swiglu_ref, w_down_ref, gain_ref, gamma_ref, cb_ref = held[:6]
    chain_ref, pad_ref, gain2_ref, wb_ref, loc_ref = held[6:]
    for copy in copies[:4]:
        copy.wait()
    gain = gain_ref[...].reshape(1, C)
    block = math.gcd(n, 128)

    def step(at):
        values = pair_ref[pl.ds(at, block)].astype(F32).reshape(-1, C)
        done = transition(values, gain, w_swiglu_ref, w_down_ref)
        done_ref[pl.ds(at, block)] = done.astype(F32).reshape(-1, local, C).astype(BF16)

    if n == block:
        step(0)
    else:
        pl.loop(0, n, step=block)(step)
    leaving = pltpu.make_async_copy(done_ref, out_hbm, out_sem.at[0])
    leaving.start()
    for copy in copies[4:]:
        copy.wait()

    diagonal = iota((HPAD, HEADS), 0) == iota((HPAD, HEADS), 1)

    def column(row):
        turned = jnp.sum(jnp.where(diagonal, row, 0.0), axis=1, keepdims=True)
        return jnp.broadcast_to(turned, (HPAD, 128))

    gamma = jax.nn.softplus(gamma_ref[...].reshape(1, HEADS))
    heads_ref[0] = column(gamma * (-0.5 * WEIGHT_C))
    heads_ref[1] = column(cb_ref[0:1, :])
    heads_ref[2] = column(cb_ref[1:2, :])
    rows_ref[0:1, :] = chain_ref[...].reshape(1, n)
    rows_ref[1:2, :] = pad_ref[...].reshape(1, n)
    gains_ref[0:1, :S] = gain2_ref[...].reshape(1, S)
    gains_ref[0:1, S:] = gain
    wb_out_ref[...] = jnp.concatenate(
        [wb_ref[...], jnp.zeros((HPAD - HEADS, C), BF16)], axis=0
    )
    local_rows = loc_ref[...].astype(F32)
    for t in range(S // 128):
        loc_scr[t] = local_rows[:, t * 128 : (t + 1) * 128]
    for y in range(3):
        w_loc_ref[y] = strided(loc_scr, y, PLANE, 3).astype(BF16)
    leaving.wait()


def place(frame, triple):
    return [
        frame[3 * x : 3 * x + 1, :] * triple[0]
        + frame[3 * x + 1 : 3 * x + 2, :] * triple[1]
        + frame[3 * x + 2 : 3 * x + 3, :] * triple[2]
        + frame[9 + x : 10 + x, :]
        for x in range(3)
    ]


def head_of_lane(rows):
    lanes = iota((rows, WIDE), 1)
    return jnp.where(lanes < 256, lanes // CH, (lanes % 128) // VP)


def base_scores(
    queries, query_pts, high_keys, low_keys, key_pts, heads_ref, chain_all, chain_row, first
):
    local = queries.shape[0]
    n = high_keys.shape[1]
    rows = local * HPAD
    owned = (iota((HPAD, FEAT), 1) // CH == iota((HPAD, FEAT), 0))[None]
    spread = jnp.broadcast_to(queries.reshape(local, 1, FEAT), (local, HPAD, FEAT))
    high, low = split(jnp.where(owned, spread, 0.0).reshape(rows, FEAT))
    both = jnp.dot(jnp.concatenate([high, low], axis=0), high_keys, preferred_element_type=F32)
    dots = both[:rows] + both[rows:] + jnp.dot(high, low_keys, preferred_element_type=F32)
    distances = []
    blank = jnp.zeros((HPAD - HEADS, n), F32)
    for i in range(local):
        distance = 0.0
        for q, k in zip(query_pts, key_pts):
            apart = q[:, i : i + 1] - k
            distance = distance + apart * apart
        distances += [distance, blank]
    distance = jnp.concatenate(distances, axis=0)

    def per_row(index):
        wide = jnp.concatenate([heads_ref[index]] * max(1, n // 128), axis=1)[:, :n]
        return jnp.concatenate([wide] * local, axis=0)

    width = chain_all.shape[1]
    lanes, order = iota((local, width), 1), iota((local, width), 0)
    mine = jnp.sum(jnp.where(lanes == first + order, chain_all, 0), axis=1, keepdims=True)
    mine = jnp.broadcast_to(mine.reshape(local, 1, 1), (local, HPAD, n)).reshape(rows, n)
    chain = jnp.where(chain_row == mine, per_row(1), per_row(2))
    return WEIGHT_L * (dots * (1.0 / math.sqrt(CH)) + chain + per_row(0) * distance)


def pair_rows(recv_ref, at, gain, w_swiglu_ref, w_down_ref, pair_scr):
    nsrc, _, local, _ = recv_ref.shape
    n = nsrc * local
    group = max(1, min(local, 512 // n))
    for start in range(0, local, group):
        block = recv_ref[:, pl.ds(at + start, group)].astype(F32)
        block = jnp.concatenate([block[:, k].reshape(n, C) for k in range(group)], axis=0)
        done = transition(block, gain, w_swiglu_ref, w_down_ref)
        for k in range(group):
            pair_scr[start + k] = done[k * n : (k + 1) * n]


def partial_attention(base, real, high_value, low_value, wb_ref, pair_scr, attn_scr, sums_scr):
    local, n, _ = pair_scr.shape
    rows = local * HPAD
    bias = jnp.concatenate([nt_dot(wb_ref[...], pair_scr[i]) for i in range(local)], axis=0)
    scores = base + WEIGHT_L * bias
    scores = jnp.where(jnp.broadcast_to(real, (rows, n)) > 0, scores, -1000000000.0)
    peak = jnp.max(scores, axis=-1, keepdims=True)
    expo = jnp.exp(scores - peak)
    high, low = split(expo)
    total = jnp.sum(expo, axis=-1, keepdims=True)
    share = 1.0 / total
    attn_scr[:rows] = high
    attn_scr[rows:] = low
    for i in range(local):
        at = i * HPAD
        sums_scr[at : at + HPAD, :] = share[at : at + HPAD] * jnp.dot(
            high[at : at + HPAD], pair_scr[i], preferred_element_type=F32
        )
    both = jnp.dot(attn_scr[...], high_value, preferred_element_type=F32)
    every = both[:rows] + both[rows:]
    every += jnp.dot(attn_scr[:rows], low_value, preferred_element_type=F32)
    every *= share
    owned = head_of_lane(HPAD) == iota((HPAD, WIDE), 0)
    every = every.reshape(local, HPAD, WIDE)
    summed = jnp.sum(jnp.where(owned[None], every, 0.0), axis=1)
    diagonal = (iota((HPAD, HPAD), 0) == iota((HPAD, HPAD), 1))[None]

    level = jnp.broadcast_to((peak + jnp.log(total)).reshape(local, HPAD, 1), (local, HPAD, HPAD))
    level = jnp.sum(jnp.where(diagonal, level, 0.0), axis=1)
    pair_sums = [sums_scr[pl.ds(h, local, stride=HPAD), :] for h in range(HEADS)]
    return pair_sums, summed, level


def origin(row_ref):
    parts = row_ref[:, S:].astype(F32)
    return parts[:, 0:12] + parts[:, 12:24] + parts[:, 24:36]


def into_frame(row_ref, summed):
    turned = origin(row_ref)
    shifted = [
        summed[:, 256 + 128 * x : 384 + 128 * x] - turned[:, 9 + x : 10 + x] for x in range(3)
    ]
    return [
        turned[:, y : y + 1] * shifted[0]
        + turned[:, 3 + y : 4 + y] * shifted[1]
        + turned[:, 6 + y : 7 + y] * shifted[2]
        for y in range(3)
    ]


def first_kernel(
    recv_ref,
    own_ref,
    partner_ref,
    heads_ref,
    rows_ref,
    gains_ref,
    wq_ref,
    wp_ref,
    wb_ref,
    w_swiglu_ref,
    w_down_ref,
    send_ref,
    value_ref,
    near_ref,
    keys_ref,
    key_pts_ref,
    query_ref,
    query_pts_ref,
    pts_scr,
    qp_scr,
    pair_scr,
    attn_scr,
    sums_scr,
):
    nsrc, _, local, _ = recv_ref.shape
    tiles, _, lane = pts_scr.shape
    n = nsrc * local
    me = lax.axis_index("rows")
    upper = me // nsrc

    def piece(index):
        return recv_ref[:, index].astype(F32).reshape(n, 128).astype(BF16)

    all_single = jnp.concatenate([piece(2 * local + k) for k in range(SMALL - 1)], axis=1)
    queries = jnp.concatenate(
        [partner_ref[...].astype(F32), own_ref[...].astype(F32)], axis=0
    ).astype(BF16)
    rows16, lanes16 = iota((16, 128), 0), iota((16, 128), 1)
    pick = ((lanes16 % 12 == rows16) & (lanes16 < 36)).astype(BF16)
    frames = nt_dot(pick, piece(2 * local + SMALL - 1))
    query_frames = nt_dot(pick, queries[:, S:])

    high_keys, low_keys = split(nt_dot(wq_ref[FEAT : 2 * FEAT, :], all_single))
    keys_ref[0] = high_keys
    keys_ref[1] = low_keys
    points = nt_dot(wp_ref[QPTS:, :], all_single)
    for t in range(tiles):
        pts_scr[t] = points[:, t * lane : (t + 1) * lane]
    features = nt_dot(queries[:, :S], wq_ref[:FEAT, :])
    qp_scr[:QPTS, :] = nt_dot(wp_ref[:QPTS, :], queries[:, :S])

    key_pts, query_pts = [], []
    for p in range(QP):
        key_pts += place(frames, [strided(pts_scr, 3 * p + y, HEADS, 3 * QP) for y in range(3)])
        query_pts += place(
            query_frames, [qp_scr[pl.ds(3 * p + y, HEADS, stride=3 * QP), :] for y in range(3)]
        )
    for k in range(3 * QP):
        key_pts_ref[k] = key_pts[k]
        query_pts_ref[k] = query_pts[k][:, local:]
    query_ref[...] = features[local:]

    chain_all = rows_ref[0:1, :]
    chain_row = jnp.where(upper == 0, chain_all[:, :n], chain_all[:, n:])
    real = jnp.where(upper == 0, rows_ref[1:2, :n], rows_ref[1:2, n:])
    near_ref[0:1, :] = chain_row
    near_ref[1:2, :] = real
    base = base_scores(
        features[:local], query_pts, high_keys, low_keys, key_pts, heads_ref, chain_all, chain_row,
        jnp.bitwise_xor(me, nsrc + 1) * local,
    )

    planes = place(frames, [strided(pts_scr, QPTS + y, PLANE, 3) for y in range(3)])
    gap = jnp.zeros((n, 128 - PLANE), F32)
    values = [nt_dot(all_single, wq_ref[2 * FEAT :, :]), jnp.zeros((n, 256 - FEAT), F32)]
    for plane in planes:
        values += [plane.T, gap]
    high, low = split(jnp.concatenate(values, axis=1))
    value_ref[0] = high
    value_ref[1] = low

    pair_rows(
        recv_ref, local, gains_ref[0:1, S:], w_swiglu_ref, w_down_ref, pair_scr
    )
    pair_sums, summed, level = partial_attention(
        base, real, high, low, wb_ref, pair_scr, attn_scr, sums_scr
    )
    for h in range(HEADS):
        send_ref[h] = pair_sums[h].astype(BF16)
    planes = into_frame(partner_ref, summed)
    send_ref[HEADS] = summed[:, :128].astype(BF16)
    send_ref[HEADS + 1] = summed[:, 128:256].astype(BF16)
    high = level.astype(BF16).astype(F32)
    middle = (level - high).astype(BF16).astype(F32)
    low = level - high - middle
    blank = jnp.zeros((local, 128 - PLANE - HPAD), F32)
    for x, part in enumerate([high, middle, low]):
        plane = planes[x][:, :PLANE]
        send_ref[HEADS + 2 + x] = jnp.concatenate([plane, part, blank], axis=1).astype(BF16)


def second_kernel(
    recv_ref,
    value_ref,
    near_ref,
    keys_ref,
    key_pts_ref,
    query_ref,
    query_pts_ref,
    heads_ref,
    rows_ref,
    gains_ref,
    wb_ref,
    w_swiglu_ref,
    w_down_ref,
    own_ref,
    sums_ref,
    wide_ref,
    level_ref,
    pair_scr,
    attn_scr,
    sums_scr,
):
    nsrc, _, local, _ = recv_ref.shape
    me = lax.axis_index("rows")
    pair_rows(
        recv_ref, 0, gains_ref[0:1, S:], w_swiglu_ref, w_down_ref, pair_scr
    )
    base = base_scores(
        query_ref[...], [query_pts_ref[k] for k in range(3 * QP)], keys_ref[0], keys_ref[1],
        [key_pts_ref[k] for k in range(3 * QP)], heads_ref, rows_ref[0:1, :], near_ref[0:1, :],
        me * local,
    )
    pair_sums, summed, level = partial_attention(
        base, near_ref[1:2, :], value_ref[0], value_ref[1], wb_ref, pair_scr, attn_scr, sums_scr
    )
    for h in range(HEADS):
        sums_ref[h] = pair_sums[h]
    wide_ref[:, :256] = summed[:, :256]
    for x, plane in enumerate(into_frame(own_ref, summed)):
        wide_ref[:, 256 + 128 * x : 384 + 128 * x] = plane
    level_ref[...] = jnp.concatenate(
        [jnp.zeros((local, PLANE), F32), level, jnp.zeros((local, 128 - PLANE - HPAD), F32)], axis=1
    )


def finish_kernel(
    got_ref,
    sums_ref,
    wide_ref,
    level_ref,
    own_ref,
    gains_ref,
    w_out_ref,
    w_loc_ref,
    out_ref,
):
    local = own_ref.shape[0]
    planes = [got_ref[HEADS + 2 + x].astype(F32) for x in range(3)]
    ahead = planes[0] + planes[1] + planes[2] - level_ref[...]
    got = 0.5 + 0.5 * jnp.tanh(0.5 * ahead)
    lanes = iota((local, 128), 1)
    low_share = jnp.zeros((local, 128), F32)
    high_share = jnp.zeros((local, 128), F32)
    plane_share = jnp.zeros((local, 128), F32)
    pair_total = []
    for h in range(HEADS):
        share = jnp.broadcast_to(got[:, PLANE + h : PLANE + h + 1], (local, 128))
        low_share = jnp.where(lanes // CH == h, share, low_share)
        high_share = jnp.where(lanes // CH + 8 == h, share, high_share)
        plane_share = jnp.where(lanes // VP == h, share, plane_share)
        mine = sums_ref[h]
        pair_total.append(mine + share * (got_ref[h].astype(F32) - mine))

    def joined(at, share, theirs):
        mine = wide_ref[:, at : at + 128]
        return mine + share * (theirs - mine)

    features = [
        joined(0, low_share, got_ref[HEADS].astype(F32)),
        joined(128, high_share, got_ref[HEADS + 1].astype(F32)),
    ]
    local_out = [joined(256 + 128 * x, plane_share, planes[x]) for x in range(3)]

    pair_total = jnp.concatenate(pair_total, axis=1).astype(BF16)
    at = FEAT + 4 * PLANE
    update = jnp.dot(pair_total, w_out_ref[at:, :], preferred_element_type=F32)
    update += jnp.dot(
        jnp.concatenate(features, axis=1)[:, :FEAT].astype(BF16),
        w_out_ref[:FEAT, :],
        preferred_element_type=F32,
    )

    lengths = jnp.sqrt(
        local_out[0] * local_out[0] + local_out[1] * local_out[1] + local_out[2] * local_out[2] + 1.0
    )
    for y in range(3):
        update += jnp.dot(
            local_out[y][:, :PLANE].astype(BF16), w_loc_ref[y], preferred_element_type=F32
        )
    update += jnp.dot(
        lengths[:, :PLANE].astype(BF16),
        w_out_ref[at - PLANE : at, :],
        preferred_element_type=F32,
    )
    own_single = own_ref[:, :S].astype(F32)
    out_ref[...] = layer_norm(own_single + update, gains_ref[0:1, :S]).astype(BF16)


def in_hbm(arrays):
    return [pltpu.with_memory_space_constraint(array, pltpu.HBM) for array in arrays]


def whole(memory=pltpu.VMEM):
    return pl.BlockSpec(memory_space=memory)


def params(mib):
    return pltpu.CompilerParams(vmem_limit_bytes=mib * MIB)


def on_device(
    single_rep,
    pair_grid,
    frames,
    chain_ids,
    pad_mask,
    ln_pair_gain,
    w_swiglu,
    w_pair_down,
    w_bias,
    w_qkv,
    w_points,
    gamma_raw,
    chain_bias,
    w_out,
    ln_single_gain,
):
    n, local, _ = pair_grid.shape
    size = n // local
    nsrc = size // 2
    near = n // 2
    tiles = max(1, near // 128)
    large = 4 * (n // 128)
    halves = [list(range(nsrc)), list(range(nsrc, size))]
    across = [(i, i ^ (nsrc + 1)) for i in range(size)]

    packed, own = pl.pallas_call(
        pack_kernel,
        out_shape=[
            jax.ShapeDtypeStruct((nsrc // 2, 2, 2 * local + SMALL, local, C), BF16),
            jax.ShapeDtypeStruct((local, S + 128), BF16),
        ],
        in_specs=[whole(pltpu.HBM)] * 3,
        out_specs=[whole(pltpu.HBM), whole()],
        scratch_shapes=[
            pltpu.VMEM((nsrc // 2, 2, 2 * local, local, C), BF16),
            pltpu.VMEM((nsrc // 2, 2, SMALL, local, C), BF16),
            pltpu.VMEM((local, 12), F32),
            pltpu.SemaphoreType.DMA((3 * PIECES + 2,)),
            pltpu.SemaphoreType.DMA((PIECES + 1,)),
        ],
        compiler_params=params(4 + large),
        name="pack",
    )(*in_hbm([pair_grid.reshape(2, nsrc // 2, 2, local, local, C), single_rep, frames.T]))
    received = lax.all_to_all(
        packed.reshape(nsrc, 2 * local + SMALL, local, C), "rows", 0, 0, tiled=True, axis_index_groups=halves
    )
    partner = lax.ppermute(own, "rows", across)

    sources = [
        pair_grid,
        w_swiglu,
        w_pair_down,
        ln_pair_gain,
        gamma_raw,
        chain_bias,
        chain_ids,
        pad_mask,
        ln_single_gain,
        w_bias.T,
        w_out,
        w_qkv.T,
        w_points.T,
    ]
    held = [pltpu.VMEM(x.shape, x.dtype) for x in sources[:10]]
    held.append(pltpu.VMEM((3 * PLANE, S), BF16))
    pair_out, heads, rows, gains, wb, w_loc, wq, wp = pl.pallas_call(
        own_kernel,
        out_shape=[
            jax.ShapeDtypeStruct(pair_grid.shape, BF16),
            jax.ShapeDtypeStruct((3, HPAD, 128), F32),
            jax.ShapeDtypeStruct((2, n), jnp.int32),
            jax.ShapeDtypeStruct((1, S + C), F32),
            jax.ShapeDtypeStruct((HPAD, C), BF16),
            jax.ShapeDtypeStruct((3, PLANE, S), BF16),
            jax.ShapeDtypeStruct(sources[11].shape, BF16),
            jax.ShapeDtypeStruct(sources[12].shape, BF16),
        ],
        in_specs=[whole(pltpu.HBM)] * len(sources),
        out_specs=[whole(pltpu.HBM)] + [whole()] * 7,
        scratch_shapes=held
        + [
            pltpu.VMEM(pair_grid.shape, BF16),
            pltpu.VMEM((S // 128, 3 * PLANE, 128), F32),
            pltpu.SemaphoreType.DMA((len(sources),)),
            pltpu.SemaphoreType.DMA((1,)),
        ],
        compiler_params=params(18 + large),
        name="own_transition",
    )(*in_hbm(sources))

    scratch = [
        pltpu.VMEM((local, near, C), BF16),
        pltpu.VMEM((2 * local * HPAD, near), BF16),
        pltpu.VMEM((local * HPAD, C), F32),
    ]
    send, *held = pl.pallas_call(
        first_kernel,
        out_shape=[
            jax.ShapeDtypeStruct((PARTS, local, 128), BF16),
            jax.ShapeDtypeStruct((2, near, WIDE), BF16),
            jax.ShapeDtypeStruct((2, near), jnp.int32),
            jax.ShapeDtypeStruct((2, FEAT, near), BF16),
            jax.ShapeDtypeStruct((3 * QP, HEADS, near), F32),
            jax.ShapeDtypeStruct((local, FEAT), F32),
            jax.ShapeDtypeStruct((3 * QP, HEADS, local), F32),
        ],
        in_specs=[whole()] * 11,
        out_specs=[whole()] * 7,
        scratch_shapes=[
            pltpu.VMEM((tiles, QPTS + 3 * PLANE, near // tiles), F32),
            pltpu.VMEM((QPTS + 4 * 3 * QP, 2 * local), F32),
        ]
        + scratch,
        compiler_params=params(16 + large),
        name="first_half",
    )(received, own, partner, heads, rows, gains, wq, wp, wb, w_swiglu, w_pair_down)
    got = lax.ppermute(send, "rows", across)

    sums, wide, level = pl.pallas_call(
        second_kernel,
        out_shape=[
            jax.ShapeDtypeStruct((HEADS, local, 128), F32),
            jax.ShapeDtypeStruct((local, WIDE), F32),
            jax.ShapeDtypeStruct((local, 128), F32),
        ],
        in_specs=[whole()] * 14,
        out_specs=[whole()] * 3,
        scratch_shapes=scratch,
        compiler_params=params(12 + large),
        name="second_half",
    )(received, *held, heads, rows, gains, wb, w_swiglu, w_pair_down, own)

    single_out = pl.pallas_call(
        finish_kernel,
        out_shape=jax.ShapeDtypeStruct((local, S), BF16),
        in_specs=[whole()] * 8,
        out_specs=whole(),
        compiler_params=params(12),
        name="finish",
    )(got, sums, wide, level, own, gains, w_out, w_loc)
    return (single_out, pair_out)


def solution(mesh):
    placed = (
        P(("groups", "rows"), None),
        P("groups", "rows", None),
        P(None, ("groups", "rows")),
        P("groups"),
        P("groups"),
    ) + (P(),) * 10
    return jax.shard_map(
        on_device,
        mesh=mesh,
        in_specs=placed,
        out_specs=(P(("groups", "rows"), None), P("groups", "rows", None)),
        check_vma=False,
    )
```

```python
import math

import jax
import jax.numpy as jnp
from jax import lax
from jax.experimental import pallas as pl
from jax.experimental.pallas import tpu as pltpu
from jax.sharding import PartitionSpec as P

C = 128
S = 384
H = 512
HEADS = 12
CH = 16
QP = 4
VP = 8
HPAD = 16
FEAT = HEADS * CH
QPTS = HEADS * QP * 3
PLANE = HEADS * VP
WIDE = 256 + 3 * 128
SMALL = S // 128 + 1
PIECES = 2
PARTS = HEADS + WIDE // 128
F32 = jnp.float32
BF16 = jnp.bfloat16
NT = (((1,), (1,)), ((), ()))
MIB = 1024 * 1024
WEIGHT_L = math.sqrt(1.0 / 3.0)
WEIGHT_C = math.sqrt(2.0 / (9.0 * QP))


def iota(shape, dim):
    return lax.broadcasted_iota(jnp.int32, shape, dim)


def nt_dot(a, b):
    return lax.dot_general(a, b, NT, preferred_element_type=F32)


def layer_norm(values, gain):
    centre = jnp.mean(values, axis=-1, keepdims=True)
    centred = values - centre
    spread = jnp.mean(centred * centred, axis=-1, keepdims=True)
    return centred * lax.rsqrt(spread + 1e-05) * gain


def transition(values, gain, w_swiglu_ref, w_down_ref):
    normed = layer_norm(values, gain).astype(BF16)
    both = jnp.dot(normed, w_swiglu_ref[...], preferred_element_type=F32)
    gate = 0.5 * both[:, :H]
    hidden = (gate * (1.0 + jnp.tanh(gate)) * both[:, H:]).astype(BF16)
    update = jnp.dot(hidden, w_down_ref[...], preferred_element_type=F32)
    return (values + update).astype(BF16)


def split(values):
    high = values.astype(BF16)
    return high, (values - high.astype(F32)).astype(BF16)


def pack_kernel(
    pair_hbm, single_hbm, frames_hbm, out_hbm, own_ref, pair_ref, small_ref, frames_ref, in_sems, out_sems
):
    chips = pair_ref.shape[0]
    local = own_ref.shape[0]
    upper = lax.axis_index("rows") // (2 * chips)
    step = max(1, chips // PIECES)
    starts = range(0, chips, step)
    arrivals = []
    for at in starts:
        span = pl.ds(at, step)
        moves = [(pair_hbm.at[upper, span], pair_ref.at[span, :, pl.ds(0, local)])]
        for core in range(2):
            moves.append(
                (
                    pair_hbm.at[1 - upper, span, 1 - core],
                    pair_ref.at[span, core, pl.ds(local, local)],
                )
            )
        for source, target in moves:
            arrivals.append(pltpu.make_async_copy(source, target, in_sems.at[len(arrivals)]))
    rows_copies = [
        pltpu.make_async_copy(single_hbm, own_ref.at[:, :S], in_sems.at[len(arrivals)]),
        pltpu.make_async_copy(frames_hbm, frames_ref, in_sems.at[len(arrivals) + 1]),
    ]
    for copy in rows_copies + arrivals:
        copy.start()
    for copy in rows_copies:
        copy.wait()
    rows = frames_ref[...]
    blank = jnp.zeros((local, 128 - 36), F32)
    turned = jnp.concatenate([rows, rows, rows, blank], axis=1)
    high = turned.astype(BF16).astype(F32)
    middle = (turned - high).astype(BF16).astype(F32)
    low = turned - high - middle
    lane = iota(turned.shape, 1)
    own_ref[:, S:] = jnp.where(lane < 12, high, jnp.where(lane < 24, middle, low)).astype(BF16)
    for chip in range(chips):
        for core in range(2):
            for piece in range(SMALL):
                small_ref[chip, core, piece] = own_ref[:, piece * 128 : piece * 128 + 128]
    departures = [
        pltpu.make_async_copy(small_ref, out_hbm.at[:, :, pl.ds(2 * local, SMALL)], out_sems.at[0])
    ]
    departures[0].start()
    for k, at in enumerate(starts):
        for copy in arrivals[3 * k : 3 * k + 3]:
            copy.wait()
        departures.append(
            pltpu.make_async_copy(
                pair_ref.at[pl.ds(at, step)],
                out_hbm.at[pl.ds(at, step), :, pl.ds(0, 2 * local)],
                out_sems.at[1 + k],
            )
        )
        departures[-1].start()
    for copy in departures:
        copy.wait()


def strided(ref, start, count, stride):
    return jnp.concatenate(
        [ref[t, pl.ds(start, count, stride=stride), :] for t in range(ref.shape[0])], axis=1
    )


def own_kernel(*refs):
    sources, refs = refs[:13], refs[13:]
    out_ref, heads_ref, rows_ref, gains_ref, wb_out_ref, w_loc_ref, wq_ref, wp_ref = refs[:8]
    held, refs = refs[8:19], refs[19:]
    loc_scr, sems = refs
    pair_hbm, *_ = sources
    n, local, _ = pair_hbm.shape
    targets = list(held) + [wq_ref, wp_ref]
    copies = []
    for k, (source, target) in enumerate(zip(sources, targets)):
        if k == 10:
            source = source.at[pl.ds(FEAT, 3 * PLANE)]
        copies.append(pltpu.make_async_copy(source, target, sems.at[k]))
        copies[k].start()
    pair_ref, w_swiglu_ref, w_down_ref, gain_ref, gamma_ref, cb_ref = held[:6]
    chain_ref, pad_ref, gain2_ref, wb_ref, loc_ref = held[6:]
    for copy in copies[:4]:
        copy.wait()
    gain = gain_ref[...].reshape(1, C)
    block = math.gcd(n, 128)

    def step(at):
        values = pair_ref[pl.ds(at, block)].astype(F32).reshape(-1, C)
        done = transition(values, gain, w_swiglu_ref, w_down_ref)
        out_ref[pl.ds(at, block)] = done.astype(F32).reshape(-1, local, C).astype(BF16)

    if n == block:
        step(0)
    else:
        pl.loop(0, n, step=block)(step)
    for copy in copies[4:]:
        copy.wait()

    diagonal = iota((HPAD, HEADS), 0) == iota((HPAD, HEADS), 1)

    def column(row):
        turned = jnp.sum(jnp.where(diagonal, row, 0.0), axis=1, keepdims=True)
        return jnp.broadcast_to(turned, (HPAD, 128))

    gamma = jax.nn.softplus(gamma_ref[...].reshape(1, HEADS))
    heads_ref[0] = column(gamma * (-0.5 * WEIGHT_C))
    heads_ref[1] = column(cb_ref[0:1, :])
    heads_ref[2] = column(cb_ref[1:2, :])
    rows_ref[0:1, :] = chain_ref[...].reshape(1, n)
    rows_ref[1:2, :] = pad_ref[...].reshape(1, n)
    gains_ref[0:1, :S] = gain2_ref[...].reshape(1, S)
    gains_ref[0:1, S:] = gain
    wb_out_ref[...] = jnp.concatenate(
        [wb_ref[...], jnp.zeros((HPAD - HEADS, C), BF16)], axis=0
    )
    local_rows = loc_ref[...].astype(F32)
    for t in range(S // 128):
        loc_scr[t] = local_rows[:, t * 128 : (t + 1) * 128]
    for y in range(3):
        w_loc_ref[y] = strided(loc_scr, y, PLANE, 3).astype(BF16)


def place(frame, triple):
    return [
        frame[3 * x : 3 * x + 1, :] * triple[0]
        + frame[3 * x + 1 : 3 * x + 2, :] * triple[1]
        + frame[3 * x + 2 : 3 * x + 3, :] * triple[2]
        + frame[9 + x : 10 + x, :]
        for x in range(3)
    ]


def head_of_lane(rows):
    lanes = iota((rows, WIDE), 1)
    return jnp.where(lanes < 256, lanes // CH, (lanes % 128) // VP)


def base_scores(
    queries, query_pts, high_keys, low_keys, key_pts, heads_ref, chain_all, chain_row, first
):
    local = queries.shape[0]
    n = high_keys.shape[1]
    rows = local * HPAD
    owned = (iota((HPAD, FEAT), 1) // CH == iota((HPAD, FEAT), 0))[None]
    spread = jnp.broadcast_to(queries.reshape(local, 1, FEAT), (local, HPAD, FEAT))
    high, low = split(jnp.where(owned, spread, 0.0).reshape(rows, FEAT))
    both = jnp.dot(jnp.concatenate([high, low], axis=0), high_keys, preferred_element_type=F32)
    dots = both[:rows] + both[rows:] + jnp.dot(high, low_keys, preferred_element_type=F32)
    distances = []
    blank = jnp.zeros((HPAD - HEADS, n), F32)
    for i in range(local):
        distance = 0.0
        for q, k in zip(query_pts, key_pts):
            apart = q[:, i : i + 1] - k
            distance = distance + apart * apart
        distances += [distance, blank]
    distance = jnp.concatenate(distances, axis=0)

    def per_row(index):
        wide = jnp.concatenate([heads_ref[index]] * max(1, n // 128), axis=1)[:, :n]
        return jnp.concatenate([wide] * local, axis=0)

    width = chain_all.shape[1]
    lanes, order = iota((local, width), 1), iota((local, width), 0)
    mine = jnp.sum(jnp.where(lanes == first + order, chain_all, 0), axis=1, keepdims=True)
    mine = jnp.broadcast_to(mine.reshape(local, 1, 1), (local, HPAD, n)).reshape(rows, n)
    chain = jnp.where(chain_row == mine, per_row(1), per_row(2))
    return WEIGHT_L * (dots * (1.0 / math.sqrt(CH)) + chain + per_row(0) * distance)


def pair_rows(recv_ref, at, gain, w_swiglu_ref, w_down_ref, pair_scr):
    nsrc, _, local, _ = recv_ref.shape
    n = nsrc * local
    group = max(1, min(local, 512 // n))
    for start in range(0, local, group):
        block = recv_ref[:, pl.ds(at + start, group)].astype(F32)
        block = jnp.concatenate([block[:, k].reshape(n, C) for k in range(group)], axis=0)
        done = transition(block, gain, w_swiglu_ref, w_down_ref)
        for k in range(group):
            pair_scr[start + k] = done[k * n : (k + 1) * n]


def partial_attention(base, real, high_value, low_value, wb_ref, pair_scr, attn_scr, sums_scr):
    local, n, _ = pair_scr.shape
    rows = local * HPAD
    bias = jnp.concatenate([nt_dot(wb_ref[...], pair_scr[i]) for i in range(local)], axis=0)
    scores = base + WEIGHT_L * bias
    scores = jnp.where(jnp.broadcast_to(real, (rows, n)) > 0, scores, -1000000000.0)
    peak = jnp.max(scores, axis=-1, keepdims=True)
    expo = jnp.exp(scores - peak)
    high, low = split(expo)
    total = jnp.sum(expo, axis=-1, keepdims=True)
    share = 1.0 / total
    attn_scr[:rows] = high
    attn_scr[rows:] = low
    for i in range(local):
        at = i * HPAD
        sums_scr[at : at + HPAD, :] = share[at : at + HPAD] * jnp.dot(
            high[at : at + HPAD], pair_scr[i], preferred_element_type=F32
        )
    both = jnp.dot(attn_scr[...], high_value, preferred_element_type=F32)
    every = both[:rows] + both[rows:]
    every += jnp.dot(attn_scr[:rows], low_value, preferred_element_type=F32)
    every *= share
    owned = head_of_lane(HPAD) == iota((HPAD, WIDE), 0)
    every = every.reshape(local, HPAD, WIDE)
    summed = jnp.sum(jnp.where(owned[None], every, 0.0), axis=1)
    diagonal = (iota((HPAD, HPAD), 0) == iota((HPAD, HPAD), 1))[None]

    level = jnp.broadcast_to((peak + jnp.log(total)).reshape(local, HPAD, 1), (local, HPAD, HPAD))
    level = jnp.sum(jnp.where(diagonal, level, 0.0), axis=1)
    pair_sums = [sums_scr[pl.ds(h, local, stride=HPAD), :] for h in range(HEADS)]
    return pair_sums, summed, level


def origin(row_ref):
    parts = row_ref[:, S:].astype(F32)
    return parts[:, 0:12] + parts[:, 12:24] + parts[:, 24:36]


def into_frame(row_ref, summed):
    turned = origin(row_ref)
    shifted = [
        summed[:, 256 + 128 * x : 384 + 128 * x] - turned[:, 9 + x : 10 + x] for x in range(3)
    ]
    return [
        turned[:, y : y + 1] * shifted[0]
        + turned[:, 3 + y : 4 + y] * shifted[1]
        + turned[:, 6 + y : 7 + y] * shifted[2]
        for y in range(3)
    ]


def first_kernel(
    recv_ref,
    own_ref,
    partner_ref,
    heads_ref,
    rows_ref,
    gains_ref,
    wq_ref,
    wp_ref,
    wb_ref,
    w_swiglu_ref,
    w_down_ref,
    send_ref,
    value_ref,
    near_ref,
    keys_ref,
    key_pts_ref,
    query_ref,
    query_pts_ref,
    pts_scr,
    qp_scr,
    pair_scr,
    attn_scr,
    sums_scr,
):
    nsrc, _, local, _ = recv_ref.shape
    tiles, _, lane = pts_scr.shape
    n = nsrc * local
    me = lax.axis_index("rows")
    upper = me // nsrc

    def piece(index):
        return recv_ref[:, index].astype(F32).reshape(n, 128).astype(BF16)

    all_single = jnp.concatenate([piece(2 * local + k) for k in range(SMALL - 1)], axis=1)
    queries = jnp.concatenate(
        [partner_ref[...].astype(F32), own_ref[...].astype(F32)], axis=0
    ).astype(BF16)
    rows16, lanes16 = iota((16, 128), 0), iota((16, 128), 1)
    pick = ((lanes16 % 12 == rows16) & (lanes16 < 36)).astype(BF16)
    frames = nt_dot(pick, piece(2 * local + SMALL - 1))
    query_frames = nt_dot(pick, queries[:, S:])

    high_keys, low_keys = split(nt_dot(wq_ref[FEAT : 2 * FEAT, :], all_single))
    keys_ref[0] = high_keys
    keys_ref[1] = low_keys
    points = nt_dot(wp_ref[QPTS:, :], all_single)
    for t in range(tiles):
        pts_scr[t] = points[:, t * lane : (t + 1) * lane]
    features = nt_dot(queries[:, :S], wq_ref[:FEAT, :])
    qp_scr[:QPTS, :] = nt_dot(wp_ref[:QPTS, :], queries[:, :S])

    key_pts, query_pts = [], []
    for p in range(QP):
        key_pts += place(frames, [strided(pts_scr, 3 * p + y, HEADS, 3 * QP) for y in range(3)])
        query_pts += place(
            query_frames, [qp_scr[pl.ds(3 * p + y, HEADS, stride=3 * QP), :] for y in range(3)]
        )
    for k in range(3 * QP):
        key_pts_ref[k] = key_pts[k]
        query_pts_ref[k] = query_pts[k][:, local:]
    query_ref[...] = features[local:]

    chain_all = rows_ref[0:1, :]
    chain_row = jnp.where(upper == 0, chain_all[:, :n], chain_all[:, n:])
    real = jnp.where(upper == 0, rows_ref[1:2, :n], rows_ref[1:2, n:])
    near_ref[0:1, :] = chain_row
    near_ref[1:2, :] = real
    base = base_scores(
        features[:local], query_pts, high_keys, low_keys, key_pts, heads_ref, chain_all, chain_row,
        jnp.bitwise_xor(me, nsrc + 1) * local,
    )

    planes = place(frames, [strided(pts_scr, QPTS + y, PLANE, 3) for y in range(3)])
    gap = jnp.zeros((n, 128 - PLANE), F32)
    values = [nt_dot(all_single, wq_ref[2 * FEAT :, :]), jnp.zeros((n, 256 - FEAT), F32)]
    for plane in planes:
        values += [plane.T, gap]
    high, low = split(jnp.concatenate(values, axis=1))
    value_ref[0] = high
    value_ref[1] = low

    pair_rows(
        recv_ref, local, gains_ref[0:1, S:], w_swiglu_ref, w_down_ref, pair_scr
    )
    pair_sums, summed, level = partial_attention(
        base, real, high, low, wb_ref, pair_scr, attn_scr, sums_scr
    )
    for h in range(HEADS):
        send_ref[h] = pair_sums[h].astype(BF16)
    planes = into_frame(partner_ref, summed)
    send_ref[HEADS] = summed[:, :128].astype(BF16)
    send_ref[HEADS + 1] = summed[:, 128:256].astype(BF16)
    high = level.astype(BF16).astype(F32)
    middle = (level - high).astype(BF16).astype(F32)
    low = level - high - middle
    blank = jnp.zeros((local, 128 - PLANE - HPAD), F32)
    for x, part in enumerate([high, middle, low]):
        plane = planes[x][:, :PLANE]
        send_ref[HEADS + 2 + x] = jnp.concatenate([plane, part, blank], axis=1).astype(BF16)


def second_kernel(
    recv_ref,
    value_ref,
    near_ref,
    keys_ref,
    key_pts_ref,
    query_ref,
    query_pts_ref,
    heads_ref,
    rows_ref,
    gains_ref,
    wb_ref,
    w_swiglu_ref,
    w_down_ref,
    own_ref,
    sums_ref,
    wide_ref,
    level_ref,
    pair_scr,
    attn_scr,
    sums_scr,
):
    nsrc, _, local, _ = recv_ref.shape
    me = lax.axis_index("rows")
    pair_rows(
        recv_ref, 0, gains_ref[0:1, S:], w_swiglu_ref, w_down_ref, pair_scr
    )
    base = base_scores(
        query_ref[...], [query_pts_ref[k] for k in range(3 * QP)], keys_ref[0], keys_ref[1],
        [key_pts_ref[k] for k in range(3 * QP)], heads_ref, rows_ref[0:1, :], near_ref[0:1, :],
        me * local,
    )
    pair_sums, summed, level = partial_attention(
        base, near_ref[1:2, :], value_ref[0], value_ref[1], wb_ref, pair_scr, attn_scr, sums_scr
    )
    for h in range(HEADS):
        sums_ref[h] = pair_sums[h]
    wide_ref[:, :256] = summed[:, :256]
    for x, plane in enumerate(into_frame(own_ref, summed)):
        wide_ref[:, 256 + 128 * x : 384 + 128 * x] = plane
    level_ref[...] = jnp.concatenate(
        [jnp.zeros((local, PLANE), F32), level, jnp.zeros((local, 128 - PLANE - HPAD), F32)], axis=1
    )


def finish_kernel(
    got_ref,
    sums_ref,
    wide_ref,
    level_ref,
    own_ref,
    gains_ref,
    w_out_ref,
    w_loc_ref,
    out_ref,
):
    local = own_ref.shape[0]
    planes = [got_ref[HEADS + 2 + x].astype(F32) for x in range(3)]
    ahead = planes[0] + planes[1] + planes[2] - level_ref[...]
    got = 0.5 + 0.5 * jnp.tanh(0.5 * ahead)
    lanes = iota((local, 128), 1)
    low_share = jnp.zeros((local, 128), F32)
    high_share = jnp.zeros((local, 128), F32)
    plane_share = jnp.zeros((local, 128), F32)
    pair_total = []
    for h in range(HEADS):
        share = jnp.broadcast_to(got[:, PLANE + h : PLANE + h + 1], (local, 128))
        low_share = jnp.where(lanes // CH == h, share, low_share)
        high_share = jnp.where(lanes // CH + 8 == h, share, high_share)
        plane_share = jnp.where(lanes // VP == h, share, plane_share)
        mine = sums_ref[h]
        pair_total.append(mine + share * (got_ref[h].astype(F32) - mine))

    def joined(at, share, theirs):
        mine = wide_ref[:, at : at + 128]
        return mine + share * (theirs - mine)

    features = [
        joined(0, low_share, got_ref[HEADS].astype(F32)),
        joined(128, high_share, got_ref[HEADS + 1].astype(F32)),
    ]
    local_out = [joined(256 + 128 * x, plane_share, planes[x]) for x in range(3)]

    pair_total = jnp.concatenate(pair_total, axis=1).astype(BF16)
    at = FEAT + 4 * PLANE
    update = jnp.dot(pair_total, w_out_ref[at:, :], preferred_element_type=F32)
    update += jnp.dot(
        jnp.concatenate(features, axis=1)[:, :FEAT].astype(BF16),
        w_out_ref[:FEAT, :],
        preferred_element_type=F32,
    )

    lengths = jnp.sqrt(
        local_out[0] * local_out[0] + local_out[1] * local_out[1] + local_out[2] * local_out[2] + 1.0
    )
    for y in range(3):
        update += jnp.dot(
            local_out[y][:, :PLANE].astype(BF16), w_loc_ref[y], preferred_element_type=F32
        )
    update += jnp.dot(
        lengths[:, :PLANE].astype(BF16),
        w_out_ref[at - PLANE : at, :],
        preferred_element_type=F32,
    )
    own_single = own_ref[:, :S].astype(F32)
    out_ref[...] = layer_norm(own_single + update, gains_ref[0:1, :S]).astype(BF16)


def in_hbm(arrays):
    return [pltpu.with_memory_space_constraint(array, pltpu.HBM) for array in arrays]


def whole(memory=pltpu.VMEM):
    return pl.BlockSpec(memory_space=memory)


def params(mib):
    return pltpu.CompilerParams(vmem_limit_bytes=mib * MIB)


def on_device(
    single_rep,
    pair_grid,
    frames,
    chain_ids,
    pad_mask,
    ln_pair_gain,
    w_swiglu,
    w_pair_down,
    w_bias,
    w_qkv,
    w_points,
    gamma_raw,
    chain_bias,
    w_out,
    ln_single_gain,
):
    n, local, _ = pair_grid.shape
    size = n // local
    nsrc = size // 2
    near = n // 2
    tiles = max(1, near // 128)
    large = 4 * (n // 128)
    halves = [list(range(nsrc)), list(range(nsrc, size))]
    across = [(i, i ^ (nsrc + 1)) for i in range(size)]

    packed, own = pl.pallas_call(
        pack_kernel,
        out_shape=[
            jax.ShapeDtypeStruct((nsrc // 2, 2, 2 * local + SMALL, local, C), BF16),
            jax.ShapeDtypeStruct((local, S + 128), BF16),
        ],
        in_specs=[whole(pltpu.HBM)] * 3,
        out_specs=[whole(pltpu.HBM), whole()],
        scratch_shapes=[
            pltpu.VMEM((nsrc // 2, 2, 2 * local, local, C), BF16),
            pltpu.VMEM((nsrc // 2, 2, SMALL, local, C), BF16),
            pltpu.VMEM((local, 12), F32),
            pltpu.SemaphoreType.DMA((3 * PIECES + 2,)),
            pltpu.SemaphoreType.DMA((PIECES + 1,)),
        ],
        compiler_params=params(4 + large),
        name="pack",
    )(*in_hbm([pair_grid.reshape(2, nsrc // 2, 2, local, local, C), single_rep, frames.T]))
    received = lax.all_to_all(
        packed.reshape(nsrc, 2 * local + SMALL, local, C), "rows", 0, 0, tiled=True, axis_index_groups=halves
    )
    partner = lax.ppermute(own, "rows", across)

    sources = [
        pair_grid,
        w_swiglu,
        w_pair_down,
        ln_pair_gain,
        gamma_raw,
        chain_bias,
        chain_ids,
        pad_mask,
        ln_single_gain,
        w_bias.T,
        w_out,
        w_qkv.T,
        w_points.T,
    ]
    held = [pltpu.VMEM(x.shape, x.dtype) for x in sources[:10]]
    held.append(pltpu.VMEM((3 * PLANE, S), BF16))
    pair_out, heads, rows, gains, wb, w_loc, wq, wp = pl.pallas_call(
        own_kernel,
        out_shape=[
            jax.ShapeDtypeStruct(pair_grid.shape, BF16),
            jax.ShapeDtypeStruct((3, HPAD, 128), F32),
            jax.ShapeDtypeStruct((2, n), jnp.int32),
            jax.ShapeDtypeStruct((1, S + C), F32),
            jax.ShapeDtypeStruct((HPAD, C), BF16),
            jax.ShapeDtypeStruct((3, PLANE, S), BF16),
            jax.ShapeDtypeStruct(sources[11].shape, BF16),
            jax.ShapeDtypeStruct(sources[12].shape, BF16),
        ],
        in_specs=[whole(pltpu.HBM)] * len(sources),
        out_specs=[whole()] * 8,
        scratch_shapes=held
        + [
            pltpu.VMEM((S // 128, 3 * PLANE, 128), F32),
            pltpu.SemaphoreType.DMA((len(sources),)),
        ],
        compiler_params=params(18 + large),
        name="own_transition",
    )(*in_hbm(sources))

    scratch = [
        pltpu.VMEM((local, near, C), BF16),
        pltpu.VMEM((2 * local * HPAD, near), BF16),
        pltpu.VMEM((local * HPAD, C), F32),
    ]
    send, *held = pl.pallas_call(
        first_kernel,
        out_shape=[
            jax.ShapeDtypeStruct((PARTS, local, 128), BF16),
            jax.ShapeDtypeStruct((2, near, WIDE), BF16),
            jax.ShapeDtypeStruct((2, near), jnp.int32),
            jax.ShapeDtypeStruct((2, FEAT, near), BF16),
            jax.ShapeDtypeStruct((3 * QP, HEADS, near), F32),
            jax.ShapeDtypeStruct((local, FEAT), F32),
            jax.ShapeDtypeStruct((3 * QP, HEADS, local), F32),
        ],
        in_specs=[whole()] * 11,
        out_specs=[whole()] * 7,
        scratch_shapes=[
            pltpu.VMEM((tiles, QPTS + 3 * PLANE, near // tiles), F32),
            pltpu.VMEM((QPTS + 4 * 3 * QP, 2 * local), F32),
        ]
        + scratch,
        compiler_params=params(16 + large),
        name="first_half",
    )(received, own, partner, heads, rows, gains, wq, wp, wb, w_swiglu, w_pair_down)
    got = lax.ppermute(send, "rows", across)

    sums, wide, level = pl.pallas_call(
        second_kernel,
        out_shape=[
            jax.ShapeDtypeStruct((HEADS, local, 128), F32),
            jax.ShapeDtypeStruct((local, WIDE), F32),
            jax.ShapeDtypeStruct((local, 128), F32),
        ],
        in_specs=[whole()] * 14,
        out_specs=[whole()] * 3,
        scratch_shapes=scratch,
        compiler_params=params(12 + large),
        name="second_half",
    )(received, *held, heads, rows, gains, wb, w_swiglu, w_pair_down, own)

    single_out = pl.pallas_call(
        finish_kernel,
        out_shape=jax.ShapeDtypeStruct((local, S), BF16),
        in_specs=[whole()] * 8,
        out_specs=whole(),
        compiler_params=params(12),
        name="finish",
    )(got, sums, wide, level, own, gains, w_out, w_loc)
    return (single_out, pair_out)


def solution(mesh):
    placed = (
        P(("groups", "rows"), None),
        P("groups", "rows", None),
        P(None, ("groups", "rows")),
        P("groups"),
        P("groups"),
    ) + (P(),) * 10
    return jax.shard_map(
        on_device,
        mesh=mesh,
        in_specs=placed,
        out_specs=(P(("groups", "rows"), None), P("groups", "rows", None)),
        check_vma=False,
    )
```
